32 devices in a mesh: seq: 16 (over z, y, x), tp: 2 (over core).
Axes of the slice: x: 2, y: 2, z: 4, core: 2. Of those that a mesh axis runs over, the one named last changes fastest.
Arguments:
- tokens: bfloat16 [4096, 1536], P('seq'), may hold values from -6 to 6
- cotangent: bfloat16 [4096, 1536], P('seq'), may hold values from -6 to 6
- step_embed: bfloat16 [4, 1024], replicated, may hold values from -6 to 6
- item_band: int32 [4], replicated, may hold values from 0 to 3, as said below
- item_length: int32 [4], replicated, may hold values from 512 to 1024, as said below
- item_width: int32 [4], replicated, may hold values from 16 to 64
- text_states: bfloat16 [1024, 4096], P('seq'), may hold values from -6 to 6
- ada_weight: bfloat16 [1024, 6144], P(None, 'tp'), may hold values from -0.1875 to 0.1875
- ada_bias: float32 [6144], P('tp'), may hold values from -1.5 to 1.5
- attn_gain: float32 [1536], replicated, may hold values from 0.5 to 1.5
- ffn_gain: float32 [1536], replicated, may hold values from 0.5 to 1.5
- query_weight: bfloat16 [1536, 1536], P(None, 'tp'), may hold values from -0.15625 to 0.15625
- key_weight: bfloat16 [1536, 1536], P(None, 'tp'), may hold values from -0.15625 to 0.15625
- value_weight: bfloat16 [1536, 1536], P(None, 'tp'), may hold values from -0.15625 to 0.15625
- query_gain: float32 [1536], P('tp'), may hold values from 1 to 2
- key_gain: float32 [1536], P('tp'), may hold values from 1 to 2
- cross_gate: float32 [24], P('tp'), may hold values from 0.3 to 1.2
- text_key_weight: bfloat16 [4096, 1536], P(None, 'tp'), may hold values from -0.09375 to 0.09375
- text_value_weight: bfloat16 [4096, 1536], P(None, 'tp'), may hold values from -0.09375 to 0.09375
- text_key_gain: float32 [1536], P('tp'), may hold values from 1 to 2
- out_weight: bfloat16 [1536, 1536], P('tp'), may hold values from -3.5 to 3.5
- gate_weight: bfloat16 [1536, 4096], P(None, 'tp'), may hold values from -0.15625 to 0.15625
- up_weight: bfloat16 [1536, 4096], P(None, 'tp'), may hold values from -0.15625 to 0.15625
- down_weight: bfloat16 [4096, 1536], P('tp'), may hold values from -0.09375 to 0.09375
Outputs:
- block_out: bfloat16 [4096, 1536], P('seq')
- tokens_grad: bfloat16 [4096, 1536], P('seq')
- text_grad: float32 [1024, 4096], P('seq', 'tp')
- ada_weight_grad: float32 [1024, 6144], P('seq', 'tp')
- ada_bias_grad: float32 [6144], P('tp')
- attn_gain_grad: float32 [1536], replicated
- ffn_gain_grad: float32 [1536], replicated
- query_weight_grad: float32 [1536, 1536], P('seq', 'tp')
- key_weight_grad: float32 [1536, 1536], P('seq', 'tp')
- value_weight_grad: float32 [1536, 1536], P('seq', 'tp')
- query_gain_grad: float32 [1536], P('tp')
- key_gain_grad: float32 [1536], P('tp')
- cross_gate_grad: float32 [24], P('tp')
- text_key_weight_grad: float32 [4096, 1536], P('seq', 'tp')
- text_value_weight_grad: float32 [4096, 1536], P('seq', 'tp')
- text_key_gain_grad: float32 [1536], P('tp')
- out_weight_grad: float32 [1536, 1536], P('tp', 'seq')
- gate_weight_grad: float32 [1536, 4096], P('seq', 'tp')
- up_weight_grad: float32 [1536, 4096], P('seq', 'tp')
- down_weight_grad: float32 [4096, 1536], P('tp', 'seq')
The draws below stay inside these ranges and needn't reach their ends.
Inputs may be any that keep to these rules, and one draw needn't show every extreme that they name: `item_band`: every band is used by some item. Item i's real tokens are its first item_length[i] positions; one item fills all 1024 positions and another has exactly 512.
All inputs are finite; a program needn't handle non-finite values.
Results may differ from the reference program's by a relative error of at most 0.024.
Values may be sent and summed in bfloat16 or wider, within the bound.
No kernel may reach another device: no remote copies, remote signals or barrier semaphores. Data moves between devices by JAX's collectives and lax.ppermute only.
A program may use at most 256 MiB of HBM per device.

```python
import jax
import jax.numpy as jnp
from jax import lax

D = 1536
HEADS = 24
HDIM = 64
FF = 4096
TW = 4096
TE = 1024
NTXT = 256
BANDS = 4
ITEMS = 4
SLOT = 64
ITEM_CAP = 1024
TOKENS = 4096
TXT_ROWS = 1024
N_SEQ = 16


def draw_item_band(key, part):
    key = jax.random.fold_in(key, 11)
    order_key, free_key, offset_key = jax.random.split(key, 3)
    order = jax.random.permutation(order_key, ITEMS)
    free_bands = jax.random.randint(free_key, (ITEMS,), 0, BANDS)
    offset = jax.random.randint(offset_key, (), 0, BANDS)
    bands = jnp.where(order < BANDS, (order + offset) % BANDS, free_bands)
    return bands.astype(jnp.int32)


def draw_item_length(key, part):
    key = jax.random.fold_in(key, 7)
    base_key, pick_key = jax.random.split(key)
    lengths = jax.random.randint(base_key, (ITEMS,), ITEM_CAP // 2, ITEM_CAP + 1)
    ranking = jax.random.permutation(pick_key, ITEMS)
    lengths = jnp.where(ranking == 0, ITEM_CAP, lengths)
    lengths = jnp.where(ranking == 1, ITEM_CAP // 2, lengths)
    return lengths.astype(jnp.int32)


def plant(drawn, key, least, largest):
    dims = drawn.shape
    place = [jax.random.randint(jax.random.fold_in(key, axis), (), 0, dims[axis]) for axis in range(len(dims))]
    drawn = drawn.at[tuple(place)].set(least)
    longest = dims.index(max(dims))
    place[longest] = (place[longest] + 1) % dims[longest]
    return drawn.at[tuple(place)].set(largest)


def shard_levels(own_key, dims, cuts, smallest, high):
    loudness = 1.0
    for dim, parts in cuts:
        draws = jax.random.uniform(jax.random.fold_in(jax.random.fold_in(own_key, 6), dim), (parts,), jnp.float32, smallest / len(cuts), high / len(cuts))
        loudness = loudness * jnp.repeat(jnp.exp(draws), dims[dim] // parts).reshape((-1,) + (1,) * (len(dims) - 1 - dim))
    return loudness


def noise(key, dims, deviation, reach, shards=(), held_as=jnp.bfloat16):
    values = deviation * jax.random.normal(key, dims, jnp.float32)
    if shards:
        values = values * shard_levels(key, dims, shards, -0.22, 0.18)
    return jnp.clip(values, -reach, reach).astype(held_as)


def setup_inputs(seed: int = 0) -> dict:
    key_list = jax.random.split(jax.random.key(seed), 25)
    tokens = noise(key_list[0], (TOKENS, D), 1.0, 6.0, ((0, 16),))
    cotangent = noise(key_list[1], (TOKENS, D), 1.0, 6.0, ((0, 16),))
    step_embed = noise(key_list[2], (BANDS, TE), 1.0, 6.0)
    item_band = draw_item_band(jax.random.fold_in(key_list[24], 71), 0)
    item_length = draw_item_length(jax.random.fold_in(key_list[24], 71), 0)
    item_width = plant(jax.random.randint(key_list[5], (ITEMS,), 16, 65), jax.random.fold_in(key_list[5], 1), 16, 64).astype(jnp.int32)
    text_states = noise(key_list[6], (TXT_ROWS, TW), 1.0, 6.0, ((0, 16),))
    ada_weight = noise(key_list[7], (TE, 4 * D), TE ** -0.5, 0.1875, ((1, 2),))
    ada_bias = noise(key_list[8], (4 * D,), 0.3, 1.5, ((0, 2),), jnp.float32)
    attn_gain = jnp.clip(1.0 + 0.1 * jax.random.normal(key_list[9], (D,), jnp.float32), 0.5, 1.5)
    ffn_gain = jnp.clip(1.0 + 0.1 * jax.random.normal(key_list[10], (D,), jnp.float32), 0.5, 1.5)
    query_weight = noise(key_list[11], (D, D), D ** -0.5, 0.15625, ((1, 2),))
    key_weight = noise(key_list[12], (D, D), D ** -0.5, 0.15625, ((1, 2),))
    value_weight = noise(key_list[13], (D, D), D ** -0.5, 0.15625, ((1, 2),))
    query_gain = jnp.clip(1.0 + 1.0 * jax.random.uniform(key_list[14], (D,), jnp.float32) ** shard_levels(key_list[14], (D,), ((0, 2),), -0.2, 0.2), 1.0, 2.0)
    key_gain = jnp.clip(1.0 + 1.0 * jax.random.uniform(key_list[15], (D,), jnp.float32) ** shard_levels(key_list[15], (D,), ((0, 2),), -0.2, 0.2), 1.0, 2.0)
    cross_gate = jnp.clip(0.3 + 0.90000004 * jax.random.uniform(key_list[16], (HEADS,), jnp.float32) ** shard_levels(key_list[16], (HEADS,), ((0, 2),), -0.2, 0.2), 0.3, 1.2)
    text_key_weight = noise(key_list[17], (TW, D), TW ** -0.5, 0.09375, ((1, 2),))
    text_value_weight = noise(key_list[18], (TW, D), TW ** -0.5, 0.09375, ((1, 2),))
    text_key_gain = jnp.clip(1.0 + 1.0 * jax.random.uniform(key_list[19], (D,), jnp.float32) ** shard_levels(key_list[19], (D,), ((0, 2),), -0.2, 0.2), 1.0, 2.0)
    out_weight = noise(key_list[20], (D, D), (max(D // 512, 1)) ** -0.5, 3.5, ((0, 2),))
    gate_weight = noise(key_list[21], (D, FF), D ** -0.5, 0.15625, ((1, 2),))
    up_weight = noise(key_list[22], (D, FF), D ** -0.5, 0.15625, ((1, 2),))
    down_weight = noise(key_list[23], (FF, D), FF ** -0.5, 0.09375, ((0, 2),))
    return {"tokens": tokens, "cotangent": cotangent, "step_embed": step_embed, "item_band": item_band, "item_length": item_length, "item_width": item_width, "text_states": text_states, "ada_weight": ada_weight, "ada_bias": ada_bias, "attn_gain": attn_gain, "ffn_gain": ffn_gain, "query_weight": query_weight, "key_weight": key_weight, "value_weight": value_weight, "query_gain": query_gain, "key_gain": key_gain, "cross_gate": cross_gate, "text_key_weight": text_key_weight, "text_value_weight": text_value_weight, "text_key_gain": text_key_gain, "out_weight": out_weight, "gate_weight": gate_weight, "up_weight": up_weight, "down_weight": down_weight}


EPSILON = 1e-06
ROPE_BASE = 10000.0
HIGHEST = lax.Precision.HIGHEST
NEG_FILL = -1e+30

@jax.custom_vjp
def low(v):
    return lax.optimization_barrier(v.astype(jnp.bfloat16)).astype(jnp.float32)

@jax.custom_vjp
def low_back(v):
    return v

def low_keep(v):
    return (low(v), None)

def low_pass(kept, grad):
    return (grad,)

def back_keep(v):
    return (v, None)

def back_low(kept, grad):
    return (low(grad),)
low.defvjp(low_keep, low_pass)
low_back.defvjp(back_keep, back_low)

def matmul(left, right):
    return jnp.dot(left, right, precision=HIGHEST)

def rms_inverse(values):
    return lax.rsqrt(lax.optimization_barrier(jnp.mean(values * values, axis=-1, keepdims=True)) + EPSILON)

def rope_angles(row_pos, col_pos, head_dim):
    quarter = head_dim // 4
    frequency = ROPE_BASE ** (-jnp.arange(quarter, dtype=jnp.float32) / quarter)
    angles = jnp.stack([row_pos[..., None] * frequency, col_pos[..., None] * frequency], axis=-2)
    return (jnp.cos(angles), jnp.sin(angles))

def rotate(vectors, cosines, sines):
    shape_all = vectors.shape
    paired = vectors.reshape(shape_all[:-1] + (2, 2, shape_all[-1] // 4))
    former = paired[..., 0, :]
    latter = paired[..., 1, :]
    turned = jnp.stack([former * cosines - latter * sines, former * sines + latter * cosines], axis=-2)
    return turned.reshape(shape_all)

def head_norm(raw_vals, gain_vec):
    return raw_vals * rms_inverse(raw_vals) * gain_vec

def softmax_rows(scores):
    row_max = lax.optimization_barrier(jnp.max(scores, axis=-1, keepdims=True))
    exp_scores = jnp.exp(scores - row_max)
    return exp_scores / lax.optimization_barrier(jnp.sum(exp_scores, axis=-1, keepdims=True))

def head_attention(operands):
    query_h, key_h, value_h, tkey_h, tvalue_h, key_mask = operands
    scaling = query_h.shape[-1] ** (-0.5)
    scores = low_back(jnp.dot(query_h, key_h.T, precision=HIGHEST) * scaling)
    scores = jnp.where(key_mask[None, :] > 0.5, scores, NEG_FILL)
    self_out = low_back(jnp.dot(low(softmax_rows(scores)), value_h, precision=HIGHEST))
    cross_scores = low_back(jnp.dot(query_h, tkey_h.T, precision=HIGHEST) * scaling)
    cross_out = low_back(jnp.dot(low(softmax_rows(cross_scores)), tvalue_h, precision=HIGHEST))
    return (self_out, cross_out)

def reference(tokens, cotangent, step_embed, item_band, item_length, item_width, text_states, ada_weight, ada_bias, attn_gain, ffn_gain, query_weight, key_weight, value_weight, query_gain, key_gain, cross_gate, text_key_weight, text_value_weight, text_key_gain, out_weight, gate_weight, up_weight, down_weight):
    capacity = SLOT * N_SEQ
    silu_embed = jax.nn.silu(step_embed.astype(jnp.float32))
    positions = jnp.arange(capacity, dtype=jnp.int32)
    row_pos = (positions[None, :] // item_width[:, None]).astype(jnp.float32)
    col_pos = (positions[None, :] % item_width[:, None]).astype(jnp.float32)
    cosines, sines = rope_angles(row_pos, col_pos, HDIM)
    cosines = cosines[:, :, None]
    sines = sines[:, :, None]
    key_valid = (positions[None, :] < item_length[:, None]).astype(jnp.float32)
    valid_heads = jnp.repeat(key_valid, HEADS, axis=0)

    def to_items(array_in):
        return array_in.reshape(N_SEQ, ITEMS, SLOT, -1).transpose(1, 0, 2, 3).reshape(ITEMS, capacity, -1)

    def from_items(array_in):
        return array_in.reshape(ITEMS, N_SEQ, SLOT, -1).transpose(1, 0, 2, 3).reshape(N_SEQ * ITEMS * SLOT, -1)

    def stack_heads(array_in, length):
        return jnp.moveaxis(array_in.reshape(ITEMS, length, HEADS, HDIM), 2, 1).reshape(ITEMS * HEADS, length, HDIM)

    def forward(token_rows, text_rows, ada_weight, ada_bias, attn_gain, ffn_gain, query_weight, key_weight, value_weight, query_gain, key_gain, cross_gate, text_key_weight, text_value_weight, text_key_gain, out_weight, gate_weight, up_weight, down_weight):
        band_mod = matmul(silu_embed, ada_weight) + ada_bias
        item_mod = band_mod[item_band]
        scale_attn = item_mod[:, None, 0:D]
        gate_attn = jnp.tanh(item_mod[:, None, D:2 * D])
        scale_ffn = item_mod[:, None, 2 * D:3 * D]
        gate_ffn = jnp.tanh(item_mod[:, None, 3 * D:])
        residual = to_items(token_rows)
        attn_in = low(residual * rms_inverse(residual) * attn_gain * (1.0 + scale_attn))
        head_shape = (ITEMS, capacity, HEADS, HDIM)
        query_raw = low_back(matmul(attn_in, query_weight)).reshape(head_shape)
        key_raw = low_back(matmul(attn_in, key_weight)).reshape(head_shape)
        value_low = low(low_back(matmul(attn_in, value_weight)))
        query_low = low(rotate(head_norm(query_raw, query_gain.reshape(HEADS, HDIM)), cosines, sines))
        key_low = low(rotate(head_norm(key_raw, key_gain.reshape(HEADS, HDIM)), cosines, sines))
        text_key_raw = low_back(matmul(text_rows, text_key_weight)).reshape(ITEMS * NTXT, HEADS, HDIM)
        text_key = low(head_norm(text_key_raw, text_key_gain.reshape(HEADS, HDIM)))
        text_value = low(low_back(matmul(text_rows, text_value_weight)))
        self_out, cross_out = lax.map(jax.checkpoint(head_attention), (stack_heads(query_low, capacity), stack_heads(key_low, capacity), stack_heads(value_low, capacity), stack_heads(text_key, NTXT), stack_heads(text_value, NTXT), valid_heads))
        gate_tanh = jnp.tanh(cross_gate)
        combined = self_out.reshape(ITEMS, HEADS, capacity, HDIM) + gate_tanh[None, :, None, None] * cross_out.reshape(ITEMS, HEADS, capacity, HDIM)
        combined_low = low(jnp.moveaxis(combined, 1, 2).reshape(ITEMS, capacity, D))
        attn_branch = low_back(matmul(combined_low, out_weight))
        middle = residual + gate_attn * attn_branch
        ffn_in = low(middle * rms_inverse(middle) * ffn_gain * (1.0 + scale_ffn))
        gate_pre = low_back(matmul(ffn_in, gate_weight))
        up_pre = low_back(matmul(ffn_in, up_weight))
        hidden = low(jax.nn.silu(gate_pre) * up_pre)
        ffn_branch = low_back(matmul(hidden, down_weight))
        layer_sum = middle + gate_ffn * ffn_branch
        return from_items(layer_sum)
    primal = [array_in.astype(jnp.float32) for array_in in (tokens, text_states, ada_weight, ada_bias, attn_gain, ffn_gain, query_weight, key_weight, value_weight, query_gain, key_gain, cross_gate, text_key_weight, text_value_weight, text_key_gain, out_weight, gate_weight, up_weight, down_weight)]
    layer_sum, pullback = jax.vjp(forward, *primal)
    gradients = pullback(cotangent.astype(jnp.float32))
    return (layer_sum.astype(jnp.bfloat16), gradients[0].astype(jnp.bfloat16), gradients[1], gradients[2], gradients[3], gradients[4], gradients[5], gradients[6], gradients[7], gradients[8], gradients[9], gradients[10], gradients[11], gradients[12], gradients[13], gradients[14], gradients[15], gradients[16], gradients[17], gradients[18])
```

```python
import jax
import jax.numpy as jnp
from jax import lax
from jax.experimental import pallas as pl
from jax.experimental.pallas import tpu as pltpu
from jax.sharding import Mesh
from jax.sharding import PartitionSpec as P

HDIM = 64
NTXT = 256
BANDS = 4
ITEMS = 4
SLOT = 64


EPSILON = 1e-06
ROPE_BASE = 10000.0
HIGHEST = lax.Precision.HIGHEST
NEG_FILL = -1e30


def rms_inverse(values):
    return lax.rsqrt(jnp.mean(values * values, axis=-1, keepdims=True) + EPSILON)


def rope_angles(row_pos, col_pos, head_dim):
    quarter = head_dim // 4
    frequency = ROPE_BASE ** (-jnp.arange(quarter, dtype=jnp.float32) / quarter)
    angles = jnp.stack([row_pos[..., None] * frequency, col_pos[..., None] * frequency], axis=-2)
    return (jnp.cos(angles), jnp.sin(angles))


def rotate(vectors, cosines, sines):
    shape_all = vectors.shape
    paired = vectors.reshape(shape_all[:-1] + (2, 2, shape_all[-1] // 4))
    former = paired[..., 0, :]
    latter = paired[..., 1, :]
    turned = jnp.stack(
        [former * cosines - latter * sines, former * sines + latter * cosines], axis=-2
    )
    return turned.reshape(shape_all)


def head_norm(raw_vals, gain_vec):
    inverse = rms_inverse(raw_vals)
    unit_vec = raw_vals * inverse
    return (unit_vec * gain_vec, unit_vec, inverse)


def head_norm_back(incoming, unit_vec, inverse, gain_vec):
    grad_unit = incoming * gain_vec
    gain_part = jnp.sum(incoming * unit_vec, axis=tuple(range(incoming.ndim - 2)))
    grad_raw = inverse * (
        grad_unit - unit_vec * jnp.mean(grad_unit * unit_vec, axis=-1, keepdims=True)
    )
    return (grad_raw, gain_part)


def token_norm_back(incoming, normed, inverse, gain_vec, scale_mod):
    lifted = 1.0 + scale_mod
    gain_part = jnp.sum(incoming * normed * lifted, axis=(0, 1))
    scale_part = jnp.sum(incoming * normed * gain_vec, axis=1)
    grad_normed = incoming * gain_vec * lifted
    grad_in = inverse * (
        grad_normed - normed * jnp.mean(grad_normed * normed, axis=-1, keepdims=True)
    )
    return (grad_in, gain_part, scale_part)


def attend(query_h, key_h, value_h, key_valid):
    scaling = query_h.shape[-1] ** (-0.5)
    scores = (
        jnp.einsum("isd,ikd->isk", query_h, key_h, preferred_element_type=jnp.float32) * scaling
    )
    if key_valid is not None:
        scores = jnp.where(key_valid[:, None, :], scores, NEG_FILL)
    row_max = jnp.max(scores, axis=-1, keepdims=True)
    exp_scores = jnp.exp(scores - row_max)
    row_total = jnp.sum(exp_scores, axis=-1, keepdims=True)
    probability = (exp_scores / row_total).astype(jnp.bfloat16)
    output = jnp.einsum("isk,ikd->isd", probability, value_h, preferred_element_type=jnp.float32)
    return (output, (row_max + jnp.log(row_total))[..., 0])


def attend_back(query_h, key_h, value_h, key_valid, lse_h, dout_h):
    scaling = query_h.shape[-1] ** (-0.5)
    scores = (
        jnp.einsum("isd,ikd->isk", query_h, key_h, preferred_element_type=jnp.float32) * scaling
    )
    if key_valid is not None:
        scores = jnp.where(key_valid[:, None, :], scores, NEG_FILL)
    probability = jnp.exp(scores - lse_h[..., None])
    d_prob = jnp.einsum("isd,ikd->isk", dout_h, value_h, preferred_element_type=jnp.float32)
    delta_row = jnp.sum(d_prob * probability, axis=-1)
    d_score = (probability * (d_prob - delta_row[..., None])).astype(jnp.bfloat16)
    d_query = (
        jnp.einsum("isk,ikd->isd", d_score, key_h, preferred_element_type=jnp.float32) * scaling
    )
    d_key = (
        jnp.einsum("isk,isd->ikd", d_score, query_h, preferred_element_type=jnp.float32) * scaling
    )
    d_value = jnp.einsum(
        "isk,isd->ikd", probability.astype(jnp.bfloat16), dout_h, preferred_element_type=jnp.float32
    )
    return (d_query, delta_row, d_key, d_value)


def head_total(partial_value):
    return lax.psum(partial_value.astype(jnp.bfloat16), "tp").astype(jnp.float32)


def feature_total(partial_value):
    return lax.psum(partial_value.astype(jnp.bfloat16), "tp").astype(jnp.float32)


def shards(
    tokens,
    cotangent,
    step_embed,
    item_band,
    item_length,
    item_width,
    text_states,
    ada_weight,
    ada_bias,
    attn_gain,
    ffn_gain,
    query_weight,
    key_weight,
    value_weight,
    query_gain,
    key_gain,
    cross_gate,
    text_key_weight,
    text_value_weight,
    text_key_gain,
    out_weight,
    gate_weight,
    up_weight,
    down_weight,
):
    seq_count = lax.axis_size("seq")
    seq_index = lax.axis_index("seq")
    tp_index = lax.axis_index("tp")
    tok_dev, model_width = tokens.shape
    local_width = query_weight.shape[1]
    local_heads = local_width // HDIM
    capacity = SLOT * seq_count
    text_rows = text_states.shape[0]
    mod_cols = ada_weight.shape[1]
    head_shape = (ITEMS, SLOT, local_heads, HDIM)
    silu_embed = jax.nn.silu(step_embed.astype(jnp.float32))
    local_mod = jnp.dot(silu_embed, ada_weight.astype(jnp.float32), precision=HIGHEST) + ada_bias
    band_mod = lax.all_gather(local_mod, "tp", axis=1, tiled=True)
    band_onehot = (item_band[:, None] == jnp.arange(BANDS, dtype=jnp.int32)[None, :]).astype(
        jnp.float32
    )
    item_mod = jnp.dot(band_onehot, band_mod, precision=HIGHEST)
    scale_attn = item_mod[:, None, 0:model_width]
    gate_attn = jnp.tanh(item_mod[:, None, model_width : 2 * model_width])
    scale_ffn = item_mod[:, None, 2 * model_width : 3 * model_width]
    gate_ffn = jnp.tanh(item_mod[:, None, 3 * model_width :])
    slot_pos = seq_index * SLOT + jnp.arange(SLOT, dtype=jnp.int32)
    row_pos = (slot_pos[None, :] // item_width[:, None]).astype(jnp.float32)
    col_pos = (slot_pos[None, :] % item_width[:, None]).astype(jnp.float32)
    cosines, sines = rope_angles(row_pos, col_pos, HDIM)
    cosines = cosines[:, :, None]
    sines = sines[:, :, None]
    key_valid = jnp.arange(capacity, dtype=jnp.int32)[None, :] < item_length[:, None]

    def by_heads(array_in, row_count):
        return jnp.moveaxis(array_in.reshape(ITEMS, row_count, local_heads, HDIM), 2, 0)

    text_key_raw = jnp.dot(
        text_states, text_key_weight, preferred_element_type=jnp.float32
    ).reshape(text_rows, local_heads, HDIM)
    text_gain_vec = text_key_gain.reshape(local_heads, HDIM)
    text_key_normed, text_unit, text_inverse = head_norm(text_key_raw, text_gain_vec)
    text_key_low = text_key_normed.reshape(text_rows, local_width).astype(jnp.bfloat16)
    text_value_low = jnp.dot(
        text_states, text_value_weight, preferred_element_type=jnp.float32
    ).astype(jnp.bfloat16)
    text_key_all, text_value_all = (
        lax.all_gather(text_key_low, "seq", axis=0, tiled=True),
        lax.all_gather(text_value_low, "seq", axis=0, tiled=True),
    )
    residual = tokens.astype(jnp.float32).reshape(ITEMS, SLOT, model_width)
    inverse_one = rms_inverse(residual)
    normed_one = residual * inverse_one
    attn_in = (
        (normed_one * attn_gain * (1.0 + scale_attn))
        .astype(jnp.bfloat16)
        .reshape(tok_dev, model_width)
    )
    query_raw = jnp.dot(attn_in, query_weight, preferred_element_type=jnp.float32).reshape(
        head_shape
    )
    key_raw = jnp.dot(attn_in, key_weight, preferred_element_type=jnp.float32).reshape(head_shape)
    value_low = (
        jnp.dot(attn_in, value_weight, preferred_element_type=jnp.float32)
        .astype(jnp.bfloat16)
        .reshape(ITEMS, SLOT, local_width)
    )
    query_gain_vec = query_gain.reshape(local_heads, HDIM)
    key_gain_vec = key_gain.reshape(local_heads, HDIM)
    query_normed, query_unit, query_inverse = head_norm(query_raw, query_gain_vec)
    key_normed, key_unit, key_inverse = head_norm(key_raw, key_gain_vec)
    query_low = rotate(query_normed, cosines, sines).astype(jnp.bfloat16)
    key_low = (
        rotate(key_normed, cosines, sines).astype(jnp.bfloat16).reshape(ITEMS, SLOT, local_width)
    )
    key_all, value_all = (
        lax.all_gather(key_low, "seq", axis=1, tiled=True),
        lax.all_gather(value_low, "seq", axis=1, tiled=True),
    )
    query_heads = jnp.moveaxis(query_low, 2, 0)
    key_heads = by_heads(key_all, capacity)
    value_heads = by_heads(value_all, capacity)
    text_key_heads = by_heads(text_key_all, NTXT)
    text_value_heads = by_heads(text_value_all, NTXT)

    def forward_head(operands):
        query_h, key_h, value_h, tkey_h, tvalue_h = operands
        self_part, self_stat = attend(query_h, key_h, value_h, key_valid)
        cross_part, cross_stat = attend(query_h, tkey_h, tvalue_h, None)
        return (self_part, self_stat, cross_part, cross_stat)

    self_out, self_lse, cross_out, cross_lse = lax.map(
        forward_head, (query_heads, key_heads, value_heads, text_key_heads, text_value_heads)
    )
    cross_tanh = jnp.tanh(cross_gate)
    combined = self_out + cross_tanh[:, None, None, None] * cross_out
    combined_low = jnp.moveaxis(combined, 0, 2).reshape(tok_dev, local_width).astype(jnp.bfloat16)
    attn_branch = head_total(
        jnp.dot(combined_low, out_weight, preferred_element_type=jnp.float32)
    ).reshape(ITEMS, SLOT, model_width)
    middle = residual + gate_attn * attn_branch
    inverse_two = rms_inverse(middle)
    normed_two = middle * inverse_two
    ffn_in = (
        (normed_two * ffn_gain * (1.0 + scale_ffn))
        .astype(jnp.bfloat16)
        .reshape(tok_dev, model_width)
    )
    gate_pre = jnp.dot(ffn_in, gate_weight, preferred_element_type=jnp.float32)
    up_pre = jnp.dot(ffn_in, up_weight, preferred_element_type=jnp.float32)
    gate_sig = jax.nn.sigmoid(gate_pre)
    hidden = (gate_pre * gate_sig * up_pre).astype(jnp.bfloat16)
    ffn_branch = head_total(
        jnp.dot(hidden, down_weight, preferred_element_type=jnp.float32)
    ).reshape(ITEMS, SLOT, model_width)
    layer_sum = middle + gate_ffn * ffn_branch
    block_out = layer_sum.reshape(tok_dev, model_width).astype(jnp.bfloat16)
    incoming = cotangent.astype(jnp.float32).reshape(ITEMS, SLOT, model_width)
    gate_ffn_tok = incoming * ffn_branch
    d_ffn = (gate_ffn * incoming).reshape(tok_dev, model_width).astype(jnp.bfloat16)
    down_grad = jnp.dot(hidden.T, d_ffn, preferred_element_type=jnp.float32)
    d_hidden = jnp.dot(d_ffn, down_weight.T, preferred_element_type=jnp.float32)
    d_gate_pre = (d_hidden * up_pre * gate_sig * (1.0 + gate_pre * (1.0 - gate_sig))).astype(
        jnp.bfloat16
    )
    d_up_pre = (d_hidden * gate_pre * gate_sig).astype(jnp.bfloat16)
    gate_grad = jnp.dot(ffn_in.T, d_gate_pre, preferred_element_type=jnp.float32)
    up_grad = jnp.dot(ffn_in.T, d_up_pre, preferred_element_type=jnp.float32)
    d_ffn_in = feature_total(
        jnp.dot(d_gate_pre, gate_weight.T, preferred_element_type=jnp.float32)
        + jnp.dot(d_up_pre, up_weight.T, preferred_element_type=jnp.float32)
    )
    d_middle_norm, ffn_gain_part, scale_ffn_part = token_norm_back(
        d_ffn_in.reshape(ITEMS, SLOT, model_width), normed_two, inverse_two, ffn_gain, scale_ffn
    )
    d_middle = incoming + d_middle_norm
    gate_attn_tok = d_middle * attn_branch
    d_attn = (gate_attn * d_middle).reshape(tok_dev, model_width).astype(jnp.bfloat16)
    out_grad = jnp.dot(combined_low.T, d_attn, preferred_element_type=jnp.float32)
    d_combined = jnp.moveaxis(
        jnp.dot(d_attn, out_weight.T, preferred_element_type=jnp.float32).reshape(head_shape), 2, 0
    )
    cross_gate_part = jnp.sum(d_combined * cross_out, axis=(1, 2, 3)) * (
        1.0 - cross_tanh * cross_tanh
    )
    d_self = d_combined.astype(jnp.bfloat16)
    d_cross = (d_combined * cross_tanh[:, None, None, None]).astype(jnp.bfloat16)

    def cross_head(operands):
        query_h, tkey_h, tvalue_h, lse_h, dout_h = operands
        d_query, unused_delta, d_key, d_value = attend_back(
            query_h, tkey_h, tvalue_h, None, lse_h, dout_h
        )
        return (d_query, d_key, d_value)

    d_query_cross, d_text_key_heads, d_text_value_heads = lax.map(
        cross_head, (query_heads, text_key_heads, text_value_heads, cross_lse, d_cross)
    )

    def full_head(operands):
        query_h, key_h, value_h, lse_h, dout_h = operands
        d_query, unused_delta, d_key, d_value = attend_back(
            query_h, key_h, value_h, key_valid, lse_h, dout_h
        )
        return (d_query, d_key, d_value)

    d_query_self, d_key_heads, d_value_heads = lax.map(
        full_head, (query_heads, key_heads, value_heads, self_lse, d_self)
    )
    d_key_own, d_value_own = (
        lax.psum_scatter(
            jnp.moveaxis(d_key_heads, 0, 2)
            .reshape(ITEMS, capacity, local_width)
            .astype(jnp.bfloat16),
            "seq",
            scatter_dimension=1,
            tiled=True,
        ).astype(jnp.float32),
        lax.psum_scatter(
            jnp.moveaxis(d_value_heads, 0, 2)
            .reshape(ITEMS, capacity, local_width)
            .astype(jnp.bfloat16),
            "seq",
            scatter_dimension=1,
            tiled=True,
        ).astype(jnp.float32),
    )
    d_key_rot = d_key_own.reshape(head_shape)
    d_query_rot = jnp.moveaxis(d_query_self + d_query_cross, 0, 2)
    d_query_raw, query_gain_part = head_norm_back(
        rotate(d_query_rot, cosines, -sines), query_unit, query_inverse, query_gain_vec
    )
    d_key_raw, key_gain_part = head_norm_back(
        rotate(d_key_rot, cosines, -sines), key_unit, key_inverse, key_gain_vec
    )
    d_query_low = d_query_raw.reshape(tok_dev, local_width).astype(jnp.bfloat16)
    d_key_low = d_key_raw.reshape(tok_dev, local_width).astype(jnp.bfloat16)
    d_value_low = d_value_own.reshape(tok_dev, local_width).astype(jnp.bfloat16)
    query_grad = jnp.dot(attn_in.T, d_query_low, preferred_element_type=jnp.float32)
    key_grad = jnp.dot(attn_in.T, d_key_low, preferred_element_type=jnp.float32)
    value_grad = jnp.dot(attn_in.T, d_value_low, preferred_element_type=jnp.float32)
    d_attn_in = feature_total(
        jnp.dot(d_query_low, query_weight.T, preferred_element_type=jnp.float32)
        + jnp.dot(d_key_low, key_weight.T, preferred_element_type=jnp.float32)
        + jnp.dot(d_value_low, value_weight.T, preferred_element_type=jnp.float32)
    )
    d_input_norm, attn_gain_part, scale_attn_part = token_norm_back(
        d_attn_in.reshape(ITEMS, SLOT, model_width), normed_one, inverse_one, attn_gain, scale_attn
    )
    tokens_grad = (d_middle + d_input_norm).reshape(tok_dev, model_width).astype(jnp.bfloat16)
    d_text_key_own, d_text_value_own = (
        lax.psum_scatter(
            jnp.moveaxis(d_text_key_heads, 0, 2)
            .reshape(ITEMS * NTXT, local_width)
            .astype(jnp.bfloat16),
            "seq",
            scatter_dimension=0,
            tiled=True,
        ).astype(jnp.float32),
        lax.psum_scatter(
            jnp.moveaxis(d_text_value_heads, 0, 2)
            .reshape(ITEMS * NTXT, local_width)
            .astype(jnp.bfloat16),
            "seq",
            scatter_dimension=0,
            tiled=True,
        ).astype(jnp.float32),
    )
    d_text_key_raw, text_gain_part = head_norm_back(
        d_text_key_own.reshape(text_rows, local_heads, HDIM), text_unit, text_inverse, text_gain_vec
    )
    d_text_key_low = d_text_key_raw.reshape(text_rows, local_width).astype(jnp.bfloat16)
    d_text_value_low = d_text_value_own.astype(jnp.bfloat16)
    text_key_grad = jnp.dot(text_states.T, d_text_key_low, preferred_element_type=jnp.float32)
    text_value_grad = jnp.dot(text_states.T, d_text_value_low, preferred_element_type=jnp.float32)
    text_grad = lax.psum_scatter(
        (
            jnp.dot(d_text_key_low, text_key_weight.T, preferred_element_type=jnp.float32)
            + jnp.dot(d_text_value_low, text_value_weight.T, preferred_element_type=jnp.float32)
        ).astype(jnp.bfloat16),
        "tp",
        scatter_dimension=1,
        tiled=True,
    ).astype(jnp.float32)
    gate_attn_item = jnp.sum(gate_attn_tok, axis=1) * (1.0 - gate_attn[:, 0] * gate_attn[:, 0])
    gate_ffn_item = jnp.sum(gate_ffn_tok, axis=1) * (1.0 - gate_ffn[:, 0] * gate_ffn[:, 0])
    item_grad = jnp.concatenate(
        [scale_attn_part, gate_attn_item, scale_ffn_part, gate_ffn_item], axis=1
    )
    band_grad = jnp.dot(band_onehot.T, item_grad, precision=HIGHEST)
    local_band_grad = lax.dynamic_slice_in_dim(band_grad, tp_index * mod_cols, mod_cols, 1)
    ada_grad = jnp.dot(silu_embed.T, local_band_grad, precision=HIGHEST)
    ada_bias_part = jnp.sum(local_band_grad, axis=0)
    summed = (
        lax.psum_scatter(
            query_grad.astype(jnp.bfloat16), "seq", scatter_dimension=0, tiled=True
        ).astype(jnp.float32),
        lax.psum_scatter(
            key_grad.astype(jnp.bfloat16), "seq", scatter_dimension=0, tiled=True
        ).astype(jnp.float32),
        lax.psum_scatter(
            value_grad.astype(jnp.bfloat16), "seq", scatter_dimension=0, tiled=True
        ).astype(jnp.float32),
        lax.psum_scatter(
            gate_grad.astype(jnp.bfloat16), "seq", scatter_dimension=0, tiled=True
        ).astype(jnp.float32),
        lax.psum_scatter(
            up_grad.astype(jnp.bfloat16), "seq", scatter_dimension=0, tiled=True
        ).astype(jnp.float32),
        lax.psum_scatter(
            text_key_grad.astype(jnp.bfloat16), "seq", scatter_dimension=0, tiled=True
        ).astype(jnp.float32),
        lax.psum_scatter(
            text_value_grad.astype(jnp.bfloat16), "seq", scatter_dimension=0, tiled=True
        ).astype(jnp.float32),
        lax.psum_scatter(
            ada_grad.astype(jnp.bfloat16), "seq", scatter_dimension=0, tiled=True
        ).astype(jnp.float32),
        lax.psum_scatter(
            out_grad.astype(jnp.bfloat16), "seq", scatter_dimension=1, tiled=True
        ).astype(jnp.float32),
        lax.psum_scatter(
            down_grad.astype(jnp.bfloat16), "seq", scatter_dimension=1, tiled=True
        ).astype(jnp.float32),
    )
    smalls = lax.psum(
        (
            attn_gain_part,
            ffn_gain_part,
            query_gain_part.reshape(local_width),
            key_gain_part.reshape(local_width),
            text_gain_part.reshape(local_width),
            cross_gate_part,
            ada_bias_part,
        ),
        "seq",
    )
    return (
        block_out,
        tokens_grad,
        text_grad,
        summed[7],
        smalls[6],
        smalls[0],
        smalls[1],
        summed[0],
        summed[1],
        summed[2],
        smalls[2],
        smalls[3],
        smalls[5],
        summed[5],
        summed[6],
        smalls[4],
        summed[8],
        summed[3],
        summed[4],
        summed[9],
    )


MESH_AXES = ("z", "y", "x", "c")
PLANE = 4
STRIPS = 4
CORES = 2


def device_pairs(target):
    pairs = []
    for strip in range(STRIPS):
        for place in range(PLANE):
            for core in range(CORES):
                aim = target(strip, place, core)
                pairs.append(
                    (
                        (strip * PLANE + place) * CORES + core,
                        (aim[0] * PLANE + aim[1]) * CORES + aim[2],
                    )
                )
    return pairs


FLIP_CORE = device_pairs(lambda strip, place, core: (strip, place, 1 - core))
FLIP_FIRST = device_pairs(lambda strip, place, core: (strip, place ^ (1 + core), core))
FLIP_SECOND = device_pairs(lambda strip, place, core: (strip, place ^ (2 - core), core))
FLIP_PLACE = {
    mask: device_pairs(lambda strip, place, core, mask=mask: (strip, place ^ mask, core))
    for mask in (1, 2, 3)
}
FLIP_STRIP = {
    mask: device_pairs(lambda strip, place, core, mask=mask: (strip ^ mask, place, core))
    for mask in (1, 2, 3)
}


def move(value, pairs):
    return lax.ppermute(value, MESH_AXES, pairs)


def plane_gather(own):
    own = jnp.concatenate([own, move(own, FLIP_FIRST)])
    own = jnp.concatenate([own, move(own, FLIP_SECOND)])
    return jnp.concatenate([own, move(own, FLIP_CORE)])


def plane_scatter(whole):
    for pairs in (FLIP_CORE, FLIP_SECOND, FLIP_FIRST):
        half = whole.shape[0] // 2
        arrived = move(whole[half:].astype(jnp.bfloat16), pairs)
        whole = whole[:half].astype(jnp.float32) + arrived.astype(jnp.float32)
    return whole


def plane_sum(value):
    for pairs in (FLIP_CORE, FLIP_PLACE[1], FLIP_PLACE[2]):
        value = value + move(value, pairs)
    return value


def strip_gather(value):
    return [value] + [move(value, FLIP_STRIP[mask]) for mask in (1, 2, 3)]


def pair_sum(four):
    return (four[0] + four[1]) + (four[2] + four[3])


def exchange(blocks, index, table):
    def pick(mask):
        return lax.dynamic_index_in_dim(blocks, index ^ mask, 0, keepdims=False)

    return [pick(0)] + [move(pick(mask), table[mask]) for mask in (1, 2, 3)]


def absolute(relative, index):
    odd = (index & 1) == 1
    high = (index & 2) == 2
    step = [jnp.where(odd, relative[i ^ 1], relative[i]) for i in range(4)]
    return [jnp.where(high, step[i ^ 2], step[i]) for i in range(4)]


def contract(left, right, left_dim, right_dim):
    return lax.dot_general(
        left,
        right,
        (((left_dim,), (right_dim,)), ((), ())),
        preferred_element_type=jnp.float32,
    )


def turn(block, cosine, sine):
    a, b, c, d = block[0:16], block[16:32], block[32:48], block[48:64]
    cr, cc = cosine[0:16], cosine[16:32]
    sr, sc = sine[0:16], sine[16:32]
    return jnp.concatenate(
        [a * cr - b * sr, a * sr + b * cr, c * cc - d * sc, c * sc + d * cc], axis=0
    )


def unit_of(raw):
    inverse = lax.rsqrt(jnp.mean(raw * raw, axis=0, keepdims=True) + EPSILON)
    return raw * inverse, inverse


def unit_back(incoming, unit, inverse, gain):
    lifted = incoming * gain
    gain_part = jnp.sum(incoming * unit, axis=1, keepdims=True)
    raw_part = inverse * (lifted - unit * jnp.mean(lifted * unit, axis=0, keepdims=True))
    return raw_part, gain_part


QBLOCK = 256


def attend_kernel(
    q_ref,
    k_ref,
    v_ref,
    tk_ref,
    tv_ref,
    qg_ref,
    kg_ref,
    tg_ref,
    cos_ref,
    sin_ref,
    valid_ref,
    gate_ref,
    comb_ref,
    self_ref,
    cross_ref,
    qlow_ref,
    klow_ref,
    tlow_ref,
    rinv_ref,
):
    cosine, sine, valid = cos_ref[...], sin_ref[...], valid_ref[...]
    query = turn(unit_of(q_ref[...])[0] * qg_ref[...], cosine, sine).astype(jnp.bfloat16)
    key = turn(unit_of(k_ref[...])[0] * kg_ref[...], cosine, sine)
    qlow_ref[...] = query
    klow_ref[...] = key.astype(jnp.bfloat16)
    key_rows = key.T.astype(jnp.bfloat16)
    text_key = unit_of(tk_ref[...])[0] * tg_ref[...]
    tlow_ref[...] = text_key.astype(jnp.bfloat16)
    text_rows = text_key.T.astype(jnp.bfloat16)
    value = v_ref[...].astype(jnp.bfloat16).astype(jnp.float32) * valid
    lanes = value.shape[1]
    value_ones = jnp.concatenate(
        [value, jnp.broadcast_to(valid, (16, lanes))], axis=0
    ).astype(jnp.bfloat16)
    tvalue = tv_ref[...]
    tvalue_ones = jnp.concatenate(
        [tvalue, jnp.ones((16, tvalue.shape[1]), jnp.float32)], axis=0
    ).astype(jnp.bfloat16)
    gate = gate_ref[0:1, 0:1]
    scaled = (query.astype(jnp.float32) * 0.125).astype(jnp.bfloat16)
    for start in range(0, lanes, QBLOCK):
        cols = slice(start, start + QBLOCK)
        weight = jnp.exp(contract(key_rows, scaled[:, cols], 1, 0)).astype(jnp.bfloat16)
        total = contract(value_ones, weight, 1, 0)
        rinv = 1.0 / total[64:65]
        own = total[:64] * rinv
        tweight = jnp.exp(contract(text_rows, scaled[:, cols], 1, 0)).astype(jnp.bfloat16)
        ttotal = contract(tvalue_ones, tweight, 1, 0)
        trinv = 1.0 / ttotal[64:65]
        text = ttotal[:64] * trinv
        self_ref[:, cols] = own
        cross_ref[:, cols] = text
        rinv_ref[0:1, cols] = rinv
        rinv_ref[1:2, cols] = trinv
        comb_ref[:, cols] = (own + gate * text).astype(jnp.bfloat16)


def attend_back_kernel(
    q_ref,
    k_ref,
    v_ref,
    tk_ref,
    tv_ref,
    qg_ref,
    kg_ref,
    tg_ref,
    cos_ref,
    sin_ref,
    valid_ref,
    gate_ref,
    self_ref,
    cross_ref,
    qlow_ref,
    klow_ref,
    tlow_ref,
    rinv_ref,
    dcomb_ref,
    dq_ref,
    dk_ref,
    dv_ref,
    dtk_ref,
    dtv_ref,
    gains_ref,
):
    cosine, sine, valid = cos_ref[...], sin_ref[...], valid_ref[...]
    lanes = valid.shape[1]
    gate = gate_ref[0:1, 0:1]
    dcomb = dcomb_ref[...]
    cross = cross_ref[...]
    dself = dcomb.astype(jnp.bfloat16)
    dcross = (dcomb * gate).astype(jnp.bfloat16)
    delta = jnp.sum(dself.astype(jnp.float32) * self_ref[...], axis=0, keepdims=True)
    tdelta = jnp.sum(dcross.astype(jnp.float32) * cross, axis=0, keepdims=True)
    gate_part = jnp.sum(
        jnp.sum(dcomb * cross, axis=0, keepdims=True), axis=1, keepdims=True
    ) * (1.0 - gate * gate)
    query = qlow_ref[...]
    scaled = (query.astype(jnp.float32) * 0.125).astype(jnp.bfloat16)
    key = klow_ref[...].astype(jnp.float32)
    key_rows = key.T.astype(jnp.bfloat16)
    key_held = (key * valid * 0.125).astype(jnp.bfloat16)
    value_rows = v_ref[...].T.astype(jnp.bfloat16)
    text_key = tlow_ref[...].astype(jnp.float32)
    text_rows = text_key.T.astype(jnp.bfloat16)
    text_held = (text_key * 0.125).astype(jnp.bfloat16)
    tvalue_rows = tv_ref[...].T.astype(jnp.bfloat16)
    dkey = dvalue = dtkey = dtvalue = 0.0
    dquery = []
    for start in range(0, lanes, QBLOCK):
        cols = slice(start, start + QBLOCK)
        probs = jnp.exp(contract(key_rows, scaled[:, cols], 1, 0)) * rinv_ref[0:1, cols]
        dprobs = contract(value_rows, dself[:, cols], 1, 0)
        dscore = (probs * (dprobs - delta[:, cols])).astype(jnp.bfloat16)
        dvalue += contract(dself[:, cols], probs.astype(jnp.bfloat16), 1, 1)
        dkey += contract(scaled[:, cols], dscore, 1, 1)
        turned = contract(key_held, dscore, 1, 0)
        tprobs = jnp.exp(contract(text_rows, scaled[:, cols], 1, 0)) * rinv_ref[1:2, cols]
        dtprobs = contract(tvalue_rows, dcross[:, cols], 1, 0)
        dtscore = (tprobs * (dtprobs - tdelta[:, cols])).astype(jnp.bfloat16)
        dtvalue += contract(dcross[:, cols], tprobs.astype(jnp.bfloat16), 1, 1)
        dtkey += contract(scaled[:, cols], dtscore, 1, 1)
        dquery.append(turned + contract(text_held, dtscore, 1, 0))
    dquery = jnp.concatenate(dquery, axis=1)
    unit, inverse = unit_of(q_ref[...])
    raw, query_gain = unit_back(turn(dquery, cosine, -sine), unit, inverse, qg_ref[...])
    dq_ref[...] = raw.astype(jnp.bfloat16)
    unit, inverse = unit_of(k_ref[...])
    raw, key_gain = unit_back(turn(dkey * valid, cosine, -sine), unit, inverse, kg_ref[...])
    dk_ref[...] = raw.astype(jnp.bfloat16)
    dv_ref[...] = (dvalue * valid).astype(jnp.bfloat16)
    unit, inverse = unit_of(tk_ref[...])
    raw, text_gain = unit_back(dtkey, unit, inverse, tg_ref[...])
    dtk_ref[...] = raw.astype(jnp.bfloat16)
    dtv_ref[...] = dtvalue.astype(jnp.bfloat16)
    gains_ref[:, 0:128] = jnp.broadcast_to(query_gain, (64, 128))
    gains_ref[:, 128:256] = jnp.broadcast_to(key_gain, (64, 128))
    gains_ref[:, 256:384] = jnp.broadcast_to(text_gain, (64, 128))
    gains_ref[:, 384:512] = jnp.broadcast_to(gate_part, (64, 128))


def head_block(width, offset=0):
    return pl.BlockSpec((HDIM, width), lambda h: (h + offset, 0))


def shared_block(rows, width):
    return pl.BlockSpec((rows, width), lambda h: (0, 0))


def attention_call(heads, lanes, texts, backward):
    f32, b16 = jnp.float32, jnp.bfloat16
    specs = [
        head_block(lanes),
        head_block(lanes, heads),
        head_block(lanes, 2 * heads),
        head_block(texts),
        head_block(texts, heads),
        head_block(1),
        head_block(1),
        head_block(1),
        shared_block(32, lanes),
        shared_block(32, lanes),
        shared_block(1, lanes),
        pl.BlockSpec((8, 128), lambda h: (h, 0)),
    ]
    wide = heads * HDIM
    rinv_spec = pl.BlockSpec((8, lanes), lambda h: (h, 0))
    saved = [head_block(lanes)] * 2 + [head_block(lanes)] * 2 + [head_block(texts), rinv_spec]
    shape = jax.ShapeDtypeStruct
    pairs = heads * lanes * (lanes + texts)
    if not backward:
        out_specs = [head_block(lanes)] + saved
        out_shape = [
            shape((wide, lanes), b16),
            shape((wide, lanes), f32),
            shape((wide, lanes), f32),
            shape((wide, lanes), b16),
            shape((wide, lanes), b16),
            shape((wide, texts), b16),
            shape((heads * 8, lanes), f32),
        ]
        body, passes = attend_kernel, 2
    else:
        specs = specs + saved + [head_block(lanes)]
        out_specs = [head_block(lanes)] * 3 + [head_block(texts)] * 2 + [head_block(512)]
        out_shape = (
            [shape((wide, lanes), b16)] * 3
            + [shape((wide, texts), b16)] * 2
            + [shape((wide, 512), f32)]
        )
        body, passes = attend_back_kernel, 5
    return pl.pallas_call(
        body,
        grid=(heads,),
        in_specs=specs,
        out_specs=out_specs,
        out_shape=out_shape,
        compiler_params=pltpu.CompilerParams(vmem_limit_bytes=48 * 1024 * 1024),
        cost_estimate=pl.CostEstimate(
            flops=8 * pairs * HDIM * passes, bytes_accessed=8 * wide * lanes, transcendentals=pairs
        ),
    )


def split_three(value):
    high = lax.reduce_precision(value, 8, 7)
    middle = lax.reduce_precision(value - high, 8, 7)
    return jnp.concatenate([high, middle, value - high - middle]).astype(jnp.bfloat16)


def strip_shards(
    tokens,
    cotangent,
    step_embed,
    item_band,
    item_length,
    item_width,
    text_states,
    ada_weight,
    ada_bias,
    attn_gain,
    ffn_gain,
    query_weight,
    key_weight,
    value_weight,
    query_gain,
    key_gain,
    cross_gate,
    text_key_weight,
    text_value_weight,
    text_key_gain,
    out_weight,
    gate_weight,
    up_weight,
    down_weight,
):
    f32, b16 = jnp.float32, jnp.bfloat16
    strip = lax.axis_index("z")
    place = lax.axis_index("y") * 2 + lax.axis_index("x")
    core = lax.axis_index("c")
    first_core = core == 0
    width = tokens.shape[1]
    half = SLOT // CORES
    own_rows = STRIPS * half
    lanes = own_rows * PLANE * CORES
    wide = query_weight.shape[1] // PLANE
    heads = wide // HDIM
    hidden_wide = gate_weight.shape[1] // PLANE
    text_own = text_states.shape[0]
    texts = text_own * PLANE

    def cols(weight, size):
        return lax.dynamic_slice_in_dim(weight, place * size, size, 1)

    def rows(weight, size):
        return lax.dynamic_slice_in_dim(weight, place * size, size, 0)

    def to_items(array_in):
        parts = lax.dynamic_slice_in_dim(
            array_in.reshape(ITEMS, SLOT, width), core * half, half, 1
        )
        return jnp.concatenate(exchange(parts, strip, FLIP_STRIP))

    def from_items(array_in):
        parts = array_in.reshape(STRIPS, half, width)
        arrived = [parts[0]] + [move(parts[m], FLIP_STRIP[m]) for m in (1, 2, 3)]
        mine = jnp.stack(absolute(arrived, strip))
        other = move(mine, FLIP_CORE)
        low = jnp.where(first_core, mine, other)
        high = jnp.where(first_core, other, mine)
        return jnp.concatenate([low, high], axis=1).reshape(ITEMS * SLOT, width)

    own_tokens = to_items(tokens)
    all_tokens = plane_gather(own_tokens)

    silu_embed = jax.nn.silu(step_embed.astype(f32))
    products = jnp.dot(split_three(silu_embed), ada_weight, preferred_element_type=f32)
    local_mod = products[0:4] + products[4:8] + products[8:12] + ada_bias
    other_mod = move(local_mod, FLIP_CORE)
    low_mod = jnp.where(first_core, local_mod, other_mod)
    high_mod = jnp.where(first_core, other_mod, local_mod)

    def banded(table, mask):
        return lax.dynamic_index_in_dim(table, item_band[strip ^ mask], 0, keepdims=False)

    scale_attn_items = [banded(low_mod[:, :width], mask) for mask in range(4)]
    scale_ffn_items = [banded(high_mod[:, :width], mask) for mask in range(4)]
    lift_attn = attn_gain * (1.0 + scale_attn_items[0])
    lift_ffn = ffn_gain * (1.0 + scale_ffn_items[0])
    gate_attn = jnp.tanh(banded(low_mod[:, width:], 0))
    gate_ffn = jnp.tanh(banded(high_mod[:, width:], 0))

    text_raw = jnp.stack(
        [
            contract(text_key_weight, text_states, 0, 1),
            contract(text_value_weight, text_states, 0, 1).astype(b16).astype(f32),
        ]
    )
    text_raw = jnp.moveaxis(text_raw.reshape(2, PLANE, wide, text_own), 1, 0)
    text_raw = jnp.concatenate(exchange(text_raw, place, FLIP_PLACE), axis=2)
    text_raw = text_raw.reshape(2 * wide, texts)

    lane = jnp.arange(lanes, dtype=jnp.int32)
    block, inner = lane // own_rows, lane % own_rows
    flipped = block // PLANE
    from_core = core ^ flipped
    mask_first, mask_second = 1 + from_core, 2 - from_core
    from_place = place ^ ((block & 1) * mask_first) ^ (((block // 2) & 1) * mask_second)
    from_strip = strip ^ (inner // half)
    position = (from_strip * PLANE + from_place) * SLOT + from_core * half + inner % half
    width_here = item_width[strip]
    grid_row = (position // width_here).astype(f32)
    grid_col = (position % width_here).astype(f32)
    quarter = HDIM // 4
    frequency = ROPE_BASE ** (-jnp.arange(quarter, dtype=f32) / quarter)
    angles = jnp.concatenate(
        [frequency[:, None] * grid_row[None, :], frequency[:, None] * grid_col[None, :]]
    )
    cosine, sine = jnp.cos(angles), jnp.sin(angles)
    valid = (position < item_length[strip]).astype(f32)[None, :]

    def column(vector):
        return lax.dynamic_slice_in_dim(vector, place * wide, wide, 0)[:, None]

    tanh_gate = jnp.tanh(lax.dynamic_slice_in_dim(cross_gate, place * heads, heads, 0))
    gate_tiles = jnp.broadcast_to(tanh_gate[:, None, None], (heads, 8, 128)).reshape(-1, 128)

    residual_all = all_tokens.astype(f32)
    attn_in = (residual_all * rms_inverse(residual_all) * lift_attn).astype(b16)
    qkv_weight = jnp.concatenate(
        [cols(query_weight, wide), cols(key_weight, wide), cols(value_weight, wide)], axis=1
    )
    qkv = contract(qkv_weight, attn_in, 0, 1)
    common = (
        qkv,
        qkv,
        qkv,
        text_raw,
        text_raw,
        column(query_gain),
        column(key_gain),
        column(text_key_gain),
        cosine,
        sine,
        valid,
        gate_tiles,
    )
    combined, *saved = attention_call(heads, lanes, texts, False)(*common)
    out_rows = rows(out_weight, wide)
    attn_branch = plane_scatter(contract(combined, out_rows, 0, 0).astype(b16))

    residual = own_tokens.reshape(own_rows, width).astype(f32)
    middle = residual + gate_attn * attn_branch
    inverse_two = rms_inverse(middle)
    normed_two = middle * inverse_two
    ffn_in = plane_gather((normed_two * lift_ffn).astype(b16))
    incoming = to_items(cotangent)
    all_incoming = plane_gather(incoming)
    incoming = incoming.reshape(own_rows, width).astype(f32)
    d_ffn = (gate_ffn * all_incoming.astype(f32)).astype(b16)
    gu_weight = jnp.concatenate(
        [cols(gate_weight, hidden_wide), cols(up_weight, hidden_wide)], axis=1
    )
    down_rows = rows(down_weight, hidden_wide)
    d_hidden = contract(d_ffn, down_rows, 1, 1)
    gate_up = jnp.dot(ffn_in, gu_weight, preferred_element_type=f32)
    gate_pre, up_pre = gate_up[:, :hidden_wide], gate_up[:, hidden_wide:]
    gate_sig = jax.nn.sigmoid(gate_pre)
    hidden = (gate_pre * gate_sig * up_pre).astype(b16)
    d_gate = (d_hidden * up_pre * gate_sig * (1.0 + gate_pre * (1.0 - gate_sig))).astype(b16)
    d_up = (d_hidden * gate_pre * gate_sig).astype(b16)
    d_gate_up = jnp.concatenate([d_gate, d_up], axis=1)
    d_ffn_in = plane_scatter(contract(d_gate_up, gu_weight, 1, 1).astype(b16))
    d_normed = d_ffn_in * normed_two
    u_ffn = jnp.sum(d_normed, axis=0)
    d_middle = incoming + inverse_two * (
        d_ffn_in * lift_ffn
        - normed_two * jnp.mean(d_normed * lift_ffn, axis=-1, keepdims=True)
    )
    w_attn = jnp.sum(d_middle * attn_branch, axis=0) * (1.0 - gate_attn * gate_attn)
    d_attn = plane_gather((gate_attn * d_middle).astype(b16))

    ffn_branch = plane_scatter(
        jnp.dot(hidden, down_rows, preferred_element_type=f32).astype(b16)
    )
    w_ffn = jnp.sum(incoming * ffn_branch, axis=0) * (1.0 - gate_ffn * gate_ffn)
    block_out = from_items((middle + gate_ffn * ffn_branch).astype(b16))

    d_comb = contract(out_rows, d_attn, 1, 1)
    dq, dk, dv, d_text_key, d_text_value, gains = attention_call(heads, lanes, texts, True)(
        *common, *saved, d_comb
    )
    d_qkv = jnp.concatenate([dq, dk, dv])
    d_attn_in = plane_scatter(contract(d_qkv, qkv_weight, 0, 1).astype(b16))
    inverse_one = rms_inverse(residual)
    normed_one = residual * inverse_one
    d_normed = d_attn_in * normed_one
    u_attn = jnp.sum(d_normed, axis=0)
    tokens_grad = d_middle + inverse_one * (
        d_attn_in * lift_attn
        - normed_one * jnp.mean(d_normed * lift_attn, axis=-1, keepdims=True)
    )
    tokens_grad = from_items(tokens_grad.astype(b16))

    def spread(grad):
        own = lax.psum_scatter(grad, "z", scatter_dimension=0, tiled=True)
        blocks = own.reshape(PLANE, own.shape[0] // PLANE, own.shape[1])
        return absolute(exchange(blocks, place, FLIP_PLACE), place)

    def sheet(blocks, start, size):
        return jnp.concatenate([b[:, start : start + size] for b in blocks], axis=1).astype(f32)

    ffn_grads = jnp.concatenate(
        [
            contract(ffn_in, d_gate_up, 0, 0).astype(b16),
            contract(d_ffn, hidden, 0, 0).astype(b16),
            contract(d_attn, combined, 0, 1).astype(b16),
        ],
        axis=1,
    )
    ffn_blocks = spread(ffn_grads)
    attn_blocks = spread(contract(attn_in, d_qkv, 0, 1).astype(b16))
    gate_grad = sheet(ffn_blocks, 0, hidden_wide)
    up_grad = sheet(ffn_blocks, hidden_wide, hidden_wide)
    down_grad = sheet(ffn_blocks, 2 * hidden_wide, hidden_wide).T
    out_grad = sheet(ffn_blocks, 3 * hidden_wide, wide).T
    query_grad = sheet(attn_blocks, 0, wide)
    key_grad = sheet(attn_blocks, wide, wide)
    value_grad = sheet(attn_blocks, 2 * wide, wide)

    d_text = jnp.stack([d_text_key, d_text_value])
    back = [d_text[:, :, :text_own]] + [
        move(d_text[:, :, m * text_own : (m + 1) * text_own], FLIP_PLACE[m]) for m in (1, 2, 3)
    ]
    back = jnp.concatenate(absolute(back, place), axis=1)
    text_part = contract(back[0], text_key_weight, 0, 1) + contract(
        back[1], text_value_weight, 0, 1
    )
    text_half = text_part.shape[1] // CORES
    text_send = lax.dynamic_slice_in_dim(text_part, (1 - core) * text_half, text_half, 1)
    text_keep = lax.dynamic_slice_in_dim(text_part, core * text_half, text_half, 1)
    text_grad = text_keep + move(text_send.astype(b16), FLIP_CORE).astype(f32)
    states_wide = text_states.shape[1] // STRIPS
    states = jnp.moveaxis(text_states.reshape(text_own, STRIPS, states_wide), 1, 0)
    states = jnp.stack(exchange(states, strip, FLIP_STRIP))
    states = jnp.stack(
        [states] + [move(states, FLIP_PLACE[m]) for m in (1, 2, 3)], axis=1
    ).reshape(STRIPS * texts, states_wide)
    d_text_all = jnp.concatenate(strip_gather(d_text.reshape(2 * wide, texts)), axis=1)
    text_sum = contract(states, d_text_all, 0, 1).astype(b16)
    text_blocks = text_sum.reshape(PLANE, states_wide // PLANE, 2 * wide)
    text_blocks = absolute(exchange(text_blocks, place, FLIP_PLACE), place)
    text_key_grad = sheet(text_blocks, 0, wide)
    text_value_grad = sheet(text_blocks, wide, wide)

    vectors = strip_gather(plane_sum(jnp.stack([u_ffn, w_ffn, w_attn])))
    last = strip_gather(plane_sum(u_attn))
    items = []
    for mask in range(4):
        low_part = jnp.concatenate([attn_gain * last[mask], vectors[mask][2]])
        high_part = jnp.concatenate([ffn_gain * vectors[mask][0], vectors[mask][1]])
        items.append(jnp.where(first_core, low_part, high_part))
    ada_bias_grad = pair_sum(items)
    attn_gain_grad = pair_sum([last[m] * (1.0 + scale_attn_items[m]) for m in range(4)])
    ffn_gain_grad = pair_sum([vectors[m][0] * (1.0 + scale_ffn_items[m]) for m in range(4)])
    ada_rows = silu_embed.shape[1] // (STRIPS * PLANE)
    silu_own = lax.dynamic_slice_in_dim(
        silu_embed, (strip * PLANE + place) * ada_rows, ada_rows, 1
    )
    ada_grad = pair_sum(
        [
            lax.dynamic_index_in_dim(silu_own, item_band[strip ^ m], 0, keepdims=False)[:, None]
            * items[m][None, :]
            for m in range(4)
        ]
    )
    head_parts = jnp.stack(
        [gains[:, 0], gains[:, 128], gains[:, 256], gains[:, 384]]
    )
    head_parts = pair_sum(strip_gather(head_parts))
    head_parts = absolute(
        [head_parts] + [move(head_parts, FLIP_PLACE[m]) for m in (1, 2, 3)], place
    )
    head_parts = jnp.concatenate(head_parts, axis=1)
    return (
        block_out,
        tokens_grad,
        text_grad,
        ada_grad,
        ada_bias_grad,
        attn_gain_grad,
        ffn_gain_grad,
        query_grad,
        key_grad,
        value_grad,
        head_parts[0],
        head_parts[1],
        head_parts[3].reshape(-1, HDIM)[:, 0],
        text_key_grad,
        text_value_grad,
        head_parts[2],
        out_grad,
        gate_grad,
        up_grad,
        down_grad,
    )


def placements(seq, tp):
    ins = (
        P(seq, None),
        P(seq, None),
        P(),
        P(),
        P(),
        P(),
        P(seq, None),
        P(None, tp),
        P(tp),
        P(),
        P(),
        P(None, tp),
        P(None, tp),
        P(None, tp),
        P(tp),
        P(tp),
        P(tp),
        P(None, tp),
        P(None, tp),
        P(tp),
        P(tp, None),
        P(None, tp),
        P(None, tp),
        P(tp, None),
    )
    outs = (
        P(seq, None),
        P(seq, None),
        P(seq, tp),
        P(seq, tp),
        P(tp),
        P(),
        P(),
        P(seq, tp),
        P(seq, tp),
        P(seq, tp),
        P(tp),
        P(tp),
        P(tp),
        P(seq, tp),
        P(seq, tp),
        P(tp),
        P(tp, seq),
        P(seq, tp),
        P(seq, tp),
        P(tp, seq),
    )
    return ins, outs


def solution(mesh):
    if mesh.shape["seq"] == STRIPS * PLANE and mesh.shape["tp"] == CORES:
        body, seq, tp = strip_shards, ("z", "y", "x"), "c"
        mesh = Mesh(mesh.devices.reshape(STRIPS, 2, 2, CORES), MESH_AXES)
    else:
        body, seq, tp = shards, "seq", "tp"
    ins, outs = placements(seq, tp)
    return jax.shard_map(body, mesh=mesh, in_specs=ins, out_specs=outs, check_vma=False)
```

```python
import jax
import jax.numpy as jnp
from jax import lax
from jax.experimental import pallas as pl
from jax.experimental.pallas import tpu as pltpu
from jax.sharding import Mesh
from jax.sharding import PartitionSpec as P

HDIM = 64
NTXT = 256
BANDS = 4
ITEMS = 4
SLOT = 64


EPSILON = 1e-06
ROPE_BASE = 10000.0
HIGHEST = lax.Precision.HIGHEST
NEG_FILL = -1e30


def rms_inverse(values):
    return lax.rsqrt(jnp.mean(values * values, axis=-1, keepdims=True) + EPSILON)


def rope_angles(row_pos, col_pos, head_dim):
    quarter = head_dim // 4
    frequency = ROPE_BASE ** (-jnp.arange(quarter, dtype=jnp.float32) / quarter)
    angles = jnp.stack([row_pos[..., None] * frequency, col_pos[..., None] * frequency], axis=-2)
    return (jnp.cos(angles), jnp.sin(angles))


def rotate(vectors, cosines, sines):
    shape_all = vectors.shape
    paired = vectors.reshape(shape_all[:-1] + (2, 2, shape_all[-1] // 4))
    former = paired[..., 0, :]
    latter = paired[..., 1, :]
    turned = jnp.stack(
        [former * cosines - latter * sines, former * sines + latter * cosines], axis=-2
    )
    return turned.reshape(shape_all)


def head_norm(raw_vals, gain_vec):
    inverse = rms_inverse(raw_vals)
    unit_vec = raw_vals * inverse
    return (unit_vec * gain_vec, unit_vec, inverse)


def head_norm_back(incoming, unit_vec, inverse, gain_vec):
    grad_unit = incoming * gain_vec
    gain_part = jnp.sum(incoming * unit_vec, axis=tuple(range(incoming.ndim - 2)))
    grad_raw = inverse * (
        grad_unit - unit_vec * jnp.mean(grad_unit * unit_vec, axis=-1, keepdims=True)
    )
    return (grad_raw, gain_part)


def token_norm_back(incoming, normed, inverse, gain_vec, scale_mod):
    lifted = 1.0 + scale_mod
    gain_part = jnp.sum(incoming * normed * lifted, axis=(0, 1))
    scale_part = jnp.sum(incoming * normed * gain_vec, axis=1)
    grad_normed = incoming * gain_vec * lifted
    grad_in = inverse * (
        grad_normed - normed * jnp.mean(grad_normed * normed, axis=-1, keepdims=True)
    )
    return (grad_in, gain_part, scale_part)


def attend(query_h, key_h, value_h, key_valid):
    scaling = query_h.shape[-1] ** (-0.5)
    scores = (
        jnp.einsum("isd,ikd->isk", query_h, key_h, preferred_element_type=jnp.float32) * scaling
    )
    if key_valid is not None:
        scores = jnp.where(key_valid[:, None, :], scores, NEG_FILL)
    row_max = jnp.max(scores, axis=-1, keepdims=True)
    exp_scores = jnp.exp(scores - row_max)
    row_total = jnp.sum(exp_scores, axis=-1, keepdims=True)
    probability = (exp_scores / row_total).astype(jnp.bfloat16)
    output = jnp.einsum("isk,ikd->isd", probability, value_h, preferred_element_type=jnp.float32)
    return (output, (row_max + jnp.log(row_total))[..., 0])


def attend_back(query_h, key_h, value_h, key_valid, lse_h, dout_h):
    scaling = query_h.shape[-1] ** (-0.5)
    scores = (
        jnp.einsum("isd,ikd->isk", query_h, key_h, preferred_element_type=jnp.float32) * scaling
    )
    if key_valid is not None:
        scores = jnp.where(key_valid[:, None, :], scores, NEG_FILL)
    probability = jnp.exp(scores - lse_h[..., None])
    d_prob = jnp.einsum("isd,ikd->isk", dout_h, value_h, preferred_element_type=jnp.float32)
    delta_row = jnp.sum(d_prob * probability, axis=-1)
    d_score = (probability * (d_prob - delta_row[..., None])).astype(jnp.bfloat16)
    d_query = (
        jnp.einsum("isk,ikd->isd", d_score, key_h, preferred_element_type=jnp.float32) * scaling
    )
    d_key = (
        jnp.einsum("isk,isd->ikd", d_score, query_h, preferred_element_type=jnp.float32) * scaling
    )
    d_value = jnp.einsum(
        "isk,isd->ikd", probability.astype(jnp.bfloat16), dout_h, preferred_element_type=jnp.float32
    )
    return (d_query, delta_row, d_key, d_value)


def head_total(partial_value):
    return lax.psum(partial_value.astype(jnp.bfloat16), "tp").astype(jnp.float32)


def feature_total(partial_value):
    return lax.psum(partial_value.astype(jnp.bfloat16), "tp").astype(jnp.float32)


def shards(
    tokens,
    cotangent,
    step_embed,
    item_band,
    item_length,
    item_width,
    text_states,
    ada_weight,
    ada_bias,
    attn_gain,
    ffn_gain,
    query_weight,
    key_weight,
    value_weight,
    query_gain,
    key_gain,
    cross_gate,
    text_key_weight,
    text_value_weight,
    text_key_gain,
    out_weight,
    gate_weight,
    up_weight,
    down_weight,
):
    seq_count = lax.axis_size("seq")
    seq_index = lax.axis_index("seq")
    tp_index = lax.axis_index("tp")
    tok_dev, model_width = tokens.shape
    local_width = query_weight.shape[1]
    local_heads = local_width // HDIM
    capacity = SLOT * seq_count
    text_rows = text_states.shape[0]
    mod_cols = ada_weight.shape[1]
    head_shape = (ITEMS, SLOT, local_heads, HDIM)
    silu_embed = jax.nn.silu(step_embed.astype(jnp.float32))
    local_mod = jnp.dot(silu_embed, ada_weight.astype(jnp.float32), precision=HIGHEST) + ada_bias
    band_mod = lax.all_gather(local_mod, "tp", axis=1, tiled=True)
    band_onehot = (item_band[:, None] == jnp.arange(BANDS, dtype=jnp.int32)[None, :]).astype(
        jnp.float32
    )
    item_mod = jnp.dot(band_onehot, band_mod, precision=HIGHEST)
    scale_attn = item_mod[:, None, 0:model_width]
    gate_attn = jnp.tanh(item_mod[:, None, model_width : 2 * model_width])
    scale_ffn = item_mod[:, None, 2 * model_width : 3 * model_width]
    gate_ffn = jnp.tanh(item_mod[:, None, 3 * model_width :])
    slot_pos = seq_index * SLOT + jnp.arange(SLOT, dtype=jnp.int32)
    row_pos = (slot_pos[None, :] // item_width[:, None]).astype(jnp.float32)
    col_pos = (slot_pos[None, :] % item_width[:, None]).astype(jnp.float32)
    cosines, sines = rope_angles(row_pos, col_pos, HDIM)
    cosines = cosines[:, :, None]
    sines = sines[:, :, None]
    key_valid = jnp.arange(capacity, dtype=jnp.int32)[None, :] < item_length[:, None]

    def by_heads(array_in, row_count):
        return jnp.moveaxis(array_in.reshape(ITEMS, row_count, local_heads, HDIM), 2, 0)

    text_key_raw = jnp.dot(
        text_states, text_key_weight, preferred_element_type=jnp.float32
    ).reshape(text_rows, local_heads, HDIM)
    text_gain_vec = text_key_gain.reshape(local_heads, HDIM)
    text_key_normed, text_unit, text_inverse = head_norm(text_key_raw, text_gain_vec)
    text_key_low = text_key_normed.reshape(text_rows, local_width).astype(jnp.bfloat16)
    text_value_low = jnp.dot(
        text_states, text_value_weight, preferred_element_type=jnp.float32
    ).astype(jnp.bfloat16)
    text_key_all, text_value_all = (
        lax.all_gather(text_key_low, "seq", axis=0, tiled=True),
        lax.all_gather(text_value_low, "seq", axis=0, tiled=True),
    )
    residual = tokens.astype(jnp.float32).reshape(ITEMS, SLOT, model_width)
    inverse_one = rms_inverse(residual)
    normed_one = residual * inverse_one
    attn_in = (
        (normed_one * attn_gain * (1.0 + scale_attn))
        .astype(jnp.bfloat16)
        .reshape(tok_dev, model_width)
    )
    query_raw = jnp.dot(attn_in, query_weight, preferred_element_type=jnp.float32).reshape(
        head_shape
    )
    key_raw = jnp.dot(attn_in, key_weight, preferred_element_type=jnp.float32).reshape(head_shape)
    value_low = (
        jnp.dot(attn_in, value_weight, preferred_element_type=jnp.float32)
        .astype(jnp.bfloat16)
        .reshape(ITEMS, SLOT, local_width)
    )
    query_gain_vec = query_gain.reshape(local_heads, HDIM)
    key_gain_vec = key_gain.reshape(local_heads, HDIM)
    query_normed, query_unit, query_inverse = head_norm(query_raw, query_gain_vec)
    key_normed, key_unit, key_inverse = head_norm(key_raw, key_gain_vec)
    query_low = rotate(query_normed, cosines, sines).astype(jnp.bfloat16)
    key_low = (
        rotate(key_normed, cosines, sines).astype(jnp.bfloat16).reshape(ITEMS, SLOT, local_width)
    )
    key_all, value_all = (
        lax.all_gather(key_low, "seq", axis=1, tiled=True),
        lax.all_gather(value_low, "seq", axis=1, tiled=True),
    )
    query_heads = jnp.moveaxis(query_low, 2, 0)
    key_heads = by_heads(key_all, capacity)
    value_heads = by_heads(value_all, capacity)
    text_key_heads = by_heads(text_key_all, NTXT)
    text_value_heads = by_heads(text_value_all, NTXT)

    def forward_head(operands):
        query_h, key_h, value_h, tkey_h, tvalue_h = operands
        self_part, self_stat = attend(query_h, key_h, value_h, key_valid)
        cross_part, cross_stat = attend(query_h, tkey_h, tvalue_h, None)
        return (self_part, self_stat, cross_part, cross_stat)

    self_out, self_lse, cross_out, cross_lse = lax.map(
        forward_head, (query_heads, key_heads, value_heads, text_key_heads, text_value_heads)
    )
    cross_tanh = jnp.tanh(cross_gate)
    combined = self_out + cross_tanh[:, None, None, None] * cross_out
    combined_low = jnp.moveaxis(combined, 0, 2).reshape(tok_dev, local_width).astype(jnp.bfloat16)
    attn_branch = head_total(
        jnp.dot(combined_low, out_weight, preferred_element_type=jnp.float32)
    ).reshape(ITEMS, SLOT, model_width)
    middle = residual + gate_attn * attn_branch
    inverse_two = rms_inverse(middle)
    normed_two = middle * inverse_two
    ffn_in = (
        (normed_two * ffn_gain * (1.0 + scale_ffn))
        .astype(jnp.bfloat16)
        .reshape(tok_dev, model_width)
    )
    gate_pre = jnp.dot(ffn_in, gate_weight, preferred_element_type=jnp.float32)
    up_pre = jnp.dot(ffn_in, up_weight, preferred_element_type=jnp.float32)
    gate_sig = jax.nn.sigmoid(gate_pre)
    hidden = (gate_pre * gate_sig * up_pre).astype(jnp.bfloat16)
    ffn_branch = head_total(
        jnp.dot(hidden, down_weight, preferred_element_type=jnp.float32)
    ).reshape(ITEMS, SLOT, model_width)
    layer_sum = middle + gate_ffn * ffn_branch
    block_out = layer_sum.reshape(tok_dev, model_width).astype(jnp.bfloat16)
    incoming = cotangent.astype(jnp.float32).reshape(ITEMS, SLOT, model_width)
    gate_ffn_tok = incoming * ffn_branch
    d_ffn = (gate_ffn * incoming).reshape(tok_dev, model_width).astype(jnp.bfloat16)
    down_grad = jnp.dot(hidden.T, d_ffn, preferred_element_type=jnp.float32)
    d_hidden = jnp.dot(d_ffn, down_weight.T, preferred_element_type=jnp.float32)
    d_gate_pre = (d_hidden * up_pre * gate_sig * (1.0 + gate_pre * (1.0 - gate_sig))).astype(
        jnp.bfloat16
    )
    d_up_pre = (d_hidden * gate_pre * gate_sig).astype(jnp.bfloat16)
    gate_grad = jnp.dot(ffn_in.T, d_gate_pre, preferred_element_type=jnp.float32)
    up_grad = jnp.dot(ffn_in.T, d_up_pre, preferred_element_type=jnp.float32)
    d_ffn_in = feature_total(
        jnp.dot(d_gate_pre, gate_weight.T, preferred_element_type=jnp.float32)
        + jnp.dot(d_up_pre, up_weight.T, preferred_element_type=jnp.float32)
    )
    d_middle_norm, ffn_gain_part, scale_ffn_part = token_norm_back(
        d_ffn_in.reshape(ITEMS, SLOT, model_width), normed_two, inverse_two, ffn_gain, scale_ffn
    )
    d_middle = incoming + d_middle_norm
    gate_attn_tok = d_middle * attn_branch
    d_attn = (gate_attn * d_middle).reshape(tok_dev, model_width).astype(jnp.bfloat16)
    out_grad = jnp.dot(combined_low.T, d_attn, preferred_element_type=jnp.float32)
    d_combined = jnp.moveaxis(
        jnp.dot(d_attn, out_weight.T, preferred_element_type=jnp.float32).reshape(head_shape), 2, 0
    )
    cross_gate_part = jnp.sum(d_combined * cross_out, axis=(1, 2, 3)) * (
        1.0 - cross_tanh * cross_tanh
    )
    d_self = d_combined.astype(jnp.bfloat16)
    d_cross = (d_combined * cross_tanh[:, None, None, None]).astype(jnp.bfloat16)

    def cross_head(operands):
        query_h, tkey_h, tvalue_h, lse_h, dout_h = operands
        d_query, unused_delta, d_key, d_value = attend_back(
            query_h, tkey_h, tvalue_h, None, lse_h, dout_h
        )
        return (d_query, d_key, d_value)

    d_query_cross, d_text_key_heads, d_text_value_heads = lax.map(
        cross_head, (query_heads, text_key_heads, text_value_heads, cross_lse, d_cross)
    )

    def full_head(operands):
        query_h, key_h, value_h, lse_h, dout_h = operands
        d_query, unused_delta, d_key, d_value = attend_back(
            query_h, key_h, value_h, key_valid, lse_h, dout_h
        )
        return (d_query, d_key, d_value)

    d_query_self, d_key_heads, d_value_heads = lax.map(
        full_head, (query_heads, key_heads, value_heads, self_lse, d_self)
    )
    d_key_own, d_value_own = (
        lax.psum_scatter(
            jnp.moveaxis(d_key_heads, 0, 2)
            .reshape(ITEMS, capacity, local_width)
            .astype(jnp.bfloat16),
            "seq",
            scatter_dimension=1,
            tiled=True,
        ).astype(jnp.float32),
        lax.psum_scatter(
            jnp.moveaxis(d_value_heads, 0, 2)
            .reshape(ITEMS, capacity, local_width)
            .astype(jnp.bfloat16),
            "seq",
            scatter_dimension=1,
            tiled=True,
        ).astype(jnp.float32),
    )
    d_key_rot = d_key_own.reshape(head_shape)
    d_query_rot = jnp.moveaxis(d_query_self + d_query_cross, 0, 2)
    d_query_raw, query_gain_part = head_norm_back(
        rotate(d_query_rot, cosines, -sines), query_unit, query_inverse, query_gain_vec
    )
    d_key_raw, key_gain_part = head_norm_back(
        rotate(d_key_rot, cosines, -sines), key_unit, key_inverse, key_gain_vec
    )
    d_query_low = d_query_raw.reshape(tok_dev, local_width).astype(jnp.bfloat16)
    d_key_low = d_key_raw.reshape(tok_dev, local_width).astype(jnp.bfloat16)
    d_value_low = d_value_own.reshape(tok_dev, local_width).astype(jnp.bfloat16)
    query_grad = jnp.dot(attn_in.T, d_query_low, preferred_element_type=jnp.float32)
    key_grad = jnp.dot(attn_in.T, d_key_low, preferred_element_type=jnp.float32)
    value_grad = jnp.dot(attn_in.T, d_value_low, preferred_element_type=jnp.float32)
    d_attn_in = feature_total(
        jnp.dot(d_query_low, query_weight.T, preferred_element_type=jnp.float32)
        + jnp.dot(d_key_low, key_weight.T, preferred_element_type=jnp.float32)
        + jnp.dot(d_value_low, value_weight.T, preferred_element_type=jnp.float32)
    )
    d_input_norm, attn_gain_part, scale_attn_part = token_norm_back(
        d_attn_in.reshape(ITEMS, SLOT, model_width), normed_one, inverse_one, attn_gain, scale_attn
    )
    tokens_grad = (d_middle + d_input_norm).reshape(tok_dev, model_width).astype(jnp.bfloat16)
    d_text_key_own, d_text_value_own = (
        lax.psum_scatter(
            jnp.moveaxis(d_text_key_heads, 0, 2)
            .reshape(ITEMS * NTXT, local_width)
            .astype(jnp.bfloat16),
            "seq",
            scatter_dimension=0,
            tiled=True,
        ).astype(jnp.float32),
        lax.psum_scatter(
            jnp.moveaxis(d_text_value_heads, 0, 2)
            .reshape(ITEMS * NTXT, local_width)
            .astype(jnp.bfloat16),
            "seq",
            scatter_dimension=0,
            tiled=True,
        ).astype(jnp.float32),
    )
    d_text_key_raw, text_gain_part = head_norm_back(
        d_text_key_own.reshape(text_rows, local_heads, HDIM), text_unit, text_inverse, text_gain_vec
    )
    d_text_key_low = d_text_key_raw.reshape(text_rows, local_width).astype(jnp.bfloat16)
    d_text_value_low = d_text_value_own.astype(jnp.bfloat16)
    text_key_grad = jnp.dot(text_states.T, d_text_key_low, preferred_element_type=jnp.float32)
    text_value_grad = jnp.dot(text_states.T, d_text_value_low, preferred_element_type=jnp.float32)
    text_grad = lax.psum_scatter(
        (
            jnp.dot(d_text_key_low, text_key_weight.T, preferred_element_type=jnp.float32)
            + jnp.dot(d_text_value_low, text_value_weight.T, preferred_element_type=jnp.float32)
        ).astype(jnp.bfloat16),
        "tp",
        scatter_dimension=1,
        tiled=True,
    ).astype(jnp.float32)
    gate_attn_item = jnp.sum(gate_attn_tok, axis=1) * (1.0 - gate_attn[:, 0] * gate_attn[:, 0])
    gate_ffn_item = jnp.sum(gate_ffn_tok, axis=1) * (1.0 - gate_ffn[:, 0] * gate_ffn[:, 0])
    item_grad = jnp.concatenate(
        [scale_attn_part, gate_attn_item, scale_ffn_part, gate_ffn_item], axis=1
    )
    band_grad = jnp.dot(band_onehot.T, item_grad, precision=HIGHEST)
    local_band_grad = lax.dynamic_slice_in_dim(band_grad, tp_index * mod_cols, mod_cols, 1)
    ada_grad = jnp.dot(silu_embed.T, local_band_grad, precision=HIGHEST)
    ada_bias_part = jnp.sum(local_band_grad, axis=0)
    summed = (
        lax.psum_scatter(
            query_grad.astype(jnp.bfloat16), "seq", scatter_dimension=0, tiled=True
        ).astype(jnp.float32),
        lax.psum_scatter(
            key_grad.astype(jnp.bfloat16), "seq", scatter_dimension=0, tiled=True
        ).astype(jnp.float32),
        lax.psum_scatter(
            value_grad.astype(jnp.bfloat16), "seq", scatter_dimension=0, tiled=True
        ).astype(jnp.float32),
        lax.psum_scatter(
            gate_grad.astype(jnp.bfloat16), "seq", scatter_dimension=0, tiled=True
        ).astype(jnp.float32),
        lax.psum_scatter(
            up_grad.astype(jnp.bfloat16), "seq", scatter_dimension=0, tiled=True
        ).astype(jnp.float32),
        lax.psum_scatter(
            text_key_grad.astype(jnp.bfloat16), "seq", scatter_dimension=0, tiled=True
        ).astype(jnp.float32),
        lax.psum_scatter(
            text_value_grad.astype(jnp.bfloat16), "seq", scatter_dimension=0, tiled=True
        ).astype(jnp.float32),
        lax.psum_scatter(
            ada_grad.astype(jnp.bfloat16), "seq", scatter_dimension=0, tiled=True
        ).astype(jnp.float32),
        lax.psum_scatter(
            out_grad.astype(jnp.bfloat16), "seq", scatter_dimension=1, tiled=True
        ).astype(jnp.float32),
        lax.psum_scatter(
            down_grad.astype(jnp.bfloat16), "seq", scatter_dimension=1, tiled=True
        ).astype(jnp.float32),
    )
    smalls = lax.psum(
        (
            attn_gain_part,
            ffn_gain_part,
            query_gain_part.reshape(local_width),
            key_gain_part.reshape(local_width),
            text_gain_part.reshape(local_width),
            cross_gate_part,
            ada_bias_part,
        ),
        "seq",
    )
    return (
        block_out,
        tokens_grad,
        text_grad,
        summed[7],
        smalls[6],
        smalls[0],
        smalls[1],
        summed[0],
        summed[1],
        summed[2],
        smalls[2],
        smalls[3],
        smalls[5],
        summed[5],
        summed[6],
        smalls[4],
        summed[8],
        summed[3],
        summed[4],
        summed[9],
    )


MESH_AXES = ("z", "y", "x", "c")
PLANE_AXES = ("y", "x")
PLANE = 4
STRIPS = 4
CORES = 2


def device_pairs(target):
    pairs = []
    for strip in range(STRIPS):
        for place in range(PLANE):
            for core in range(CORES):
                aim = target(strip, place, core)
                pairs.append(
                    (
                        (strip * PLANE + place) * CORES + core,
                        (aim[0] * PLANE + aim[1]) * CORES + aim[2],
                    )
                )
    return pairs


FLIP_CORE = device_pairs(lambda strip, place, core: (strip, place, 1 - core))
FLIP_FIRST = device_pairs(lambda strip, place, core: (strip, place ^ (1 + core), core))
FLIP_SECOND = device_pairs(lambda strip, place, core: (strip, place ^ (2 - core), core))
FLIP_PLACE = {
    mask: device_pairs(lambda strip, place, core, mask=mask: (strip, place ^ mask, core))
    for mask in (1, 2, 3)
}
FLIP_STRIP = {
    mask: device_pairs(lambda strip, place, core, mask=mask: (strip ^ mask, place, core))
    for mask in (1, 2, 3)
}


def move(value, pairs):
    return lax.ppermute(value, MESH_AXES, pairs)


def gather_by(value, table):
    return [value] + [move(value, table[mask]) for mask in (1, 2, 3)]


def after(value, *earlier):
    return lax.optimization_barrier((value, earlier))[0]


def plane_gather(own, beside=()):
    own = jnp.concatenate([own, after(move(own, FLIP_FIRST), beside)])
    own = jnp.concatenate([own, move(own, FLIP_SECOND)])
    return own, move(own, FLIP_CORE)


SCATTER_STEPS = (FLIP_CORE, FLIP_SECOND, FLIP_FIRST)


def core_half(whole):
    half = whole.shape[0] // 2
    arrived = move(whole[half:], FLIP_CORE)
    return whole[:half].astype(jnp.float32) + arrived.astype(jnp.float32)


def plane_scatter(whole, *besides):
    for step, pairs in enumerate(SCATTER_STEPS[-(whole.shape[0] // 256).bit_length() :]):
        half = whole.shape[0] // 2
        arrived = move(whole[half:].astype(jnp.bfloat16), pairs)
        if step < len(besides):
            arrived = after(arrived, besides[step])
        whole = whole[:half].astype(jnp.float32) + arrived.astype(jnp.float32)
    return whole


def pair_sum(four):
    return (four[0] + four[1]) + (four[2] + four[3])


def absolute(relative, index):
    odd = (index & 1) == 1
    high = (index & 2) == 2
    step = [jnp.where(odd, relative[i ^ 1], relative[i]) for i in range(4)]
    return [jnp.where(high, step[i ^ 2], step[i]) for i in range(4)]


def across(value, axes, split, concat):
    return lax.all_to_all(value, axes, split, concat, tiled=True)


def contract(left, right, left_dim, right_dim):
    return lax.dot_general(
        left,
        right,
        (((left_dim,), (right_dim,)), ((), ())),
        preferred_element_type=jnp.float32,
    )


def turn(block, cosine, sine):
    a, b, c, d = block[0:16], block[16:32], block[32:48], block[48:64]
    cr, cc = cosine[0:16], cosine[16:32]
    sr, sc = sine[0:16], sine[16:32]
    return jnp.concatenate(
        [a * cr - b * sr, a * sr + b * cr, c * cc - d * sc, c * sc + d * cc], axis=0
    )


def unit_of(raw):
    inverse = lax.rsqrt(jnp.mean(raw * raw, axis=0, keepdims=True) + EPSILON)
    return raw * inverse, inverse


def unit_back(incoming, unit, inverse, gain):
    lifted = incoming * gain
    gain_part = jnp.sum(incoming * unit, axis=1, keepdims=True)
    raw_part = inverse * (lifted - unit * jnp.mean(lifted * unit, axis=0, keepdims=True))
    return raw_part, gain_part


QBLOCK = 256
VMEM_LIMIT = 56 * 1024 * 1024


def lanes_of(ref):
    return jnp.concatenate([ref[i] for i in range(PLANE)], axis=-1)


def text_of(ref, kind):
    part = ref.shape[-1] // 2
    lanes = slice(kind * part, (kind + 1) * part)
    return jnp.concatenate([ref[i, :, lanes] for i in range(PLANE)], axis=-1)


def attend_kernel(
    spot_ref,
    q_ref,
    k_ref,
    v_ref,
    text_ref,
    norm_ref,
    cos_ref,
    sin_ref,
    valid_ref,
    gate_ref,
    comb_ref,
    self_ref,
    cross_ref,
    qlow_ref,
    klow_ref,
    tlow_ref,
    rinv_ref,
):
    cosine, sine, valid = cos_ref[...], sin_ref[...], valid_ref[...]
    query = turn(unit_of(q_ref[...])[0] * norm_ref[:, 0:1], cosine, sine).astype(jnp.bfloat16)
    key = turn(unit_of(k_ref[...])[0] * norm_ref[:, 1:2], cosine, sine)
    qlow_ref[...] = query
    klow_ref[...] = key.astype(jnp.bfloat16)
    key_rows = key.T.astype(jnp.bfloat16)
    text_key = unit_of(text_of(text_ref, 0))[0] * norm_ref[:, 2:3]
    tlow_ref[...] = text_key.astype(jnp.bfloat16)
    text_rows = text_key.T.astype(jnp.bfloat16)
    value = v_ref[...].astype(jnp.bfloat16).astype(jnp.float32) * valid
    lanes = value.shape[1]
    value_ones = jnp.concatenate(
        [value, jnp.broadcast_to(valid, (16, lanes))], axis=0
    ).astype(jnp.bfloat16)
    tvalue = text_of(text_ref, 1)
    tvalue_ones = jnp.concatenate(
        [tvalue, jnp.ones((16, tvalue.shape[1]), jnp.float32)], axis=0
    ).astype(jnp.bfloat16)
    gate = gate_ref[0:1, 0:1]
    scaled = (query.astype(jnp.float32) * 0.125).astype(jnp.bfloat16)
    for chunk in range(lanes // QBLOCK):
        cols = slice(chunk * QBLOCK, (chunk + 1) * QBLOCK)
        weight = jnp.exp(contract(key_rows, scaled[:, cols], 1, 0)).astype(jnp.bfloat16)
        total = contract(value_ones, weight, 1, 0)
        rinv = 1.0 / total[64:65]
        own = total[:64] * rinv
        tweight = jnp.exp(contract(text_rows, scaled[:, cols], 1, 0)).astype(jnp.bfloat16)
        ttotal = contract(tvalue_ones, tweight, 1, 0)
        trinv = 1.0 / ttotal[64:65]
        text = ttotal[:64] * trinv
        self_ref[:, cols] = own
        cross_ref[:, cols] = text
        rinv_ref[0:1, cols] = rinv
        rinv_ref[1:2, cols] = trinv
        comb_ref[chunk] = (own + gate * text).astype(jnp.bfloat16)


def attend_back_kernel(
    spot_ref,
    q_ref,
    k_ref,
    v_ref,
    text_ref,
    norm_ref,
    cos_ref,
    sin_ref,
    valid_ref,
    gate_ref,
    self_ref,
    cross_ref,
    qlow_ref,
    klow_ref,
    tlow_ref,
    rinv_ref,
    dcomb_ref,
    dqkv_ref,
    dtext_ref,
    gains_ref,
):
    cosine, sine, valid = cos_ref[...], sin_ref[...], valid_ref[...]
    lanes = valid.shape[1]
    gate = gate_ref[0:1, 0:1]
    dcomb = lanes_of(dcomb_ref).astype(jnp.float32)
    cross = cross_ref[...]
    dself = dcomb.astype(jnp.bfloat16)
    dcross = (dcomb * gate).astype(jnp.bfloat16)
    delta = jnp.sum(dself.astype(jnp.float32) * self_ref[...], axis=0, keepdims=True)
    tdelta = jnp.sum(dcross.astype(jnp.float32) * cross, axis=0, keepdims=True)
    gate_part = jnp.sum(
        jnp.sum(dcomb * cross, axis=0, keepdims=True), axis=1, keepdims=True
    ) * (1.0 - gate * gate)
    query = qlow_ref[...]
    scaled = (query.astype(jnp.float32) * 0.125).astype(jnp.bfloat16)
    key = klow_ref[...].astype(jnp.float32)
    key_rows = key.T.astype(jnp.bfloat16)
    key_held = (key * valid * 0.125).astype(jnp.bfloat16)
    value_rows = v_ref[...].T.astype(jnp.bfloat16)
    text_key = tlow_ref[...].astype(jnp.float32)
    text_rows = text_key.T.astype(jnp.bfloat16)
    text_held = (text_key * 0.125).astype(jnp.bfloat16)
    tvalue_rows = text_of(text_ref, 1).T.astype(jnp.bfloat16)
    dkey = dvalue = dtkey = dtvalue = 0.0
    dquery = []
    for start in range(0, lanes, QBLOCK):
        cols = slice(start, start + QBLOCK)
        probs = jnp.exp(contract(key_rows, scaled[:, cols], 1, 0)) * rinv_ref[0:1, cols]
        dprobs = contract(value_rows, dself[:, cols], 1, 0)
        dscore = (probs * (dprobs - delta[:, cols])).astype(jnp.bfloat16)
        dvalue += contract(dself[:, cols], probs.astype(jnp.bfloat16), 1, 1)
        dkey += contract(scaled[:, cols], dscore, 1, 1)
        turned = contract(key_held, dscore, 1, 0)
        tprobs = jnp.exp(contract(text_rows, scaled[:, cols], 1, 0)) * rinv_ref[1:2, cols]
        dtprobs = contract(tvalue_rows, dcross[:, cols], 1, 0)
        dtscore = (tprobs * (dtprobs - tdelta[:, cols])).astype(jnp.bfloat16)
        dtvalue += contract(dcross[:, cols], tprobs.astype(jnp.bfloat16), 1, 1)
        dtkey += contract(scaled[:, cols], dtscore, 1, 1)
        dquery.append(turned + contract(text_held, dtscore, 1, 0))
    dquery = jnp.concatenate(dquery, axis=1)
    unit, inverse = unit_of(q_ref[...])
    draw_q, query_gain = unit_back(turn(dquery, cosine, -sine), unit, inverse, norm_ref[:, 0:1])
    unit, inverse = unit_of(k_ref[...])
    draw_k, key_gain = unit_back(turn(dkey * valid, cosine, -sine), unit, inverse, norm_ref[:, 1:2])
    unit, inverse = unit_of(text_of(text_ref, 0))
    draw_t, text_gain = unit_back(dtkey, unit, inverse, norm_ref[:, 2:3])
    dvalue = dvalue * valid
    for chunk in range(PLANE):
        cols = slice(chunk * QBLOCK, (chunk + 1) * QBLOCK)
        dqkv_ref[chunk, 0:64] = draw_q[:, cols].astype(jnp.bfloat16)
        dqkv_ref[chunk, 64:128] = draw_k[:, cols].astype(jnp.bfloat16)
        dqkv_ref[chunk, 128:192] = dvalue[:, cols].astype(jnp.bfloat16)
        size = draw_t.shape[1] // PLANE
        cols = slice(chunk * size, (chunk + 1) * size)
        dtext_ref[chunk] = jnp.concatenate([draw_t[:, cols], dtvalue[:, cols]], axis=1).astype(
            jnp.bfloat16
        )
    gains_ref[:, 0:128] = jnp.broadcast_to(query_gain, (64, 128))
    gains_ref[:, 128:256] = jnp.broadcast_to(key_gain, (64, 128))
    gains_ref[:, 256:384] = jnp.broadcast_to(text_gain, (64, 128))
    gains_ref[:, 384:512] = jnp.broadcast_to(gate_part, (64, 128))


def head_block(width, offset=0):
    return pl.BlockSpec((HDIM, width), lambda h, s: (h + offset, 0))


def shared_block(rows, width):
    return pl.BlockSpec((rows, width), lambda h, s: (0, 0))


def params():
    return pltpu.CompilerParams(vmem_limit_bytes=VMEM_LIMIT)


def cost(flops, moved):
    return pl.CostEstimate(flops=flops, bytes_accessed=moved, transcendentals=0)


def attention_call(heads, lanes, texts, backward):
    f32, b16 = jnp.float32, jnp.bfloat16
    part = texts // PLANE
    specs = [
        head_block(lanes),
        head_block(lanes, heads),
        head_block(lanes, 2 * heads),
        pl.BlockSpec((PLANE, HDIM, 2 * part), lambda h, s: (0, h, 0)),
        pl.BlockSpec((HDIM, 3), lambda h, s: (s[0] * heads + h, 0)),
        shared_block(32, lanes),
        shared_block(32, lanes),
        shared_block(1, lanes),
        pl.BlockSpec((8, 128), lambda h, s: (s[0] * heads + h, 0)),
    ]
    wide = heads * HDIM
    chunk_spec = pl.BlockSpec((PLANE, HDIM, QBLOCK), lambda h, s: (0, h, 0))
    rinv_spec = pl.BlockSpec((8, lanes), lambda h, s: (h, 0))
    saved = [head_block(lanes)] * 4 + [head_block(texts), rinv_spec]
    shape = jax.ShapeDtypeStruct
    pairs = heads * lanes * (lanes + texts)
    if not backward:
        out_specs = [chunk_spec] + saved
        out_shape = [
            shape((PLANE, wide, lanes // PLANE), b16),
            shape((wide, lanes), f32),
            shape((wide, lanes), f32),
            shape((wide, lanes), b16),
            shape((wide, lanes), b16),
            shape((wide, texts), b16),
            shape((heads * 8, lanes), f32),
        ]
        body, passes = attend_kernel, 2
    else:
        specs = specs + saved + [chunk_spec]
        out_specs = [
            pl.BlockSpec((PLANE, 3 * HDIM, QBLOCK), lambda h, s: (0, h, 0)),
            pl.BlockSpec((PLANE, HDIM, 2 * part), lambda h, s: (0, h, 0)),
            head_block(512),
        ]
        out_shape = [
            shape((PLANE, 3 * wide, lanes // PLANE), b16),
            shape((PLANE, wide, 2 * part), b16),
            shape((wide, 512), f32),
        ]
        body, passes = attend_back_kernel, 5
    return pl.pallas_call(
        body,
        grid_spec=pltpu.PrefetchScalarGridSpec(
            num_scalar_prefetch=1, grid=(heads,), in_specs=specs, out_specs=out_specs
        ),
        out_shape=out_shape,
        compiler_params=params(),
        cost_estimate=cost(8 * pairs * HDIM * passes, 8 * wide * lanes),
    )


def project_kernel(spot_ref, own_ref, other_ref, lift_ref, weight_ref, in_ref, qkv_ref, turned):
    @pl.when(pl.program_id(0) == 0)
    def _():
        turned[...] = weight_ref[...].T

    first = spot_ref[1] == 0
    own, other = own_ref[...].astype(jnp.float32), other_ref[...].astype(jnp.float32)
    values = jnp.concatenate([jnp.where(first, own, other), jnp.where(first, other, own)])
    normed = (values * rms_inverse(values) * lift_ref[...]).astype(jnp.bfloat16)
    in_ref[...] = normed
    qkv_ref[...] = contract(turned[...], normed, 1, 1)


def project(spot, halves, lift, weight):
    rows, width = halves[0].shape
    wide = weight.shape[1]
    block = rows // PLANE
    return pl.pallas_call(
        project_kernel,
        grid_spec=pltpu.PrefetchScalarGridSpec(
            num_scalar_prefetch=1,
            grid=(PLANE,),
            in_specs=[
                pl.BlockSpec((block, width), lambda i, s: (i, 0)),
                pl.BlockSpec((block, width), lambda i, s: (i % 2 * 2 + i // 2, 0)),
                pl.BlockSpec((1, width), lambda i, s: (0, 0)),
                pl.BlockSpec((width, wide), lambda i, s: (0, 0)),
            ],
            out_specs=[
                pl.BlockSpec((2 * block, width), lambda i, s: (s[2 + i] // 2, 0)),
                pl.BlockSpec((wide, 2 * block), lambda i, s: (0, s[2 + i] // 2)),
            ],
            scratch_shapes=[pltpu.VMEM((wide, width), jnp.bfloat16)],
        ),
        out_shape=[
            jax.ShapeDtypeStruct((2 * rows, width), jnp.bfloat16),
            jax.ShapeDtypeStruct((wide, 2 * rows), jnp.float32),
        ],
        compiler_params=params(),
        cost_estimate=cost(4 * rows * width * wide, 16 * rows * width),
    )(spot, *halves, lift, weight)


def ffn_kernel(spot_ref, a_ref, b_ref, d0_ref, d1_ref, gw_ref, uw_ref, dw_ref, h_ref, din_ref):
    early = pl.program_id(0) < 2
    rows_in = jnp.where(early, a_ref[...], b_ref[...])
    d_out = jnp.concatenate([d0_ref[...], d1_ref[...]])
    size = gw_ref.shape[1]
    gate_pre = jnp.dot(rows_in, gw_ref[...], preferred_element_type=jnp.float32)
    up_pre = jnp.dot(rows_in, uw_ref[...], preferred_element_type=jnp.float32)
    d_hidden = contract(d_out, dw_ref[...], 1, 1)
    gate_sig = jax.nn.sigmoid(gate_pre)
    swish = gate_pre * gate_sig
    d_gate = (d_hidden * up_pre * (gate_sig + swish * (1.0 - gate_sig))).astype(jnp.bfloat16)
    d_up = (d_hidden * swish).astype(jnp.bfloat16)
    h_ref[:, 0:size] = d_gate
    h_ref[:, size : 2 * size] = d_up
    h_ref[:, 2 * size : 3 * size] = (swish * up_pre).astype(jnp.bfloat16)
    din_ref[...] = (
        contract(d_gate, gw_ref[...], 1, 1) + contract(d_up, uw_ref[...], 1, 1)
    ).astype(jnp.bfloat16)


def ffn(spot, halves, d_ffn, gate_weight, up_weight, down_weight):
    rows, width = halves[0].shape
    size = gate_weight.shape[1] // PLANE
    block = rows // 2
    early = pl.BlockSpec((block, width), lambda i, s: (jnp.minimum(i, 1), 0))
    late = pl.BlockSpec((block, width), lambda i, s: (jnp.maximum(i - 2, 0), 0))
    col = pl.BlockSpec((width, size), lambda i, s: (0, s[0]))
    return pl.pallas_call(
        ffn_kernel,
        grid_spec=pltpu.PrefetchScalarGridSpec(
            num_scalar_prefetch=1,
            grid=(4,),
            in_specs=[
                early,
                late,
                pl.BlockSpec((block // 2, width), lambda i, s: (s[2 + 2 * i], 0)),
                pl.BlockSpec((block // 2, width), lambda i, s: (s[3 + 2 * i], 0)),
                col,
                col,
                pl.BlockSpec((size, width), lambda i, s: (s[0], 0)),
            ],
            out_specs=[
                pl.BlockSpec((block, 3 * size), lambda i, s: (i, 0)),
                pl.BlockSpec((block, width), lambda i, s: (i, 0)),
            ],
        ),
        out_shape=[
            jax.ShapeDtypeStruct((2 * rows, 3 * size), jnp.bfloat16),
            jax.ShapeDtypeStruct((2 * rows, width), jnp.bfloat16),
        ],
        compiler_params=params(),
        cost_estimate=cost(20 * rows * width * size, 16 * rows * width),
    )(spot, *halves, d_ffn, d_ffn, gate_weight, up_weight, down_weight)


def ffn_grad_kernel(
    spot_ref, a_ref, b_ref, d_ref, tile_ref, hid_ref, dw_ref, grad_ref, out_ref, turned
):
    step = pl.program_id(0)
    rows = a_ref.shape[0]

    @pl.when(step == 0)
    def _():
        turned[:, :rows] = a_ref[...].T
        turned[:, rows:] = b_ref[...].T

    @pl.when(step == 4)
    def _():
        size = rows // 4
        for block in range(8):
            start = pl.multiple_of(spot_ref[2 + block] * size, size)
            turned[:, block * size : (block + 1) * size] = d_ref[pl.ds(start, size), :].T

    grad_ref[...] = jnp.dot(
        turned[...], tile_ref[...], preferred_element_type=jnp.float32
    ).astype(jnp.bfloat16)

    @pl.when(step < 4)
    def _():
        out_ref[...] = jnp.dot(
            hid_ref[...], dw_ref[...], preferred_element_type=jnp.float32
        ).astype(jnp.bfloat16)


def ffn_grad(spot, halves, d_ffn, inner, down_weight):
    rows, width = halves[0].shape
    size = inner.shape[1] // 3
    whole = pl.BlockSpec((rows, width), lambda i, s: (0, 0))
    tile = size // 2
    quarter = rows // 2
    return pl.pallas_call(
        ffn_grad_kernel,
        grid_spec=pltpu.PrefetchScalarGridSpec(
            num_scalar_prefetch=1,
            grid=(6,),
            in_specs=[
                whole,
                whole,
                pl.BlockSpec((2 * rows, width), lambda i, s: (0, 0)),
                pl.BlockSpec((2 * rows, tile), lambda i, s: (0, i)),
                pl.BlockSpec((quarter, size), lambda i, s: (jnp.minimum(i, 3), 2)),
                pl.BlockSpec((size, width), lambda i, s: (s[0], 0)),
            ],
            out_specs=[
                pl.BlockSpec((width, tile), lambda i, s: (0, i)),
                pl.BlockSpec((quarter, width), lambda i, s: (jnp.minimum(i, 3), 0)),
            ],
            scratch_shapes=[pltpu.VMEM((width, 2 * rows), jnp.bfloat16)],
        ),
        out_shape=[
            jax.ShapeDtypeStruct((width, 3 * size), jnp.bfloat16),
            jax.ShapeDtypeStruct((2 * rows, width), jnp.bfloat16),
        ],
        compiler_params=params(),
        cost_estimate=cost(16 * rows * width * size, 16 * rows * width),
    )(spot, *halves, d_ffn, inner, inner, down_weight)


def by_kind(block, kind, heads):
    return jnp.concatenate(
        [
            block[i, (3 * h + kind) * HDIM : (3 * h + kind + 1) * HDIM]
            for i in range(block.shape[0])
            for h in range(heads)
        ],
        axis=0,
    )


def input_grad_kernel(d_ref, qw_ref, kw_ref, vw_ref, out_ref):
    heads = d_ref.shape[1] // (3 * HDIM)
    total = 0.0
    for kind, weight in enumerate((qw_ref, kw_ref, vw_ref)):
        total += contract(by_kind(d_ref, kind, heads).T, weight[...], 1, 1)
    out_ref[...] = total


def input_grad(d_qkv, query_weight, key_weight, value_weight):
    width, wide = query_weight.shape
    rows = d_qkv.shape[2]
    tile = width // 3
    weight = pl.BlockSpec((tile, wide), lambda i: (i, 0))
    return pl.pallas_call(
        input_grad_kernel,
        grid=(3,),
        in_specs=[pl.BlockSpec(d_qkv.shape, lambda i: (0, 0, 0)), weight, weight, weight],
        out_specs=pl.BlockSpec((rows, tile), lambda i: (0, i)),
        out_shape=jax.ShapeDtypeStruct((rows, width), jnp.float32),
        compiler_params=params(),
        cost_estimate=cost(6 * rows * width * wide, 6 * width * wide),
    )(d_qkv, query_weight, key_weight, value_weight)


def attn_grad_kernel(spot_ref, in_ref, own_ref, other_ref, d_ref, comb_ref, out_ref):
    places, _, rows = d_ref.shape
    wide = comb_ref.shape[1]
    heads = wide // HDIM
    first = spot_ref[1] == 0
    total = branch = 0.0
    for place in range(places):
        part = slice(place * rows, (place + 1) * rows)
        block = d_ref[place : place + 1]
        ordered = jnp.concatenate([by_kind(block, kind, heads) for kind in range(3)])
        total += contract(in_ref[part].T, ordered, 1, 1)
        own, other = own_ref[place], other_ref[place]
        d_attn = jnp.concatenate([jnp.where(first, own, other), jnp.where(first, other, own)])
        branch += contract(d_attn.T, comb_ref[place], 1, 1)
    out_ref[:, : 3 * wide] = total.astype(jnp.bfloat16)
    out_ref[:, 3 * wide :] = branch.astype(jnp.bfloat16)


def attn_grad(spot, attn_in, own_d_attn, other_d_attn, d_qkv, combined):
    rows, width = attn_in.shape
    wide = combined.shape[1]
    tile = width // 3
    core_rows = pl.BlockSpec(own_d_attn.shape[:2] + (tile,), lambda i, s: (0, 0, i))
    return pl.pallas_call(
        attn_grad_kernel,
        grid_spec=pltpu.PrefetchScalarGridSpec(
            num_scalar_prefetch=1,
            grid=(3,),
            in_specs=[
                pl.BlockSpec((rows, tile), lambda i, s: (0, i)),
                core_rows,
                core_rows,
                pl.BlockSpec(d_qkv.shape, lambda i, s: (0, 0, 0)),
                pl.BlockSpec(combined.shape, lambda i, s: (0, 0, 0)),
            ],
            out_specs=pl.BlockSpec((tile, 4 * wide), lambda i, s: (i, 0)),
        ),
        out_shape=jax.ShapeDtypeStruct((width, 4 * wide), jnp.bfloat16),
        compiler_params=params(),
        cost_estimate=cost(8 * rows * width * wide, 4 * rows * width),
    )(spot, attn_in, own_d_attn, other_d_attn, d_qkv, combined)


def strips_kernel(in_ref, out_ref):
    size = out_ref.shape[2]
    for strip in range(out_ref.shape[0]):
        out_ref[strip] = in_ref[:, strip * size : (strip + 1) * size]


def by_strips(states):
    rows, cols = states.shape
    return pl.pallas_call(
        strips_kernel,
        out_shape=jax.ShapeDtypeStruct((STRIPS, rows, cols // STRIPS), states.dtype),
        compiler_params=params(),
        cost_estimate=cost(0, 4 * rows * cols),
    )(states)


def text_grad_kernel(where_ref, *refs):
    states, d_text, out_ref = refs[:PLANE], refs[PLANE : 2 * PLANE], refs[2 * PLANE]
    own = where_ref[1]
    part = d_text[0].shape[2] // 2
    total = 0.0
    for mask in range(PLANE):
        place = where_ref[0] ^ mask
        blocks = [
            jnp.concatenate([piece[place, :, :part], piece[place, :, part:]]) for piece in d_text
        ]
        rows = [
            states[mask][pl.ds(pl.multiple_of((own ^ strip) * part, part), part), :]
            for strip in range(STRIPS)
        ]
        total += jnp.dot(
            jnp.concatenate(blocks, axis=-1),
            jnp.concatenate(rows),
            preferred_element_type=jnp.float32,
        )
    size = total.shape[1] // PLANE
    for place in range(PLANE):
        out_ref[place] = total[:, place * size : (place + 1) * size].astype(jnp.bfloat16)


def text_weight_grad(where_here, states, strips):
    rows, cols = states[0].shape
    wide = 2 * strips[0].shape[1]
    whole = pl.BlockSpec(memory_space=pltpu.VMEM)
    return pl.pallas_call(
        text_grad_kernel,
        in_specs=[pl.BlockSpec(memory_space=pltpu.SMEM)] + [whole] * 8,
        out_specs=whole,
        out_shape=jax.ShapeDtypeStruct((PLANE, wide, cols // PLANE), jnp.bfloat16),
        compiler_params=params(),
        cost_estimate=cost(8 * rows * cols * wide, 8 * rows * cols),
    )(where_here, *states, *strips)


def split_three(value):
    high = lax.reduce_precision(value, 8, 7)
    middle = lax.reduce_precision(value - high, 8, 7)
    return jnp.concatenate([high, middle, value - high - middle]).astype(jnp.bfloat16)


def strip_shards(
    tokens,
    cotangent,
    step_embed,
    item_band,
    item_length,
    item_width,
    text_states,
    ada_weight,
    ada_bias,
    attn_gain,
    ffn_gain,
    query_weight,
    key_weight,
    value_weight,
    query_gain,
    key_gain,
    cross_gate,
    text_key_weight,
    text_value_weight,
    text_key_gain,
    out_weight,
    gate_weight,
    up_weight,
    down_weight,
):
    f32, b16 = jnp.float32, jnp.bfloat16
    strip = lax.axis_index("z")
    place = lax.axis_index("y") * 2 + lax.axis_index("x")
    core = lax.axis_index("c")
    first_core = core == 0
    spot = [place, core]
    for block in range(2 * PLANE):
        from_core = core ^ (block // PLANE)
        from_place = place
        if block & 1:
            from_place = from_place ^ (1 + from_core)
        if block & 2:
            from_place = from_place ^ (2 - from_core)
        spot.append(from_place * CORES + from_core)
    spot = jnp.stack(spot).astype(jnp.int32)
    width = tokens.shape[1]
    half = SLOT // CORES
    own_rows = STRIPS * half
    lanes = own_rows * PLANE * CORES
    wide = query_weight.shape[1] // PLANE
    heads = wide // HDIM
    hidden_wide = gate_weight.shape[1] // PLANE
    text_own = text_states.shape[0]
    texts = text_own * PLANE

    def both_cores(own, axis=0):
        other = move(own, FLIP_CORE)
        low = jnp.where(first_core, own, other)
        high = jnp.where(first_core, other, own)
        return jnp.concatenate([low, high], axis=axis)

    def core_scatter(partial, axis=0):
        size = partial.shape[axis] // CORES
        sent = lax.dynamic_slice_in_dim(partial, (1 - core) * size, size, axis)
        kept = lax.dynamic_slice_in_dim(partial, core * size, size, axis)
        return kept.astype(f32) + move(sent.astype(b16), FLIP_CORE).astype(f32)

    def to_items(*arrays):
        parts = [
            lax.dynamic_slice_in_dim(a.reshape(ITEMS, SLOT, width), core * half, half, 1)
            for a in arrays
        ]
        parts = across(jnp.concatenate(parts, axis=1), "z", 0, 0)
        parts = parts.reshape(STRIPS, len(arrays), half, width)
        return [parts[:, i].reshape(own_rows, width) for i in range(len(arrays))]

    def from_items(beside, *arrays):
        parts = jnp.concatenate([a.reshape(STRIPS, half, width) for a in arrays], axis=1)
        parts = across(parts, "z", 0, 0)
        other = move(after(parts, beside), FLIP_CORE)
        outs = []
        for i in range(len(arrays)):
            own_part, other_part = (p[:, i * half : (i + 1) * half] for p in (parts, other))
            low = jnp.where(first_core, own_part, other_part)
            high = jnp.where(first_core, other_part, own_part)
            outs.append(jnp.concatenate([low, high], axis=1).reshape(ITEMS * SLOT, width))
        return outs

    own_tokens, incoming_low = to_items(tokens, cotangent)
    text_raw = jnp.concatenate(
        [
            contract(text_key_weight, text_states, 0, 1),
            contract(text_value_weight, text_states, 0, 1).astype(b16).astype(f32),
        ],
        axis=1,
    ).reshape(PLANE, wide, 2 * text_own)
    qkv_weight = jnp.concatenate(
        [
            lax.dynamic_slice_in_dim(weight, place * wide, wide, 1)
            for weight in (query_weight, key_weight, value_weight)
        ],
        axis=1,
    )
    silu_embed = jax.nn.silu(step_embed.astype(f32))
    products = jnp.dot(split_three(silu_embed), ada_weight, preferred_element_type=f32)
    local_mod = products[0:4] + products[4:8] + products[8:12] + ada_bias
    own_tokens = after(own_tokens, text_raw, qkv_weight, local_mod)
    pair = jnp.concatenate([own_tokens, move(own_tokens, FLIP_FIRST)])
    pair_arrived = move(pair, FLIP_SECOND)
    text_raw = across(after(text_raw, pair), PLANE_AXES, 0, 0)

    other_mod = move(after(local_mod, own_tokens), FLIP_CORE)
    low_mod = jnp.where(first_core, local_mod, other_mod)
    high_mod = jnp.where(first_core, other_mod, local_mod)

    item_ids = jnp.arange(ITEMS, dtype=jnp.int32)
    band_mask = (item_band[:, None] == item_ids[None, :]).astype(f32)
    own_mask = jnp.sum(jnp.where(item_ids[:, None] == strip, band_mask, 0.0), axis=0)

    own_low = jnp.sum(own_mask[:, None] * low_mod, axis=0)
    own_high = jnp.sum(own_mask[:, None] * high_mod, axis=0)
    scale_attn, scale_ffn = own_low[:width], own_high[:width]
    lift_attn = attn_gain * (1.0 + scale_attn)
    lift_ffn = ffn_gain * (1.0 + scale_ffn)
    gate_attn = jnp.tanh(own_low[width:])
    gate_ffn = jnp.tanh(own_high[width:])

    lane = jnp.arange(lanes, dtype=jnp.int32)
    from_place = lane // (own_rows * CORES)
    from_core = (lane // own_rows) % CORES
    from_strip = (lane % own_rows) // half
    position = (from_strip * PLANE + from_place) * SLOT + from_core * half + lane % half
    chosen = jnp.where(item_ids[:, None] == strip, 1, 0)
    width_here = jnp.sum(chosen * after(item_width, pair)[:, None], axis=0)
    length_here = jnp.sum(chosen * item_length[:, None], axis=0)
    grid_row = (position // width_here).astype(f32)
    grid_col = (position % width_here).astype(f32)
    quarter = HDIM // 4
    frequency = ROPE_BASE ** (-jnp.arange(quarter, dtype=f32) / quarter)
    angles = jnp.concatenate(
        [frequency[:, None] * grid_row[None, :], frequency[:, None] * grid_col[None, :]]
    )
    cosine, sine = jnp.cos(angles), jnp.sin(angles)
    valid = (position < length_here).astype(f32)[None, :]

    norm_gains = jnp.stack([query_gain, key_gain, text_key_gain], axis=1)
    gate_tiles = jnp.broadcast_to(jnp.tanh(cross_gate)[:, None, None], (cross_gate.shape[0], 8, 128))
    gate_tiles = gate_tiles.reshape(-1, 128)

    low_half = jnp.concatenate([pair, after(pair_arrived, lift_attn, text_raw)])
    incoming = after(incoming_low, pair).astype(f32)
    own_d_ffn = (gate_ffn * incoming).astype(b16)
    high_half = after(move(low_half, FLIP_CORE), cosine, sine, norm_gains, gate_tiles, own_d_ffn)
    d_ffn = lax.all_gather(after(own_d_ffn, low_half), PLANE_AXES + ("c",), axis=0, tiled=True)
    attn_in, qkv = project(spot, (low_half, high_half), lift_attn[None, :], qkv_weight)
    common = (
        spot,
        qkv,
        qkv,
        qkv,
        text_raw,
        norm_gains,
        cosine,
        sine,
        valid,
        gate_tiles,
    )
    combined, *saved = attention_call(heads, lanes, texts, False)(*common)
    states_wide = text_states.shape[1] // STRIPS
    states = across(by_strips(after(text_states, qkv)), "z", 0, 0).reshape(texts, states_wide)
    combined = after(combined, states)
    chip_combined = across(combined, PLANE_AXES, 0, 0).reshape(-1, own_rows * CORES)
    attn_branch = core_scatter(contract(chip_combined, out_weight, 0, 0))

    residual = own_tokens.astype(f32)
    middle = residual + gate_attn * attn_branch
    inverse_two = rms_inverse(middle)
    normed_two = middle * inverse_two
    own_ffn_in = (normed_two * lift_ffn).astype(b16)
    ffn_in = plane_gather(after(own_ffn_in, d_ffn))
    inner, d_ffn_in = ffn(spot, ffn_in, d_ffn, gate_weight, up_weight, down_weight)
    ffn_grads, ffn_branch = ffn_grad(spot, ffn_in, d_ffn, inner, down_weight)
    branch_half = core_half(ffn_branch)
    d_ffn_in = plane_scatter(d_ffn_in, (ffn_grads,), (branch_half,))
    d_normed = d_ffn_in * normed_two
    u_ffn = jnp.sum(d_normed, axis=0)
    d_middle = incoming + inverse_two * (
        d_ffn_in * lift_ffn
        - normed_two * jnp.mean(d_normed * lift_ffn, axis=-1, keepdims=True)
    )
    w_attn = jnp.sum(d_middle * attn_branch, axis=0) * (1.0 - gate_attn * gate_attn)
    own_d_attn = (gate_attn * d_middle).astype(b16)
    d_attn = both_cores(own_d_attn)

    d_comb = contract(out_weight, d_attn, 1, 1).astype(b16).reshape(PLANE, wide, -1)
    d_comb = across(d_comb, PLANE_AXES, 0, 0)
    ffn_branch = plane_scatter(after(branch_half, d_comb))
    d_qkv, d_text, gains = attention_call(heads, lanes, texts, True)(*common, *saved, d_comb)
    own_rows_d = jnp.broadcast_to(after(own_d_attn, d_comb), (PLANE, own_rows, width))
    own_rows_d = across(own_rows_d, PLANE_AXES, 0, 0)
    own_rows_d = after(own_rows_d, d_qkv)
    attn_grads = attn_grad(spot, attn_in, own_rows_d, move(own_rows_d, FLIP_CORE), d_qkv, combined)
    chip_d_qkv = after(across(d_qkv, PLANE_AXES, 0, 0), attn_grads)
    d_attn_in = core_scatter(input_grad(chip_d_qkv, query_weight, key_weight, value_weight))
    inverse_one = rms_inverse(residual)
    normed_one = residual * inverse_one
    d_normed = d_attn_in * normed_one
    u_attn = jnp.sum(d_normed, axis=0)
    tokens_grad = d_middle + inverse_one * (
        d_attn_in * lift_attn
        - normed_one * jnp.mean(d_normed * lift_attn, axis=-1, keepdims=True)
    )

    w_ffn = jnp.sum(incoming * ffn_branch, axis=0) * (1.0 - gate_ffn * gate_ffn)
    block_out = (middle + gate_ffn * ffn_branch).astype(b16)

    def spread(own):
        blocks = own.reshape(PLANE, own.shape[0] // PLANE, own.shape[1])
        return across(blocks, PLANE_AXES, 0, 0)

    def sheet(blocks, start, size):
        return jnp.concatenate(
            [blocks[i, :, start : start + size] for i in range(PLANE)], axis=1
        ).astype(f32)

    ffn_own = lax.psum_scatter(ffn_grads, "z", scatter_dimension=0, tiled=True)
    d_text_all = gather_by(d_text, FLIP_STRIP)
    attn_grads = lax.psum_scatter(after(attn_grads, ffn_own, d_text_all), "z", scatter_dimension=0, tiled=True)
    ffn_blocks = spread(ffn_own)
    attn_blocks = spread(attn_grads)
    block_out, tokens_grad = from_items(ffn_blocks, block_out, tokens_grad.astype(b16))
    gate_grad = sheet(ffn_blocks, 0, hidden_wide)
    up_grad = sheet(ffn_blocks, hidden_wide, hidden_wide)
    down_grad = sheet(ffn_blocks, 2 * hidden_wide, hidden_wide).T
    out_grad = sheet(attn_blocks, 3 * wide, wide).T
    query_grad = sheet(attn_blocks, 0, wide)
    key_grad = sheet(attn_blocks, wide, wide)
    value_grad = sheet(attn_blocks, 2 * wide, wide)

    back = across(after(d_text, chip_d_qkv), PLANE_AXES, 0, 0)
    back = after(back, attn_grads).reshape(-1, 2 * text_own)
    back = [back[:, :text_own], back[:, text_own:]]
    text_grad = core_scatter(
        contract(back[0], text_key_weight, 0, 1) + contract(back[1], text_value_weight, 0, 1), 1
    )
    states = gather_by(after(states, d_qkv), FLIP_PLACE)
    where_here = jnp.stack([place, strip]).astype(jnp.int32)
    states[0] = after(states[0], ffn_blocks)
    text_sum = text_weight_grad(where_here, states, d_text_all)
    text_blocks = across(text_sum, PLANE_AXES, 0, 0)
    text_key_grad = text_blocks[:, :wide].reshape(PLANE * wide, -1).T.astype(f32)
    text_value_grad = text_blocks[:, wide:].reshape(PLANE * wide, -1).T.astype(f32)

    own_sums = jnp.concatenate([u_attn, u_ffn, w_ffn, w_attn])
    own_sums = own_sums + move(own_sums, FLIP_CORE)
    count = own_sums.shape[0]
    parts = jnp.concatenate(
        [own_sums, gains[:, 0], gains[:, 128], gains[:, 256], gains[:, 384]]
    )
    parts = gather_by(parts, FLIP_PLACE)
    head_parts = absolute([p[count:].reshape(4, wide) for p in parts], place)
    parts = jnp.concatenate(
        [pair_sum([p[:count] for p in parts]), jnp.concatenate(head_parts, axis=1).reshape(-1)]
    )
    parts = gather_by(after(parts, attn_grads), FLIP_STRIP)
    head_parts = pair_sum([p[count:] for p in parts]).reshape(4, PLANE * wide)
    sums = [p[:count].reshape(4, width) for p in absolute(parts, strip)]
    items = []
    for item in range(ITEMS):
        low_part = jnp.concatenate([attn_gain * sums[item][0], sums[item][3]])
        high_part = jnp.concatenate([ffn_gain * sums[item][1], sums[item][2]])
        items.append(jnp.where(first_core, low_part, high_part))
    ada_bias_grad = pair_sum(items)
    def by_item(table):
        return jnp.sum(band_mask[:, :, None] * table[None], axis=1)

    scales = by_item(low_mod[:, :width]), by_item(high_mod[:, :width])
    attn_gain_grad = pair_sum([sums[i][0] * (1.0 + scales[0][i]) for i in range(ITEMS)])
    ffn_gain_grad = pair_sum([sums[i][1] * (1.0 + scales[1][i]) for i in range(ITEMS)])
    ada_rows = silu_embed.shape[1] // (STRIPS * PLANE)
    silu_own = lax.dynamic_slice_in_dim(
        silu_embed, (strip * PLANE + place) * ada_rows, ada_rows, 1
    )
    ada_grad = lax.dot_general(
        by_item(silu_own), jnp.stack(items), (((0,), (0,)), ((), ())), precision=HIGHEST
    )
    return (
        block_out,
        tokens_grad,
        text_grad,
        ada_grad,
        ada_bias_grad,
        attn_gain_grad,
        ffn_gain_grad,
        query_grad,
        key_grad,
        value_grad,
        head_parts[0],
        head_parts[1],
        head_parts[3].reshape(-1, HDIM)[:, 0],
        text_key_grad,
        text_value_grad,
        head_parts[2],
        out_grad,
        gate_grad,
        up_grad,
        down_grad,
    )


def placements(seq, tp):
    ins = (
        P(seq, None),
        P(seq, None),
        P(),
        P(),
        P(),
        P(),
        P(seq, None),
        P(None, tp),
        P(tp),
        P(),
        P(),
        P(None, tp),
        P(None, tp),
        P(None, tp),
        P(tp),
        P(tp),
        P(tp),
        P(None, tp),
        P(None, tp),
        P(tp),
        P(tp, None),
        P(None, tp),
        P(None, tp),
        P(tp, None),
    )
    outs = (
        P(seq, None),
        P(seq, None),
        P(seq, tp),
        P(seq, tp),
        P(tp),
        P(),
        P(),
        P(seq, tp),
        P(seq, tp),
        P(seq, tp),
        P(tp),
        P(tp),
        P(tp),
        P(seq, tp),
        P(seq, tp),
        P(tp),
        P(tp, seq),
        P(seq, tp),
        P(seq, tp),
        P(tp, seq),
    )
    return ins, outs


def solution(mesh):
    if mesh.shape["seq"] == STRIPS * PLANE and mesh.shape["tp"] == CORES:
        body, seq, tp = strip_shards, ("z", "y", "x"), "c"
        mesh = Mesh(mesh.devices.reshape(STRIPS, 2, 2, CORES), MESH_AXES)
    else:
        body, seq, tp = shards, "seq", "tp"
    ins, outs = placements(seq, tp)
    return jax.shard_map(body, mesh=mesh, in_specs=ins, out_specs=outs, check_vma=False)
```

```python
import jax
import jax.numpy as jnp
from jax import lax
from jax.experimental import pallas as pl
from jax.experimental.pallas import tpu as pltpu
from jax.sharding import Mesh
from jax.sharding import PartitionSpec as P

HDIM = 64
NTXT = 256
BANDS = 4
ITEMS = 4
SLOT = 64


EPSILON = 1e-06
ROPE_BASE = 10000.0
HIGHEST = lax.Precision.HIGHEST
NEG_FILL = -1e30


def rms_inverse(values):
    return lax.rsqrt(jnp.mean(values * values, axis=-1, keepdims=True) + EPSILON)


def rope_angles(row_pos, col_pos, head_dim):
    quarter = head_dim // 4
    frequency = ROPE_BASE ** (-jnp.arange(quarter, dtype=jnp.float32) / quarter)
    angles = jnp.stack([row_pos[..., None] * frequency, col_pos[..., None] * frequency], axis=-2)
    return (jnp.cos(angles), jnp.sin(angles))


def rotate(vectors, cosines, sines):
    shape_all = vectors.shape
    paired = vectors.reshape(shape_all[:-1] + (2, 2, shape_all[-1] // 4))
    former = paired[..., 0, :]
    latter = paired[..., 1, :]
    turned = jnp.stack(
        [former * cosines - latter * sines, former * sines + latter * cosines], axis=-2
    )
    return turned.reshape(shape_all)


def head_norm(raw_vals, gain_vec):
    inverse = rms_inverse(raw_vals)
    unit_vec = raw_vals * inverse
    return (unit_vec * gain_vec, unit_vec, inverse)


def head_norm_back(incoming, unit_vec, inverse, gain_vec):
    grad_unit = incoming * gain_vec
    gain_part = jnp.sum(incoming * unit_vec, axis=tuple(range(incoming.ndim - 2)))
    grad_raw = inverse * (
        grad_unit - unit_vec * jnp.mean(grad_unit * unit_vec, axis=-1, keepdims=True)
    )
    return (grad_raw, gain_part)


def token_norm_back(incoming, normed, inverse, gain_vec, scale_mod):
    lifted = 1.0 + scale_mod
    gain_part = jnp.sum(incoming * normed * lifted, axis=(0, 1))
    scale_part = jnp.sum(incoming * normed * gain_vec, axis=1)
    grad_normed = incoming * gain_vec * lifted
    grad_in = inverse * (
        grad_normed - normed * jnp.mean(grad_normed * normed, axis=-1, keepdims=True)
    )
    return (grad_in, gain_part, scale_part)


def attend(query_h, key_h, value_h, key_valid):
    scaling = query_h.shape[-1] ** (-0.5)
    scores = (
        jnp.einsum("isd,ikd->isk", query_h, key_h, preferred_element_type=jnp.float32) * scaling
    )
    if key_valid is not None:
        scores = jnp.where(key_valid[:, None, :], scores, NEG_FILL)
    row_max = jnp.max(scores, axis=-1, keepdims=True)
    exp_scores = jnp.exp(scores - row_max)
    row_total = jnp.sum(exp_scores, axis=-1, keepdims=True)
    probability = (exp_scores / row_total).astype(jnp.bfloat16)
    output = jnp.einsum("isk,ikd->isd", probability, value_h, preferred_element_type=jnp.float32)
    return (output, (row_max + jnp.log(row_total))[..., 0])


def attend_back(query_h, key_h, value_h, key_valid, lse_h, dout_h):
    scaling = query_h.shape[-1] ** (-0.5)
    scores = (
        jnp.einsum("isd,ikd->isk", query_h, key_h, preferred_element_type=jnp.float32) * scaling
    )
    if key_valid is not None:
        scores = jnp.where(key_valid[:, None, :], scores, NEG_FILL)
    probability = jnp.exp(scores - lse_h[..., None])
    d_prob = jnp.einsum("isd,ikd->isk", dout_h, value_h, preferred_element_type=jnp.float32)
    delta_row = jnp.sum(d_prob * probability, axis=-1)
    d_score = (probability * (d_prob - delta_row[..., None])).astype(jnp.bfloat16)
    d_query = (
        jnp.einsum("isk,ikd->isd", d_score, key_h, preferred_element_type=jnp.float32) * scaling
    )
    d_key = (
        jnp.einsum("isk,isd->ikd", d_score, query_h, preferred_element_type=jnp.float32) * scaling
    )
    d_value = jnp.einsum(
        "isk,isd->ikd", probability.astype(jnp.bfloat16), dout_h, preferred_element_type=jnp.float32
    )
    return (d_query, delta_row, d_key, d_value)


def head_total(partial_value):
    return lax.psum(partial_value.astype(jnp.bfloat16), "tp").astype(jnp.float32)


def feature_total(partial_value):
    return lax.psum(partial_value.astype(jnp.bfloat16), "tp").astype(jnp.float32)


def shards(
    tokens,
    cotangent,
    step_embed,
    item_band,
    item_length,
    item_width,
    text_states,
    ada_weight,
    ada_bias,
    attn_gain,
    ffn_gain,
    query_weight,
    key_weight,
    value_weight,
    query_gain,
    key_gain,
    cross_gate,
    text_key_weight,
    text_value_weight,
    text_key_gain,
    out_weight,
    gate_weight,
    up_weight,
    down_weight,
):
    seq_count = lax.axis_size("seq")
    seq_index = lax.axis_index("seq")
    tp_index = lax.axis_index("tp")
    tok_dev, model_width = tokens.shape
    local_width = query_weight.shape[1]
    local_heads = local_width // HDIM
    capacity = SLOT * seq_count
    text_rows = text_states.shape[0]
    mod_cols = ada_weight.shape[1]
    head_shape = (ITEMS, SLOT, local_heads, HDIM)
    silu_embed = jax.nn.silu(step_embed.astype(jnp.float32))
    local_mod = jnp.dot(silu_embed, ada_weight.astype(jnp.float32), precision=HIGHEST) + ada_bias
    band_mod = lax.all_gather(local_mod, "tp", axis=1, tiled=True)
    band_onehot = (item_band[:, None] == jnp.arange(BANDS, dtype=jnp.int32)[None, :]).astype(
        jnp.float32
    )
    item_mod = jnp.dot(band_onehot, band_mod, precision=HIGHEST)
    scale_attn = item_mod[:, None, 0:model_width]
    gate_attn = jnp.tanh(item_mod[:, None, model_width : 2 * model_width])
    scale_ffn = item_mod[:, None, 2 * model_width : 3 * model_width]
    gate_ffn = jnp.tanh(item_mod[:, None, 3 * model_width :])
    slot_pos = seq_index * SLOT + jnp.arange(SLOT, dtype=jnp.int32)
    row_pos = (slot_pos[None, :] // item_width[:, None]).astype(jnp.float32)
    col_pos = (slot_pos[None, :] % item_width[:, None]).astype(jnp.float32)
    cosines, sines = rope_angles(row_pos, col_pos, HDIM)
    cosines = cosines[:, :, None]
    sines = sines[:, :, None]
    key_valid = jnp.arange(capacity, dtype=jnp.int32)[None, :] < item_length[:, None]

    def by_heads(array_in, row_count):
        return jnp.moveaxis(array_in.reshape(ITEMS, row_count, local_heads, HDIM), 2, 0)

    text_key_raw = jnp.dot(
        text_states, text_key_weight, preferred_element_type=jnp.float32
    ).reshape(text_rows, local_heads, HDIM)
    text_gain_vec = text_key_gain.reshape(local_heads, HDIM)
    text_key_normed, text_unit, text_inverse = head_norm(text_key_raw, text_gain_vec)
    text_key_low = text_key_normed.reshape(text_rows, local_width).astype(jnp.bfloat16)
    text_value_low = jnp.dot(
        text_states, text_value_weight, preferred_element_type=jnp.float32
    ).astype(jnp.bfloat16)
    text_key_all, text_value_all = (
        lax.all_gather(text_key_low, "seq", axis=0, tiled=True),
        lax.all_gather(text_value_low, "seq", axis=0, tiled=True),
    )
    residual = tokens.astype(jnp.float32).reshape(ITEMS, SLOT, model_width)
    inverse_one = rms_inverse(residual)
    normed_one = residual * inverse_one
    attn_in = (
        (normed_one * attn_gain * (1.0 + scale_attn))
        .astype(jnp.bfloat16)
        .reshape(tok_dev, model_width)
    )
    query_raw = jnp.dot(attn_in, query_weight, preferred_element_type=jnp.float32).reshape(
        head_shape
    )
    key_raw = jnp.dot(attn_in, key_weight, preferred_element_type=jnp.float32).reshape(head_shape)
    value_low = (
        jnp.dot(attn_in, value_weight, preferred_element_type=jnp.float32)
        .astype(jnp.bfloat16)
        .reshape(ITEMS, SLOT, local_width)
    )
    query_gain_vec = query_gain.reshape(local_heads, HDIM)
    key_gain_vec = key_gain.reshape(local_heads, HDIM)
    query_normed, query_unit, query_inverse = head_norm(query_raw, query_gain_vec)
    key_normed, key_unit, key_inverse = head_norm(key_raw, key_gain_vec)
    query_low = rotate(query_normed, cosines, sines).astype(jnp.bfloat16)
    key_low = (
        rotate(key_normed, cosines, sines).astype(jnp.bfloat16).reshape(ITEMS, SLOT, local_width)
    )
    key_all, value_all = (
        lax.all_gather(key_low, "seq", axis=1, tiled=True),
        lax.all_gather(value_low, "seq", axis=1, tiled=True),
    )
    query_heads = jnp.moveaxis(query_low, 2, 0)
    key_heads = by_heads(key_all, capacity)
    value_heads = by_heads(value_all, capacity)
    text_key_heads = by_heads(text_key_all, NTXT)
    text_value_heads = by_heads(text_value_all, NTXT)

    def forward_head(operands):
        query_h, key_h, value_h, tkey_h, tvalue_h = operands
        self_part, self_stat = attend(query_h, key_h, value_h, key_valid)
        cross_part, cross_stat = attend(query_h, tkey_h, tvalue_h, None)
        return (self_part, self_stat, cross_part, cross_stat)

    self_out, self_lse, cross_out, cross_lse = lax.map(
        forward_head, (query_heads, key_heads, value_heads, text_key_heads, text_value_heads)
    )
    cross_tanh = jnp.tanh(cross_gate)
    combined = self_out + cross_tanh[:, None, None, None] * cross_out
    combined_low = jnp.moveaxis(combined, 0, 2).reshape(tok_dev, local_width).astype(jnp.bfloat16)
    attn_branch = head_total(
        jnp.dot(combined_low, out_weight, preferred_element_type=jnp.float32)
    ).reshape(ITEMS, SLOT, model_width)
    middle = residual + gate_attn * attn_branch
    inverse_two = rms_inverse(middle)
    normed_two = middle * inverse_two
    ffn_in = (
        (normed_two * ffn_gain * (1.0 + scale_ffn))
        .astype(jnp.bfloat16)
        .reshape(tok_dev, model_width)
    )
    gate_pre = jnp.dot(ffn_in, gate_weight, preferred_element_type=jnp.float32)
    up_pre = jnp.dot(ffn_in, up_weight, preferred_element_type=jnp.float32)
    gate_sig = jax.nn.sigmoid(gate_pre)
    hidden = (gate_pre * gate_sig * up_pre).astype(jnp.bfloat16)
    ffn_branch = head_total(
        jnp.dot(hidden, down_weight, preferred_element_type=jnp.float32)
    ).reshape(ITEMS, SLOT, model_width)
    layer_sum = middle + gate_ffn * ffn_branch
    block_out = layer_sum.reshape(tok_dev, model_width).astype(jnp.bfloat16)
    incoming = cotangent.astype(jnp.float32).reshape(ITEMS, SLOT, model_width)
    gate_ffn_tok = incoming * ffn_branch
    d_ffn = (gate_ffn * incoming).reshape(tok_dev, model_width).astype(jnp.bfloat16)
    down_grad = jnp.dot(hidden.T, d_ffn, preferred_element_type=jnp.float32)
    d_hidden = jnp.dot(d_ffn, down_weight.T, preferred_element_type=jnp.float32)
    d_gate_pre = (d_hidden * up_pre * gate_sig * (1.0 + gate_pre * (1.0 - gate_sig))).astype(
        jnp.bfloat16
    )
    d_up_pre = (d_hidden * gate_pre * gate_sig).astype(jnp.bfloat16)
    gate_grad = jnp.dot(ffn_in.T, d_gate_pre, preferred_element_type=jnp.float32)
    up_grad = jnp.dot(ffn_in.T, d_up_pre, preferred_element_type=jnp.float32)
    d_ffn_in = feature_total(
        jnp.dot(d_gate_pre, gate_weight.T, preferred_element_type=jnp.float32)
        + jnp.dot(d_up_pre, up_weight.T, preferred_element_type=jnp.float32)
    )
    d_middle_norm, ffn_gain_part, scale_ffn_part = token_norm_back(
        d_ffn_in.reshape(ITEMS, SLOT, model_width), normed_two, inverse_two, ffn_gain, scale_ffn
    )
    d_middle = incoming + d_middle_norm
    gate_attn_tok = d_middle * attn_branch
    d_attn = (gate_attn * d_middle).reshape(tok_dev, model_width).astype(jnp.bfloat16)
    out_grad = jnp.dot(combined_low.T, d_attn, preferred_element_type=jnp.float32)
    d_combined = jnp.moveaxis(
        jnp.dot(d_attn, out_weight.T, preferred_element_type=jnp.float32).reshape(head_shape), 2, 0
    )
    cross_gate_part = jnp.sum(d_combined * cross_out, axis=(1, 2, 3)) * (
        1.0 - cross_tanh * cross_tanh
    )
    d_self = d_combined.astype(jnp.bfloat16)
    d_cross = (d_combined * cross_tanh[:, None, None, None]).astype(jnp.bfloat16)

    def cross_head(operands):
        query_h, tkey_h, tvalue_h, lse_h, dout_h = operands
        d_query, unused_delta, d_key, d_value = attend_back(
            query_h, tkey_h, tvalue_h, None, lse_h, dout_h
        )
        return (d_query, d_key, d_value)

    d_query_cross, d_text_key_heads, d_text_value_heads = lax.map(
        cross_head, (query_heads, text_key_heads, text_value_heads, cross_lse, d_cross)
    )

    def full_head(operands):
        query_h, key_h, value_h, lse_h, dout_h = operands
        d_query, unused_delta, d_key, d_value = attend_back(
            query_h, key_h, value_h, key_valid, lse_h, dout_h
        )
        return (d_query, d_key, d_value)

    d_query_self, d_key_heads, d_value_heads = lax.map(
        full_head, (query_heads, key_heads, value_heads, self_lse, d_self)
    )
    d_key_own, d_value_own = (
        lax.psum_scatter(
            jnp.moveaxis(d_key_heads, 0, 2)
            .reshape(ITEMS, capacity, local_width)
            .astype(jnp.bfloat16),
            "seq",
            scatter_dimension=1,
            tiled=True,
        ).astype(jnp.float32),
        lax.psum_scatter(
            jnp.moveaxis(d_value_heads, 0, 2)
            .reshape(ITEMS, capacity, local_width)
            .astype(jnp.bfloat16),
            "seq",
            scatter_dimension=1,
            tiled=True,
        ).astype(jnp.float32),
    )
    d_key_rot = d_key_own.reshape(head_shape)
    d_query_rot = jnp.moveaxis(d_query_self + d_query_cross, 0, 2)
    d_query_raw, query_gain_part = head_norm_back(
        rotate(d_query_rot, cosines, -sines), query_unit, query_inverse, query_gain_vec
    )
    d_key_raw, key_gain_part = head_norm_back(
        rotate(d_key_rot, cosines, -sines), key_unit, key_inverse, key_gain_vec
    )
    d_query_low = d_query_raw.reshape(tok_dev, local_width).astype(jnp.bfloat16)
    d_key_low = d_key_raw.reshape(tok_dev, local_width).astype(jnp.bfloat16)
    d_value_low = d_value_own.reshape(tok_dev, local_width).astype(jnp.bfloat16)
    query_grad = jnp.dot(attn_in.T, d_query_low, preferred_element_type=jnp.float32)
    key_grad = jnp.dot(attn_in.T, d_key_low, preferred_element_type=jnp.float32)
    value_grad = jnp.dot(attn_in.T, d_value_low, preferred_element_type=jnp.float32)
    d_attn_in = feature_total(
        jnp.dot(d_query_low, query_weight.T, preferred_element_type=jnp.float32)
        + jnp.dot(d_key_low, key_weight.T, preferred_element_type=jnp.float32)
        + jnp.dot(d_value_low, value_weight.T, preferred_element_type=jnp.float32)
    )
    d_input_norm, attn_gain_part, scale_attn_part = token_norm_back(
        d_attn_in.reshape(ITEMS, SLOT, model_width), normed_one, inverse_one, attn_gain, scale_attn
    )
    tokens_grad = (d_middle + d_input_norm).reshape(tok_dev, model_width).astype(jnp.bfloat16)
    d_text_key_own, d_text_value_own = (
        lax.psum_scatter(
            jnp.moveaxis(d_text_key_heads, 0, 2)
            .reshape(ITEMS * NTXT, local_width)
            .astype(jnp.bfloat16),
            "seq",
            scatter_dimension=0,
            tiled=True,
        ).astype(jnp.float32),
        lax.psum_scatter(
            jnp.moveaxis(d_text_value_heads, 0, 2)
            .reshape(ITEMS * NTXT, local_width)
            .astype(jnp.bfloat16),
            "seq",
            scatter_dimension=0,
            tiled=True,
        ).astype(jnp.float32),
    )
    d_text_key_raw, text_gain_part = head_norm_back(
        d_text_key_own.reshape(text_rows, local_heads, HDIM), text_unit, text_inverse, text_gain_vec
    )
    d_text_key_low = d_text_key_raw.reshape(text_rows, local_width).astype(jnp.bfloat16)
    d_text_value_low = d_text_value_own.astype(jnp.bfloat16)
    text_key_grad = jnp.dot(text_states.T, d_text_key_low, preferred_element_type=jnp.float32)
    text_value_grad = jnp.dot(text_states.T, d_text_value_low, preferred_element_type=jnp.float32)
    text_grad = lax.psum_scatter(
        (
            jnp.dot(d_text_key_low, text_key_weight.T, preferred_element_type=jnp.float32)
            + jnp.dot(d_text_value_low, text_value_weight.T, preferred_element_type=jnp.float32)
        ).astype(jnp.bfloat16),
        "tp",
        scatter_dimension=1,
        tiled=True,
    ).astype(jnp.float32)
    gate_attn_item = jnp.sum(gate_attn_tok, axis=1) * (1.0 - gate_attn[:, 0] * gate_attn[:, 0])
    gate_ffn_item = jnp.sum(gate_ffn_tok, axis=1) * (1.0 - gate_ffn[:, 0] * gate_ffn[:, 0])
    item_grad = jnp.concatenate(
        [scale_attn_part, gate_attn_item, scale_ffn_part, gate_ffn_item], axis=1
    )
    band_grad = jnp.dot(band_onehot.T, item_grad, precision=HIGHEST)
    local_band_grad = lax.dynamic_slice_in_dim(band_grad, tp_index * mod_cols, mod_cols, 1)
    ada_grad = jnp.dot(silu_embed.T, local_band_grad, precision=HIGHEST)
    ada_bias_part = jnp.sum(local_band_grad, axis=0)
    summed = (
        lax.psum_scatter(
            query_grad.astype(jnp.bfloat16), "seq", scatter_dimension=0, tiled=True
        ).astype(jnp.float32),
        lax.psum_scatter(
            key_grad.astype(jnp.bfloat16), "seq", scatter_dimension=0, tiled=True
        ).astype(jnp.float32),
        lax.psum_scatter(
            value_grad.astype(jnp.bfloat16), "seq", scatter_dimension=0, tiled=True
        ).astype(jnp.float32),
        lax.psum_scatter(
            gate_grad.astype(jnp.bfloat16), "seq", scatter_dimension=0, tiled=True
        ).astype(jnp.float32),
        lax.psum_scatter(
            up_grad.astype(jnp.bfloat16), "seq", scatter_dimension=0, tiled=True
        ).astype(jnp.float32),
        lax.psum_scatter(
            text_key_grad.astype(jnp.bfloat16), "seq", scatter_dimension=0, tiled=True
        ).astype(jnp.float32),
        lax.psum_scatter(
            text_value_grad.astype(jnp.bfloat16), "seq", scatter_dimension=0, tiled=True
        ).astype(jnp.float32),
        lax.psum_scatter(
            ada_grad.astype(jnp.bfloat16), "seq", scatter_dimension=0, tiled=True
        ).astype(jnp.float32),
        lax.psum_scatter(
            out_grad.astype(jnp.bfloat16), "seq", scatter_dimension=1, tiled=True
        ).astype(jnp.float32),
        lax.psum_scatter(
            down_grad.astype(jnp.bfloat16), "seq", scatter_dimension=1, tiled=True
        ).astype(jnp.float32),
    )
    smalls = lax.psum(
        (
            attn_gain_part,
            ffn_gain_part,
            query_gain_part.reshape(local_width),
            key_gain_part.reshape(local_width),
            text_gain_part.reshape(local_width),
            cross_gate_part,
            ada_bias_part,
        ),
        "seq",
    )
    return (
        block_out,
        tokens_grad,
        text_grad,
        summed[7],
        smalls[6],
        smalls[0],
        smalls[1],
        summed[0],
        summed[1],
        summed[2],
        smalls[2],
        smalls[3],
        smalls[5],
        summed[5],
        summed[6],
        smalls[4],
        summed[8],
        summed[3],
        summed[4],
        summed[9],
    )


MESH_AXES = ("z", "y", "x", "c")
PLANE_AXES = ("y", "x")
PLANE = 4
STRIPS = 4
CORES = 2


def device_pairs(target):
    pairs = []
    for strip in range(STRIPS):
        for place in range(PLANE):
            for core in range(CORES):
                aim = target(strip, place, core)
                pairs.append(
                    (
                        (strip * PLANE + place) * CORES + core,
                        (aim[0] * PLANE + aim[1]) * CORES + aim[2],
                    )
                )
    return pairs


FLIP_CORE = device_pairs(lambda strip, place, core: (strip, place, 1 - core))
FLIP_FIRST = device_pairs(lambda strip, place, core: (strip, place ^ (1 + core), core))
FLIP_SECOND = device_pairs(lambda strip, place, core: (strip, place ^ (2 - core), core))
FLIP_PLACE = {
    mask: device_pairs(lambda strip, place, core, mask=mask: (strip, place ^ mask, core))
    for mask in (1, 2, 3)
}
FLIP_STRIP = {
    mask: device_pairs(lambda strip, place, core, mask=mask: (strip ^ mask, place, core))
    for mask in (1, 2, 3)
}


def move(value, pairs):
    return lax.ppermute(value, MESH_AXES, pairs)


def gather_by(value, table):
    return [value] + [move(value, table[mask]) for mask in (1, 2, 3)]


def after(value, *earlier):
    return lax.optimization_barrier((value, earlier))[0]


def plane_gather(own, beside=()):
    own = jnp.concatenate([own, move(own, FLIP_FIRST)])
    own = jnp.concatenate([own, after(move(own, FLIP_SECOND), beside)])
    return own, move(own, FLIP_CORE)


SCATTER_STEPS = (FLIP_CORE, FLIP_SECOND, FLIP_FIRST)


def core_half(whole):
    half = whole.shape[0] // 2
    arrived = move(whole[half:], FLIP_CORE)
    return whole[:half].astype(jnp.float32) + arrived.astype(jnp.float32)


def plane_scatter(whole, *besides):
    for step, pairs in enumerate(SCATTER_STEPS[-(whole.shape[0] // 256).bit_length() :]):
        half = whole.shape[0] // 2
        arrived = move(whole[half:].astype(jnp.bfloat16), pairs)
        if step < len(besides):
            arrived = after(arrived, besides[step])
        whole = whole[:half].astype(jnp.float32) + arrived.astype(jnp.float32)
    return whole


def pair_sum(four):
    return (four[0] + four[1]) + (four[2] + four[3])


def absolute(relative, index):
    odd = (index & 1) == 1
    high = (index & 2) == 2
    step = [jnp.where(odd, relative[i ^ 1], relative[i]) for i in range(4)]
    return [jnp.where(high, step[i ^ 2], step[i]) for i in range(4)]


def across(value, axes, split, concat):
    return lax.all_to_all(value, axes, split, concat, tiled=True)


def contract(left, right, left_dim, right_dim):
    return lax.dot_general(
        left,
        right,
        (((left_dim,), (right_dim,)), ((), ())),
        preferred_element_type=jnp.float32,
    )


def turn(block, cosine, sine):
    a, b, c, d = block[0:16], block[16:32], block[32:48], block[48:64]
    cr, cc = cosine[0:16], cosine[16:32]
    sr, sc = sine[0:16], sine[16:32]
    return jnp.concatenate(
        [a * cr - b * sr, a * sr + b * cr, c * cc - d * sc, c * sc + d * cc], axis=0
    )


def unit_of(raw):
    inverse = lax.rsqrt(jnp.mean(raw * raw, axis=0, keepdims=True) + EPSILON)
    return raw * inverse, inverse


def unit_back(incoming, unit, inverse, gain):
    lifted = incoming * gain
    gain_part = jnp.sum(incoming * unit, axis=1, keepdims=True)
    raw_part = inverse * (lifted - unit * jnp.mean(lifted * unit, axis=0, keepdims=True))
    return raw_part, gain_part


QBLOCK = 256
VMEM_LIMIT = 56 * 1024 * 1024


def lanes_of(ref):
    return jnp.concatenate([ref[i] for i in range(PLANE)], axis=-1)


def text_of(ref, kind):
    part = ref.shape[-1] // 2
    lanes = slice(kind * part, (kind + 1) * part)
    return jnp.concatenate([ref[i, :, lanes] for i in range(PLANE)], axis=-1)


def attend_kernel(
    spot_ref,
    q_ref,
    k_ref,
    v_ref,
    text_ref,
    norm_ref,
    cos_ref,
    sin_ref,
    valid_ref,
    gate_ref,
    comb_ref,
    self_ref,
    cross_ref,
    qlow_ref,
    klow_ref,
    tlow_ref,
    rinv_ref,
):
    cosine, sine, valid = cos_ref[...], sin_ref[...], valid_ref[...]
    query = turn(unit_of(q_ref[...])[0] * norm_ref[:, 0:1], cosine, sine).astype(jnp.bfloat16)
    key = turn(unit_of(k_ref[...])[0] * norm_ref[:, 1:2], cosine, sine)
    qlow_ref[...] = query
    klow_ref[...] = key.astype(jnp.bfloat16)
    key_rows = key.T.astype(jnp.bfloat16)
    text_key = unit_of(text_of(text_ref, 0))[0] * norm_ref[:, 2:3]
    tlow_ref[...] = text_key.astype(jnp.bfloat16)
    text_rows = text_key.T.astype(jnp.bfloat16)
    value = v_ref[...].astype(jnp.bfloat16).astype(jnp.float32) * valid
    lanes = value.shape[1]
    value_ones = jnp.concatenate(
        [value, jnp.broadcast_to(valid, (16, lanes))], axis=0
    ).astype(jnp.bfloat16)
    tvalue = text_of(text_ref, 1)
    tvalue_ones = jnp.concatenate(
        [tvalue, jnp.ones((16, tvalue.shape[1]), jnp.float32)], axis=0
    ).astype(jnp.bfloat16)
    gate = gate_ref[0:1, 0:1]
    scaled = (query.astype(jnp.float32) * 0.125).astype(jnp.bfloat16)
    for chunk in range(lanes // QBLOCK):
        cols = slice(chunk * QBLOCK, (chunk + 1) * QBLOCK)
        weight = jnp.exp(contract(key_rows, scaled[:, cols], 1, 0)).astype(jnp.bfloat16)
        total = contract(value_ones, weight, 1, 0)
        rinv = 1.0 / total[64:65]
        own = total[:64] * rinv
        tweight = jnp.exp(contract(text_rows, scaled[:, cols], 1, 0)).astype(jnp.bfloat16)
        ttotal = contract(tvalue_ones, tweight, 1, 0)
        trinv = 1.0 / ttotal[64:65]
        text = ttotal[:64] * trinv
        self_ref[:, cols] = own
        cross_ref[:, cols] = text
        rinv_ref[0:1, cols] = rinv
        rinv_ref[1:2, cols] = trinv
        comb_ref[chunk] = (own + gate * text).astype(jnp.bfloat16)


def attend_back_kernel(
    spot_ref,
    q_ref,
    k_ref,
    v_ref,
    text_ref,
    norm_ref,
    cos_ref,
    sin_ref,
    valid_ref,
    gate_ref,
    self_ref,
    cross_ref,
    qlow_ref,
    klow_ref,
    tlow_ref,
    rinv_ref,
    dcomb_ref,
    dqkv_ref,
    dtext_ref,
    gains_ref,
):
    cosine, sine, valid = cos_ref[...], sin_ref[...], valid_ref[...]
    lanes = valid.shape[1]
    gate = gate_ref[0:1, 0:1]
    dcomb = lanes_of(dcomb_ref).astype(jnp.float32)
    cross = cross_ref[...]
    dself = dcomb.astype(jnp.bfloat16)
    dcross = (dcomb * gate).astype(jnp.bfloat16)
    delta = jnp.sum(dself.astype(jnp.float32) * self_ref[...], axis=0, keepdims=True)
    tdelta = jnp.sum(dcross.astype(jnp.float32) * cross, axis=0, keepdims=True)
    gate_part = jnp.sum(
        jnp.sum(dcomb * cross, axis=0, keepdims=True), axis=1, keepdims=True
    ) * (1.0 - gate * gate)
    query = qlow_ref[...]
    scaled = (query.astype(jnp.float32) * 0.125).astype(jnp.bfloat16)
    key = klow_ref[...].astype(jnp.float32)
    key_rows = key.T.astype(jnp.bfloat16)
    key_held = (key * valid * 0.125).astype(jnp.bfloat16)
    value_rows = v_ref[...].T.astype(jnp.bfloat16)
    text_key = tlow_ref[...].astype(jnp.float32)
    text_rows = text_key.T.astype(jnp.bfloat16)
    text_held = (text_key * 0.125).astype(jnp.bfloat16)
    tvalue_rows = text_of(text_ref, 1).T.astype(jnp.bfloat16)
    dkey = dvalue = dtkey = dtvalue = 0.0
    dquery = []
    for start in range(0, lanes, QBLOCK):
        cols = slice(start, start + QBLOCK)
        probs = jnp.exp(contract(key_rows, scaled[:, cols], 1, 0)) * rinv_ref[0:1, cols]
        dprobs = contract(value_rows, dself[:, cols], 1, 0)
        dscore = (probs * (dprobs - delta[:, cols])).astype(jnp.bfloat16)
        dvalue += contract(dself[:, cols], probs.astype(jnp.bfloat16), 1, 1)
        dkey += contract(scaled[:, cols], dscore, 1, 1)
        turned = contract(key_held, dscore, 1, 0)
        tprobs = jnp.exp(contract(text_rows, scaled[:, cols], 1, 0)) * rinv_ref[1:2, cols]
        dtprobs = contract(tvalue_rows, dcross[:, cols], 1, 0)
        dtscore = (tprobs * (dtprobs - tdelta[:, cols])).astype(jnp.bfloat16)
        dtvalue += contract(dcross[:, cols], tprobs.astype(jnp.bfloat16), 1, 1)
        dtkey += contract(scaled[:, cols], dtscore, 1, 1)
        dquery.append(turned + contract(text_held, dtscore, 1, 0))
    dquery = jnp.concatenate(dquery, axis=1)
    unit, inverse = unit_of(q_ref[...])
    draw_q, query_gain = unit_back(turn(dquery, cosine, -sine), unit, inverse, norm_ref[:, 0:1])
    unit, inverse = unit_of(k_ref[...])
    draw_k, key_gain = unit_back(turn(dkey * valid, cosine, -sine), unit, inverse, norm_ref[:, 1:2])
    unit, inverse = unit_of(text_of(text_ref, 0))
    draw_t, text_gain = unit_back(dtkey, unit, inverse, norm_ref[:, 2:3])
    dvalue = dvalue * valid
    for chunk in range(PLANE):
        cols = slice(chunk * QBLOCK, (chunk + 1) * QBLOCK)
        dqkv_ref[chunk, 0:64] = draw_q[:, cols].astype(jnp.bfloat16)
        dqkv_ref[chunk, 64:128] = draw_k[:, cols].astype(jnp.bfloat16)
        dqkv_ref[chunk, 128:192] = dvalue[:, cols].astype(jnp.bfloat16)
        size = draw_t.shape[1] // PLANE
        cols = slice(chunk * size, (chunk + 1) * size)
        dtext_ref[chunk] = jnp.concatenate([draw_t[:, cols], dtvalue[:, cols]], axis=1).astype(
            jnp.bfloat16
        )
    gains_ref[:, 0:128] = jnp.broadcast_to(query_gain, (64, 128))
    gains_ref[:, 128:256] = jnp.broadcast_to(key_gain, (64, 128))
    gains_ref[:, 256:384] = jnp.broadcast_to(text_gain, (64, 128))
    gains_ref[:, 384:512] = jnp.broadcast_to(gate_part, (64, 128))


def head_block(width, offset=0):
    return pl.BlockSpec((HDIM, width), lambda h, s: (h + offset, 0))


def shared_block(rows, width):
    return pl.BlockSpec((rows, width), lambda h, s: (0, 0))


def params():
    return pltpu.CompilerParams(vmem_limit_bytes=VMEM_LIMIT)


def cost(flops, moved):
    return pl.CostEstimate(flops=flops, bytes_accessed=moved, transcendentals=0)


def attention_call(heads, lanes, texts, backward):
    f32, b16 = jnp.float32, jnp.bfloat16
    part = texts // PLANE
    specs = [
        head_block(lanes),
        head_block(lanes, heads),
        head_block(lanes, 2 * heads),
        pl.BlockSpec((PLANE, HDIM, 2 * part), lambda h, s: (0, h, 0)),
        pl.BlockSpec((HDIM, 3), lambda h, s: (s[0] * heads + h, 0)),
        shared_block(32, lanes),
        shared_block(32, lanes),
        shared_block(1, lanes),
        pl.BlockSpec((8, 128), lambda h, s: (s[0] * heads + h, 0)),
    ]
    wide = heads * HDIM
    chunk_spec = pl.BlockSpec((PLANE, HDIM, QBLOCK), lambda h, s: (0, h, 0))
    rinv_spec = pl.BlockSpec((8, lanes), lambda h, s: (h, 0))
    saved = [head_block(lanes)] * 4 + [head_block(texts), rinv_spec]
    shape = jax.ShapeDtypeStruct
    pairs = heads * lanes * (lanes + texts)
    if not backward:
        out_specs = [chunk_spec] + saved
        out_shape = [
            shape((PLANE, wide, lanes // PLANE), b16),
            shape((wide, lanes), f32),
            shape((wide, lanes), f32),
            shape((wide, lanes), b16),
            shape((wide, lanes), b16),
            shape((wide, texts), b16),
            shape((heads * 8, lanes), f32),
        ]
        body, passes = attend_kernel, 2
    else:
        specs = specs + saved + [chunk_spec]
        out_specs = [
            pl.BlockSpec((PLANE, 3 * HDIM, QBLOCK), lambda h, s: (0, h, 0)),
            pl.BlockSpec((PLANE, HDIM, 2 * part), lambda h, s: (0, h, 0)),
            head_block(512),
        ]
        out_shape = [
            shape((PLANE, 3 * wide, lanes // PLANE), b16),
            shape((PLANE, wide, 2 * part), b16),
            shape((wide, 512), f32),
        ]
        body, passes = attend_back_kernel, 5
    return pl.pallas_call(
        body,
        grid_spec=pltpu.PrefetchScalarGridSpec(
            num_scalar_prefetch=1, grid=(heads,), in_specs=specs, out_specs=out_specs
        ),
        out_shape=out_shape,
        compiler_params=params(),
        cost_estimate=cost(8 * pairs * HDIM * passes, 8 * wide * lanes),
    )


def project_kernel(spot_ref, own_ref, other_ref, lift_ref, weight_ref, in_ref, qkv_ref, turned):
    @pl.when(pl.program_id(0) == 0)
    def _():
        turned[...] = weight_ref[...].T

    first = spot_ref[1] == 0
    own, other = own_ref[...].astype(jnp.float32), other_ref[...].astype(jnp.float32)
    values = jnp.concatenate([jnp.where(first, own, other), jnp.where(first, other, own)])
    normed = (values * rms_inverse(values) * lift_ref[...]).astype(jnp.bfloat16)
    in_ref[...] = normed
    qkv_ref[...] = contract(turned[...], normed, 1, 1)


def project(spot, halves, lift, weight):
    rows, width = halves[0].shape
    wide = weight.shape[1]
    block = rows // PLANE
    return pl.pallas_call(
        project_kernel,
        grid_spec=pltpu.PrefetchScalarGridSpec(
            num_scalar_prefetch=1,
            grid=(PLANE,),
            in_specs=[
                pl.BlockSpec((block, width), lambda i, s: (i, 0)),
                pl.BlockSpec((block, width), lambda i, s: (i % 2 * 2 + i // 2, 0)),
                pl.BlockSpec((1, width), lambda i, s: (0, 0)),
                pl.BlockSpec((width, wide), lambda i, s: (0, 0)),
            ],
            out_specs=[
                pl.BlockSpec((2 * block, width), lambda i, s: (s[2 + i] // 2, 0)),
                pl.BlockSpec((wide, 2 * block), lambda i, s: (0, s[2 + i] // 2)),
            ],
            scratch_shapes=[pltpu.VMEM((wide, width), jnp.bfloat16)],
        ),
        out_shape=[
            jax.ShapeDtypeStruct((2 * rows, width), jnp.bfloat16),
            jax.ShapeDtypeStruct((wide, 2 * rows), jnp.float32),
        ],
        compiler_params=params(),
        cost_estimate=cost(4 * rows * width * wide, 16 * rows * width),
    )(spot, *halves, lift, weight)


def ffn_kernel(spot_ref, a_ref, b_ref, d0_ref, d1_ref, gw_ref, uw_ref, dw_ref, h_ref, din_ref):
    early = pl.program_id(0) < 2
    rows_in = jnp.where(early, a_ref[...], b_ref[...])
    d_out = jnp.concatenate([d0_ref[...], d1_ref[...]])
    size = gw_ref.shape[1]
    gate_pre = jnp.dot(rows_in, gw_ref[...], preferred_element_type=jnp.float32)
    up_pre = jnp.dot(rows_in, uw_ref[...], preferred_element_type=jnp.float32)
    d_hidden = contract(d_out, dw_ref[...], 1, 1)
    gate_sig = jax.nn.sigmoid(gate_pre)
    swish = gate_pre * gate_sig
    d_gate = (d_hidden * up_pre * (gate_sig + swish * (1.0 - gate_sig))).astype(jnp.bfloat16)
    d_up = (d_hidden * swish).astype(jnp.bfloat16)
    h_ref[:, 0:size] = d_gate
    h_ref[:, size : 2 * size] = d_up
    h_ref[:, 2 * size : 3 * size] = (swish * up_pre).astype(jnp.bfloat16)
    din_ref[...] = (
        contract(d_gate, gw_ref[...], 1, 1) + contract(d_up, uw_ref[...], 1, 1)
    ).astype(jnp.bfloat16)


def ffn(spot, halves, d_ffn, gate_weight, up_weight, down_weight):
    rows, width = halves[0].shape
    size = gate_weight.shape[1] // PLANE
    block = rows // 2
    early = pl.BlockSpec((block, width), lambda i, s: (jnp.minimum(i, 1), 0))
    late = pl.BlockSpec((block, width), lambda i, s: (jnp.maximum(i - 2, 0), 0))
    col = pl.BlockSpec((width, size), lambda i, s: (0, s[0]))
    return pl.pallas_call(
        ffn_kernel,
        grid_spec=pltpu.PrefetchScalarGridSpec(
            num_scalar_prefetch=1,
            grid=(4,),
            in_specs=[
                early,
                late,
                pl.BlockSpec((block // 2, width), lambda i, s: (s[2 + 2 * i], 0)),
                pl.BlockSpec((block // 2, width), lambda i, s: (s[3 + 2 * i], 0)),
                col,
                col,
                pl.BlockSpec((size, width), lambda i, s: (s[0], 0)),
            ],
            out_specs=[
                pl.BlockSpec((block, 3 * size), lambda i, s: (i, 0)),
                pl.BlockSpec((block, width), lambda i, s: (i, 0)),
            ],
        ),
        out_shape=[
            jax.ShapeDtypeStruct((2 * rows, 3 * size), jnp.bfloat16),
            jax.ShapeDtypeStruct((2 * rows, width), jnp.bfloat16),
        ],
        compiler_params=params(),
        cost_estimate=cost(20 * rows * width * size, 16 * rows * width),
    )(spot, *halves, d_ffn, d_ffn, gate_weight, up_weight, down_weight)


def ffn_grad_kernel(
    spot_ref, a_ref, b_ref, d_ref, inner_ref, hid_ref, dw_ref, grad_ref, out_ref
):
    rows = a_ref.shape[0]
    size = hid_ref.shape[1]
    block = rows // 4
    starts = [pl.multiple_of(spot_ref[2 + i] * block, block) for i in range(8)]
    d_rows = jnp.concatenate([d_ref[pl.ds(start, block), :] for start in starts])
    in_rows = jnp.concatenate([a_ref[...], b_ref[...]])
    hidden = hid_ref[...]
    grad_ref[:, : 2 * size] = contract(in_rows, inner_ref[...], 0, 0).astype(jnp.bfloat16)
    grad_ref[:, 2 * size :] = contract(d_rows, hidden, 0, 0).astype(jnp.bfloat16)
    out_ref[...] = jnp.dot(hidden, dw_ref[...], preferred_element_type=jnp.float32).astype(
        jnp.bfloat16
    )


def ffn_grad(spot, halves, d_ffn, inner, down_weight):
    rows, width = halves[0].shape
    size = inner.shape[1] // 3
    tile = width // 3
    return pl.pallas_call(
        ffn_grad_kernel,
        grid_spec=pltpu.PrefetchScalarGridSpec(
            num_scalar_prefetch=1,
            grid=(3,),
            in_specs=[
                pl.BlockSpec((rows, tile), lambda i, s: (0, i)),
                pl.BlockSpec((rows, tile), lambda i, s: (0, i)),
                pl.BlockSpec((2 * rows, tile), lambda i, s: (0, i)),
                pl.BlockSpec((2 * rows, 2 * size), lambda i, s: (0, 0)),
                pl.BlockSpec((2 * rows, size), lambda i, s: (0, 2)),
                pl.BlockSpec((size, tile), lambda i, s: (s[0], i)),
            ],
            out_specs=[
                pl.BlockSpec((tile, 3 * size), lambda i, s: (i, 0)),
                pl.BlockSpec((2 * rows, tile), lambda i, s: (0, i)),
            ],
        ),
        out_shape=[
            jax.ShapeDtypeStruct((width, 3 * size), jnp.bfloat16),
            jax.ShapeDtypeStruct((2 * rows, width), jnp.bfloat16),
        ],
        compiler_params=params(),
        cost_estimate=cost(16 * rows * width * size, 16 * rows * width),
    )(spot, *halves, d_ffn, inner, inner, down_weight)


def by_kind(block, kind, heads):
    return jnp.concatenate(
        [
            block[i, (3 * h + kind) * HDIM : (3 * h + kind + 1) * HDIM]
            for i in range(block.shape[0])
            for h in range(heads)
        ],
        axis=0,
    )


def input_grad_kernel(d_ref, qw_ref, kw_ref, vw_ref, out_ref):
    heads = d_ref.shape[1] // (3 * HDIM)
    total = 0.0
    for kind, weight in enumerate((qw_ref, kw_ref, vw_ref)):
        total += contract(by_kind(d_ref, kind, heads).T, weight[...], 1, 1)
    out_ref[...] = total


def input_grad(d_qkv, query_weight, key_weight, value_weight):
    width, wide = query_weight.shape
    rows = d_qkv.shape[2]
    tile = width // 3
    weight = pl.BlockSpec((tile, wide), lambda i: (i, 0))
    return pl.pallas_call(
        input_grad_kernel,
        grid=(3,),
        in_specs=[pl.BlockSpec(d_qkv.shape, lambda i: (0, 0, 0)), weight, weight, weight],
        out_specs=pl.BlockSpec((rows, tile), lambda i: (0, i)),
        out_shape=jax.ShapeDtypeStruct((rows, width), jnp.float32),
        compiler_params=params(),
        cost_estimate=cost(6 * rows * width * wide, 6 * width * wide),
    )(d_qkv, query_weight, key_weight, value_weight)


def attn_grad_kernel(spot_ref, in_ref, own_ref, other_ref, d_ref, comb_ref, out_ref):
    places, _, rows = d_ref.shape
    wide = comb_ref.shape[1]
    heads = wide // HDIM
    first = spot_ref[1] == 0
    total = branch = 0.0
    for place in range(places):
        part = slice(place * rows, (place + 1) * rows)
        block = d_ref[place : place + 1]
        ordered = jnp.concatenate([by_kind(block, kind, heads) for kind in range(3)])
        total += contract(in_ref[part].T, ordered, 1, 1)
        own, other = own_ref[place], other_ref[place]
        d_attn = jnp.concatenate([jnp.where(first, own, other), jnp.where(first, other, own)])
        branch += contract(d_attn.T, comb_ref[place], 1, 1)
    out_ref[:, : 3 * wide] = total.astype(jnp.bfloat16)
    out_ref[:, 3 * wide :] = branch.astype(jnp.bfloat16)


def attn_grad(spot, attn_in, own_d_attn, other_d_attn, d_qkv, combined):
    rows, width = attn_in.shape
    wide = combined.shape[1]
    tile = width // 3
    core_rows = pl.BlockSpec(own_d_attn.shape[:2] + (tile,), lambda i, s: (0, 0, i))
    return pl.pallas_call(
        attn_grad_kernel,
        grid_spec=pltpu.PrefetchScalarGridSpec(
            num_scalar_prefetch=1,
            grid=(3,),
            in_specs=[
                pl.BlockSpec((rows, tile), lambda i, s: (0, i)),
                core_rows,
                core_rows,
                pl.BlockSpec(d_qkv.shape, lambda i, s: (0, 0, 0)),
                pl.BlockSpec(combined.shape, lambda i, s: (0, 0, 0)),
            ],
            out_specs=pl.BlockSpec((tile, 4 * wide), lambda i, s: (i, 0)),
        ),
        out_shape=jax.ShapeDtypeStruct((width, 4 * wide), jnp.bfloat16),
        compiler_params=params(),
        cost_estimate=cost(8 * rows * width * wide, 4 * rows * width),
    )(spot, attn_in, own_d_attn, other_d_attn, d_qkv, combined)


def strips_kernel(in_ref, out_ref):
    size = out_ref.shape[2]
    for strip in range(out_ref.shape[0]):
        out_ref[strip] = in_ref[:, strip * size : (strip + 1) * size]


def by_strips(states):
    rows, cols = states.shape
    return pl.pallas_call(
        strips_kernel,
        out_shape=jax.ShapeDtypeStruct((STRIPS, rows, cols // STRIPS), states.dtype),
        compiler_params=params(),
        cost_estimate=cost(0, 4 * rows * cols),
    )(states)


def text_grad_kernel(where_ref, *refs):
    states, d_text, out_ref = refs[:PLANE], refs[PLANE : 2 * PLANE], refs[2 * PLANE]
    own = where_ref[1]
    part = d_text[0].shape[2] // 2
    total = 0.0
    for mask in range(PLANE):
        place = where_ref[0] ^ mask
        blocks = [
            jnp.concatenate([piece[place, :, :part], piece[place, :, part:]]) for piece in d_text
        ]
        rows = [
            states[mask][pl.ds(pl.multiple_of((own ^ strip) * part, part), part), :]
            for strip in range(STRIPS)
        ]
        total += jnp.dot(
            jnp.concatenate(blocks, axis=-1),
            jnp.concatenate(rows),
            preferred_element_type=jnp.float32,
        )
    size = total.shape[1] // PLANE
    for place in range(PLANE):
        out_ref[place] = total[:, place * size : (place + 1) * size].astype(jnp.bfloat16)


def text_weight_grad(where_here, states, strips):
    rows, cols = states[0].shape
    wide = 2 * strips[0].shape[1]
    whole = pl.BlockSpec(memory_space=pltpu.VMEM)
    return pl.pallas_call(
        text_grad_kernel,
        in_specs=[pl.BlockSpec(memory_space=pltpu.SMEM)] + [whole] * 8,
        out_specs=whole,
        out_shape=jax.ShapeDtypeStruct((PLANE, wide, cols // PLANE), jnp.bfloat16),
        compiler_params=params(),
        cost_estimate=cost(8 * rows * cols * wide, 8 * rows * cols),
    )(where_here, *states, *strips)


def split_three(value):
    high = lax.reduce_precision(value, 8, 7)
    middle = lax.reduce_precision(value - high, 8, 7)
    return jnp.concatenate([high, middle, value - high - middle]).astype(jnp.bfloat16)


def strip_shards(
    tokens,
    cotangent,
    step_embed,
    item_band,
    item_length,
    item_width,
    text_states,
    ada_weight,
    ada_bias,
    attn_gain,
    ffn_gain,
    query_weight,
    key_weight,
    value_weight,
    query_gain,
    key_gain,
    cross_gate,
    text_key_weight,
    text_value_weight,
    text_key_gain,
    out_weight,
    gate_weight,
    up_weight,
    down_weight,
):
    f32, b16 = jnp.float32, jnp.bfloat16
    strip = lax.axis_index("z")
    place = lax.axis_index("y") * 2 + lax.axis_index("x")
    core = lax.axis_index("c")
    first_core = core == 0
    spot = [place, core]
    for block in range(2 * PLANE):
        from_core = core ^ (block // PLANE)
        from_place = place
        if block & 1:
            from_place = from_place ^ (1 + from_core)
        if block & 2:
            from_place = from_place ^ (2 - from_core)
        spot.append(from_place * CORES + from_core)
    spot = jnp.stack(spot).astype(jnp.int32)
    width = tokens.shape[1]
    half = SLOT // CORES
    own_rows = STRIPS * half
    lanes = own_rows * PLANE * CORES
    wide = query_weight.shape[1] // PLANE
    heads = wide // HDIM
    hidden_wide = gate_weight.shape[1] // PLANE
    text_own = text_states.shape[0]
    texts = text_own * PLANE

    def both_cores(own, axis=0):
        other = move(own, FLIP_CORE)
        low = jnp.where(first_core, own, other)
        high = jnp.where(first_core, other, own)
        return jnp.concatenate([low, high], axis=axis)

    def core_scatter(partial, axis=0):
        size = partial.shape[axis] // CORES
        sent = lax.dynamic_slice_in_dim(partial, (1 - core) * size, size, axis)
        kept = lax.dynamic_slice_in_dim(partial, core * size, size, axis)
        return kept.astype(f32) + move(sent.astype(b16), FLIP_CORE).astype(f32)

    def to_items(*arrays):
        parts = [
            lax.dynamic_slice_in_dim(a.reshape(ITEMS, SLOT, width), core * half, half, 1)
            for a in arrays
        ]
        parts = across(jnp.concatenate(parts, axis=1), "z", 0, 0)
        parts = parts.reshape(STRIPS, len(arrays), half, width)
        return [parts[:, i].reshape(own_rows, width) for i in range(len(arrays))]

    def from_items(beside, *arrays):
        parts = jnp.concatenate([a.reshape(STRIPS, half, width) for a in arrays], axis=1)
        parts = across(parts, "z", 0, 0)
        other = move(after(parts, beside), FLIP_CORE)
        outs = []
        for i in range(len(arrays)):
            own_part, other_part = (p[:, i * half : (i + 1) * half] for p in (parts, other))
            low = jnp.where(first_core, own_part, other_part)
            high = jnp.where(first_core, other_part, own_part)
            outs.append(jnp.concatenate([low, high], axis=1).reshape(ITEMS * SLOT, width))
        return outs

    own_tokens, incoming_low = to_items(tokens, cotangent)
    text_raw = jnp.concatenate(
        [
            contract(text_key_weight, text_states, 0, 1),
            contract(text_value_weight, text_states, 0, 1).astype(b16).astype(f32),
        ],
        axis=1,
    ).reshape(PLANE, wide, 2 * text_own)
    qkv_weight = jnp.concatenate(
        [
            lax.dynamic_slice_in_dim(weight, place * wide, wide, 1)
            for weight in (query_weight, key_weight, value_weight)
        ],
        axis=1,
    )
    silu_embed = jax.nn.silu(step_embed.astype(f32))
    products = jnp.dot(split_three(silu_embed), ada_weight, preferred_element_type=f32)
    local_mod = products[0:4] + products[4:8] + products[8:12] + ada_bias
    own_tokens = after(own_tokens, text_raw, qkv_weight, local_mod)
    pair = jnp.concatenate([own_tokens, move(own_tokens, FLIP_FIRST)])
    pair_arrived = move(pair, FLIP_SECOND)
    text_raw = across(after(text_raw, pair), PLANE_AXES, 0, 0)

    other_mod = move(after(local_mod, own_tokens), FLIP_CORE)
    low_mod = jnp.where(first_core, local_mod, other_mod)
    high_mod = jnp.where(first_core, other_mod, local_mod)

    item_ids = jnp.arange(ITEMS, dtype=jnp.int32)
    band_mask = (item_band[:, None] == item_ids[None, :]).astype(f32)
    own_mask = jnp.sum(jnp.where(item_ids[:, None] == strip, band_mask, 0.0), axis=0)

    own_low = jnp.sum(own_mask[:, None] * low_mod, axis=0)
    own_high = jnp.sum(own_mask[:, None] * high_mod, axis=0)
    scale_attn, scale_ffn = own_low[:width], own_high[:width]
    lift_attn = attn_gain * (1.0 + scale_attn)
    lift_ffn = ffn_gain * (1.0 + scale_ffn)
    gate_attn = jnp.tanh(own_low[width:])
    gate_ffn = jnp.tanh(own_high[width:])

    lane = jnp.arange(lanes, dtype=jnp.int32)
    from_place = lane // (own_rows * CORES)
    from_core = (lane // own_rows) % CORES
    from_strip = (lane % own_rows) // half
    position = (from_strip * PLANE + from_place) * SLOT + from_core * half + lane % half
    chosen = jnp.where(item_ids[:, None] == strip, 1, 0)
    width_here = jnp.sum(chosen * after(item_width, pair)[:, None], axis=0)
    length_here = jnp.sum(chosen * item_length[:, None], axis=0)
    grid_row = (position // width_here).astype(f32)
    grid_col = (position % width_here).astype(f32)
    quarter = HDIM // 4
    frequency = ROPE_BASE ** (-jnp.arange(quarter, dtype=f32) / quarter)
    angles = jnp.concatenate(
        [frequency[:, None] * grid_row[None, :], frequency[:, None] * grid_col[None, :]]
    )
    cosine, sine = jnp.cos(angles), jnp.sin(angles)
    valid = (position < length_here).astype(f32)[None, :]

    norm_gains = jnp.stack([query_gain, key_gain, text_key_gain], axis=1)
    gate_tiles = jnp.broadcast_to(jnp.tanh(cross_gate)[:, None, None], (cross_gate.shape[0], 8, 128))
    gate_tiles = gate_tiles.reshape(-1, 128)

    low_half = jnp.concatenate(
        [pair, after(pair_arrived, lift_attn, text_raw, cosine, sine, norm_gains, gate_tiles)]
    )
    incoming = after(incoming_low, pair).astype(f32)
    own_d_ffn = (gate_ffn * incoming).astype(b16)
    high_half = after(move(low_half, FLIP_CORE), own_d_ffn)
    d_ffn = lax.all_gather(after(own_d_ffn, low_half), PLANE_AXES + ("c",), axis=0, tiled=True)
    attn_in, qkv = project(spot, (low_half, high_half), lift_attn[None, :], qkv_weight)
    common = (
        spot,
        qkv,
        qkv,
        qkv,
        text_raw,
        norm_gains,
        cosine,
        sine,
        valid,
        gate_tiles,
    )
    combined, *saved = attention_call(heads, lanes, texts, False)(*common)
    chip_combined = across(combined, PLANE_AXES, 0, 0).reshape(-1, own_rows * CORES)
    attn_branch = core_scatter(contract(chip_combined, out_weight, 0, 0))

    residual = own_tokens.astype(f32)
    middle = residual + gate_attn * attn_branch
    inverse_two = rms_inverse(middle)
    normed_two = middle * inverse_two
    own_ffn_in = (normed_two * lift_ffn).astype(b16)
    own_ffn_in = after(own_ffn_in, d_ffn)
    states_wide = text_states.shape[1] // STRIPS
    states = by_strips(after(text_states, own_ffn_in))
    states = across(states, "z", 0, 0).reshape(texts, states_wide)
    ffn_in = plane_gather(own_ffn_in, (states,))
    inner, d_ffn_in = ffn(spot, ffn_in, d_ffn, gate_weight, up_weight, down_weight)
    ffn_grads, ffn_branch = ffn_grad(spot, ffn_in, d_ffn, inner, down_weight)
    branch_half = core_half(ffn_branch)
    d_ffn_in = plane_scatter(d_ffn_in, (ffn_grads,), (branch_half,))
    d_normed = d_ffn_in * normed_two
    u_ffn = jnp.sum(d_normed, axis=0)
    d_middle = incoming + inverse_two * (
        d_ffn_in * lift_ffn
        - normed_two * jnp.mean(d_normed * lift_ffn, axis=-1, keepdims=True)
    )
    w_attn = jnp.sum(d_middle * attn_branch, axis=0) * (1.0 - gate_attn * gate_attn)
    own_d_attn = (gate_attn * d_middle).astype(b16)
    d_attn = both_cores(own_d_attn)

    d_comb = contract(out_weight, d_attn, 1, 1).astype(b16).reshape(PLANE, wide, -1)
    d_comb = across(d_comb, PLANE_AXES, 0, 0)
    d_qkv, d_text, gains = attention_call(heads, lanes, texts, True)(*common, *saved, d_comb)
    own_rows_d = jnp.broadcast_to(after(own_d_attn, d_comb), (PLANE, own_rows, width))
    own_rows_d = across(own_rows_d, PLANE_AXES, 0, 0)
    own_rows_d = after(own_rows_d, d_qkv)
    attn_grads = attn_grad(spot, attn_in, own_rows_d, move(own_rows_d, FLIP_CORE), d_qkv, combined)
    chip_d_qkv = after(across(d_qkv, PLANE_AXES, 0, 0), attn_grads)
    ffn_branch = plane_scatter(after(branch_half, chip_d_qkv))
    d_attn_in = core_scatter(input_grad(chip_d_qkv, query_weight, key_weight, value_weight))
    inverse_one = rms_inverse(residual)
    normed_one = residual * inverse_one
    d_normed = d_attn_in * normed_one
    u_attn = jnp.sum(d_normed, axis=0)
    tokens_grad = d_middle + inverse_one * (
        d_attn_in * lift_attn
        - normed_one * jnp.mean(d_normed * lift_attn, axis=-1, keepdims=True)
    )

    w_ffn = jnp.sum(incoming * ffn_branch, axis=0) * (1.0 - gate_ffn * gate_ffn)
    block_out = (middle + gate_ffn * ffn_branch).astype(b16)

    def spread(own):
        blocks = own.reshape(PLANE, own.shape[0] // PLANE, own.shape[1])
        return across(blocks, PLANE_AXES, 0, 0)

    def sheet(blocks, start, size):
        return jnp.concatenate(
            [blocks[i, :, start : start + size] for i in range(PLANE)], axis=1
        ).astype(f32)

    ffn_own = lax.psum_scatter(ffn_grads, "z", scatter_dimension=0, tiled=True)
    d_text_all = gather_by(d_text, FLIP_STRIP)
    attn_grads = lax.psum_scatter(after(attn_grads, ffn_own, d_text_all), "z", scatter_dimension=0, tiled=True)
    ffn_blocks = spread(ffn_own)
    attn_blocks = spread(attn_grads)
    block_out, tokens_grad = from_items(ffn_blocks, block_out, tokens_grad.astype(b16))
    gate_grad = sheet(ffn_blocks, 0, hidden_wide)
    up_grad = sheet(ffn_blocks, hidden_wide, hidden_wide)
    down_grad = sheet(ffn_blocks, 2 * hidden_wide, hidden_wide).T
    out_grad = sheet(attn_blocks, 3 * wide, wide).T
    query_grad = sheet(attn_blocks, 0, wide)
    key_grad = sheet(attn_blocks, wide, wide)
    value_grad = sheet(attn_blocks, 2 * wide, wide)

    back = across(after(d_text, chip_d_qkv), PLANE_AXES, 0, 0)
    back = after(back, attn_grads).reshape(-1, 2 * text_own)
    back = [back[:, :text_own], back[:, text_own:]]
    text_grad = core_scatter(
        contract(back[0], text_key_weight, 0, 1) + contract(back[1], text_value_weight, 0, 1), 1
    )
    states = gather_by(after(states, d_qkv), FLIP_PLACE)
    where_here = jnp.stack([place, strip]).astype(jnp.int32)
    states[0] = after(states[0], ffn_blocks)
    text_sum = text_weight_grad(where_here, states, d_text_all)
    text_blocks = across(text_sum, PLANE_AXES, 0, 0)
    text_key_grad = text_blocks[:, :wide].reshape(PLANE * wide, -1).T.astype(f32)
    text_value_grad = text_blocks[:, wide:].reshape(PLANE * wide, -1).T.astype(f32)

    own_sums = jnp.concatenate([u_attn, u_ffn, w_ffn, w_attn])
    own_sums = own_sums + move(own_sums, FLIP_CORE)
    count = own_sums.shape[0]
    parts = jnp.concatenate(
        [own_sums, gains[:, 0], gains[:, 128], gains[:, 256], gains[:, 384]]
    )
    parts = gather_by(parts, FLIP_PLACE)
    head_parts = absolute([p[count:].reshape(4, wide) for p in parts], place)
    parts = jnp.concatenate(
        [pair_sum([p[:count] for p in parts]), jnp.concatenate(head_parts, axis=1).reshape(-1)]
    )
    parts = gather_by(after(parts, attn_grads), FLIP_STRIP)
    head_parts = pair_sum([p[count:] for p in parts]).reshape(4, PLANE * wide)
    sums = [p[:count].reshape(4, width) for p in absolute(parts, strip)]
    items = []
    for item in range(ITEMS):
        low_part = jnp.concatenate([attn_gain * sums[item][0], sums[item][3]])
        high_part = jnp.concatenate([ffn_gain * sums[item][1], sums[item][2]])
        items.append(jnp.where(first_core, low_part, high_part))
    ada_bias_grad = pair_sum(items)
    def by_item(table):
        return jnp.sum(band_mask[:, :, None] * table[None], axis=1)

    scales = by_item(low_mod[:, :width]), by_item(high_mod[:, :width])
    attn_gain_grad = pair_sum([sums[i][0] * (1.0 + scales[0][i]) for i in range(ITEMS)])
    ffn_gain_grad = pair_sum([sums[i][1] * (1.0 + scales[1][i]) for i in range(ITEMS)])
    ada_rows = silu_embed.shape[1] // (STRIPS * PLANE)
    silu_own = lax.dynamic_slice_in_dim(
        silu_embed, (strip * PLANE + place) * ada_rows, ada_rows, 1
    )
    ada_grad = lax.dot_general(
        by_item(silu_own), jnp.stack(items), (((0,), (0,)), ((), ())), precision=HIGHEST
    )
    return (
        block_out,
        tokens_grad,
        text_grad,
        ada_grad,
        ada_bias_grad,
        attn_gain_grad,
        ffn_gain_grad,
        query_grad,
        key_grad,
        value_grad,
        head_parts[0],
        head_parts[1],
        head_parts[3].reshape(-1, HDIM)[:, 0],
        text_key_grad,
        text_value_grad,
        head_parts[2],
        out_grad,
        gate_grad,
        up_grad,
        down_grad,
    )


def placements(seq, tp):
    ins = (
        P(seq, None),
        P(seq, None),
        P(),
        P(),
        P(),
        P(),
        P(seq, None),
        P(None, tp),
        P(tp),
        P(),
        P(),
        P(None, tp),
        P(None, tp),
        P(None, tp),
        P(tp),
        P(tp),
        P(tp),
        P(None, tp),
        P(None, tp),
        P(tp),
        P(tp, None),
        P(None, tp),
        P(None, tp),
        P(tp, None),
    )
    outs = (
        P(seq, None),
        P(seq, None),
        P(seq, tp),
        P(seq, tp),
        P(tp),
        P(),
        P(),
        P(seq, tp),
        P(seq, tp),
        P(seq, tp),
        P(tp),
        P(tp),
        P(tp),
        P(seq, tp),
        P(seq, tp),
        P(tp),
        P(tp, seq),
        P(seq, tp),
        P(seq, tp),
        P(tp, seq),
    )
    return ins, outs


def solution(mesh):
    if mesh.shape["seq"] == STRIPS * PLANE and mesh.shape["tp"] == CORES:
        body, seq, tp = strip_shards, ("z", "y", "x"), "c"
        mesh = Mesh(mesh.devices.reshape(STRIPS, 2, 2, CORES), MESH_AXES)
    else:
        body, seq, tp = shards, "seq", "tp"
    ins, outs = placements(seq, tp)
    return jax.shard_map(body, mesh=mesh, in_specs=ins, out_specs=outs, check_vma=False)
```

```python
import jax
import jax.numpy as jnp
from jax import lax
from jax.experimental import pallas as pl
from jax.experimental.pallas import tpu as pltpu
from jax.sharding import Mesh
from jax.sharding import PartitionSpec as P

HDIM = 64
NTXT = 256
BANDS = 4
ITEMS = 4
SLOT = 64


EPSILON = 1e-06
ROPE_BASE = 10000.0
HIGHEST = lax.Precision.HIGHEST
NEG_FILL = -1e30


def rms_inverse(values):
    return lax.rsqrt(jnp.mean(values * values, axis=-1, keepdims=True) + EPSILON)


def rope_angles(row_pos, col_pos, head_dim):
    quarter = head_dim // 4
    frequency = ROPE_BASE ** (-jnp.arange(quarter, dtype=jnp.float32) / quarter)
    angles = jnp.stack([row_pos[..., None] * frequency, col_pos[..., None] * frequency], axis=-2)
    return (jnp.cos(angles), jnp.sin(angles))


def rotate(vectors, cosines, sines):
    shape_all = vectors.shape
    paired = vectors.reshape(shape_all[:-1] + (2, 2, shape_all[-1] // 4))
    former = paired[..., 0, :]
    latter = paired[..., 1, :]
    turned = jnp.stack(
        [former * cosines - latter * sines, former * sines + latter * cosines], axis=-2
    )
    return turned.reshape(shape_all)


def head_norm(raw_vals, gain_vec):
    inverse = rms_inverse(raw_vals)
    unit_vec = raw_vals * inverse
    return (unit_vec * gain_vec, unit_vec, inverse)


def head_norm_back(incoming, unit_vec, inverse, gain_vec):
    grad_unit = incoming * gain_vec
    gain_part = jnp.sum(incoming * unit_vec, axis=tuple(range(incoming.ndim - 2)))
    grad_raw = inverse * (
        grad_unit - unit_vec * jnp.mean(grad_unit * unit_vec, axis=-1, keepdims=True)
    )
    return (grad_raw, gain_part)


def token_norm_back(incoming, normed, inverse, gain_vec, scale_mod):
    lifted = 1.0 + scale_mod
    gain_part = jnp.sum(incoming * normed * lifted, axis=(0, 1))
    scale_part = jnp.sum(incoming * normed * gain_vec, axis=1)
    grad_normed = incoming * gain_vec * lifted
    grad_in = inverse * (
        grad_normed - normed * jnp.mean(grad_normed * normed, axis=-1, keepdims=True)
    )
    return (grad_in, gain_part, scale_part)


def attend(query_h, key_h, value_h, key_valid):
    scaling = query_h.shape[-1] ** (-0.5)
    scores = (
        jnp.einsum("isd,ikd->isk", query_h, key_h, preferred_element_type=jnp.float32) * scaling
    )
    if key_valid is not None:
        scores = jnp.where(key_valid[:, None, :], scores, NEG_FILL)
    row_max = jnp.max(scores, axis=-1, keepdims=True)
    exp_scores = jnp.exp(scores - row_max)
    row_total = jnp.sum(exp_scores, axis=-1, keepdims=True)
    probability = (exp_scores / row_total).astype(jnp.bfloat16)
    output = jnp.einsum("isk,ikd->isd", probability, value_h, preferred_element_type=jnp.float32)
    return (output, (row_max + jnp.log(row_total))[..., 0])


def attend_back(query_h, key_h, value_h, key_valid, lse_h, dout_h):
    scaling = query_h.shape[-1] ** (-0.5)
    scores = (
        jnp.einsum("isd,ikd->isk", query_h, key_h, preferred_element_type=jnp.float32) * scaling
    )
    if key_valid is not None:
        scores = jnp.where(key_valid[:, None, :], scores, NEG_FILL)
    probability = jnp.exp(scores - lse_h[..., None])
    d_prob = jnp.einsum("isd,ikd->isk", dout_h, value_h, preferred_element_type=jnp.float32)
    delta_row = jnp.sum(d_prob * probability, axis=-1)
    d_score = (probability * (d_prob - delta_row[..., None])).astype(jnp.bfloat16)
    d_query = (
        jnp.einsum("isk,ikd->isd", d_score, key_h, preferred_element_type=jnp.float32) * scaling
    )
    d_key = (
        jnp.einsum("isk,isd->ikd", d_score, query_h, preferred_element_type=jnp.float32) * scaling
    )
    d_value = jnp.einsum(
        "isk,isd->ikd", probability.astype(jnp.bfloat16), dout_h, preferred_element_type=jnp.float32
    )
    return (d_query, delta_row, d_key, d_value)


def head_total(partial_value):
    return lax.psum(partial_value.astype(jnp.bfloat16), "tp").astype(jnp.float32)


def feature_total(partial_value):
    return lax.psum(partial_value.astype(jnp.bfloat16), "tp").astype(jnp.float32)


def shards(
    tokens,
    cotangent,
    step_embed,
    item_band,
    item_length,
    item_width,
    text_states,
    ada_weight,
    ada_bias,
    attn_gain,
    ffn_gain,
    query_weight,
    key_weight,
    value_weight,
    query_gain,
    key_gain,
    cross_gate,
    text_key_weight,
    text_value_weight,
    text_key_gain,
    out_weight,
    gate_weight,
    up_weight,
    down_weight,
):
    seq_count = lax.axis_size("seq")
    seq_index = lax.axis_index("seq")
    tp_index = lax.axis_index("tp")
    tok_dev, model_width = tokens.shape
    local_width = query_weight.shape[1]
    local_heads = local_width // HDIM
    capacity = SLOT * seq_count
    text_rows = text_states.shape[0]
    mod_cols = ada_weight.shape[1]
    head_shape = (ITEMS, SLOT, local_heads, HDIM)
    silu_embed = jax.nn.silu(step_embed.astype(jnp.float32))
    local_mod = jnp.dot(silu_embed, ada_weight.astype(jnp.float32), precision=HIGHEST) + ada_bias
    band_mod = lax.all_gather(local_mod, "tp", axis=1, tiled=True)
    band_onehot = (item_band[:, None] == jnp.arange(BANDS, dtype=jnp.int32)[None, :]).astype(
        jnp.float32
    )
    item_mod = jnp.dot(band_onehot, band_mod, precision=HIGHEST)
    scale_attn = item_mod[:, None, 0:model_width]
    gate_attn = jnp.tanh(item_mod[:, None, model_width : 2 * model_width])
    scale_ffn = item_mod[:, None, 2 * model_width : 3 * model_width]
    gate_ffn = jnp.tanh(item_mod[:, None, 3 * model_width :])
    slot_pos = seq_index * SLOT + jnp.arange(SLOT, dtype=jnp.int32)
    row_pos = (slot_pos[None, :] // item_width[:, None]).astype(jnp.float32)
    col_pos = (slot_pos[None, :] % item_width[:, None]).astype(jnp.float32)
    cosines, sines = rope_angles(row_pos, col_pos, HDIM)
    cosines = cosines[:, :, None]
    sines = sines[:, :, None]
    key_valid = jnp.arange(capacity, dtype=jnp.int32)[None, :] < item_length[:, None]

    def by_heads(array_in, row_count):
        return jnp.moveaxis(array_in.reshape(ITEMS, row_count, local_heads, HDIM), 2, 0)

    text_key_raw = jnp.dot(
        text_states, text_key_weight, preferred_element_type=jnp.float32
    ).reshape(text_rows, local_heads, HDIM)
    text_gain_vec = text_key_gain.reshape(local_heads, HDIM)
    text_key_normed, text_unit, text_inverse = head_norm(text_key_raw, text_gain_vec)
    text_key_low = text_key_normed.reshape(text_rows, local_width).astype(jnp.bfloat16)
    text_value_low = jnp.dot(
        text_states, text_value_weight, preferred_element_type=jnp.float32
    ).astype(jnp.bfloat16)
    text_key_all, text_value_all = (
        lax.all_gather(text_key_low, "seq", axis=0, tiled=True),
        lax.all_gather(text_value_low, "seq", axis=0, tiled=True),
    )
    residual = tokens.astype(jnp.float32).reshape(ITEMS, SLOT, model_width)
    inverse_one = rms_inverse(residual)
    normed_one = residual * inverse_one
    attn_in = (
        (normed_one * attn_gain * (1.0 + scale_attn))
        .astype(jnp.bfloat16)
        .reshape(tok_dev, model_width)
    )
    query_raw = jnp.dot(attn_in, query_weight, preferred_element_type=jnp.float32).reshape(
        head_shape
    )
    key_raw = jnp.dot(attn_in, key_weight, preferred_element_type=jnp.float32).reshape(head_shape)
    value_low = (
        jnp.dot(attn_in, value_weight, preferred_element_type=jnp.float32)
        .astype(jnp.bfloat16)
        .reshape(ITEMS, SLOT, local_width)
    )
    query_gain_vec = query_gain.reshape(local_heads, HDIM)
    key_gain_vec = key_gain.reshape(local_heads, HDIM)
    query_normed, query_unit, query_inverse = head_norm(query_raw, query_gain_vec)
    key_normed, key_unit, key_inverse = head_norm(key_raw, key_gain_vec)
    query_low = rotate(query_normed, cosines, sines).astype(jnp.bfloat16)
    key_low = (
        rotate(key_normed, cosines, sines).astype(jnp.bfloat16).reshape(ITEMS, SLOT, local_width)
    )
    key_all, value_all = (
        lax.all_gather(key_low, "seq", axis=1, tiled=True),
        lax.all_gather(value_low, "seq", axis=1, tiled=True),
    )
    query_heads = jnp.moveaxis(query_low, 2, 0)
    key_heads = by_heads(key_all, capacity)
    value_heads = by_heads(value_all, capacity)
    text_key_heads = by_heads(text_key_all, NTXT)
    text_value_heads = by_heads(text_value_all, NTXT)

    def forward_head(operands):
        query_h, key_h, value_h, tkey_h, tvalue_h = operands
        self_part, self_stat = attend(query_h, key_h, value_h, key_valid)
        cross_part, cross_stat = attend(query_h, tkey_h, tvalue_h, None)
        return (self_part, self_stat, cross_part, cross_stat)

    self_out, self_lse, cross_out, cross_lse = lax.map(
        forward_head, (query_heads, key_heads, value_heads, text_key_heads, text_value_heads)
    )
    cross_tanh = jnp.tanh(cross_gate)
    combined = self_out + cross_tanh[:, None, None, None] * cross_out
    combined_low = jnp.moveaxis(combined, 0, 2).reshape(tok_dev, local_width).astype(jnp.bfloat16)
    attn_branch = head_total(
        jnp.dot(combined_low, out_weight, preferred_element_type=jnp.float32)
    ).reshape(ITEMS, SLOT, model_width)
    middle = residual + gate_attn * attn_branch
    inverse_two = rms_inverse(middle)
    normed_two = middle * inverse_two
    ffn_in = (
        (normed_two * ffn_gain * (1.0 + scale_ffn))
        .astype(jnp.bfloat16)
        .reshape(tok_dev, model_width)
    )
    gate_pre = jnp.dot(ffn_in, gate_weight, preferred_element_type=jnp.float32)
    up_pre = jnp.dot(ffn_in, up_weight, preferred_element_type=jnp.float32)
    gate_sig = jax.nn.sigmoid(gate_pre)
    hidden = (gate_pre * gate_sig * up_pre).astype(jnp.bfloat16)
    ffn_branch = head_total(
        jnp.dot(hidden, down_weight, preferred_element_type=jnp.float32)
    ).reshape(ITEMS, SLOT, model_width)
    layer_sum = middle + gate_ffn * ffn_branch
    block_out = layer_sum.reshape(tok_dev, model_width).astype(jnp.bfloat16)
    incoming = cotangent.astype(jnp.float32).reshape(ITEMS, SLOT, model_width)
    gate_ffn_tok = incoming * ffn_branch
    d_ffn = (gate_ffn * incoming).reshape(tok_dev, model_width).astype(jnp.bfloat16)
    down_grad = jnp.dot(hidden.T, d_ffn, preferred_element_type=jnp.float32)
    d_hidden = jnp.dot(d_ffn, down_weight.T, preferred_element_type=jnp.float32)
    d_gate_pre = (d_hidden * up_pre * gate_sig * (1.0 + gate_pre * (1.0 - gate_sig))).astype(
        jnp.bfloat16
    )
    d_up_pre = (d_hidden * gate_pre * gate_sig).astype(jnp.bfloat16)
    gate_grad = jnp.dot(ffn_in.T, d_gate_pre, preferred_element_type=jnp.float32)
    up_grad = jnp.dot(ffn_in.T, d_up_pre, preferred_element_type=jnp.float32)
    d_ffn_in = feature_total(
        jnp.dot(d_gate_pre, gate_weight.T, preferred_element_type=jnp.float32)
        + jnp.dot(d_up_pre, up_weight.T, preferred_element_type=jnp.float32)
    )
    d_middle_norm, ffn_gain_part, scale_ffn_part = token_norm_back(
        d_ffn_in.reshape(ITEMS, SLOT, model_width), normed_two, inverse_two, ffn_gain, scale_ffn
    )
    d_middle = incoming + d_middle_norm
    gate_attn_tok = d_middle * attn_branch
    d_attn = (gate_attn * d_middle).reshape(tok_dev, model_width).astype(jnp.bfloat16)
    out_grad = jnp.dot(combined_low.T, d_attn, preferred_element_type=jnp.float32)
    d_combined = jnp.moveaxis(
        jnp.dot(d_attn, out_weight.T, preferred_element_type=jnp.float32).reshape(head_shape), 2, 0
    )
    cross_gate_part = jnp.sum(d_combined * cross_out, axis=(1, 2, 3)) * (
        1.0 - cross_tanh * cross_tanh
    )
    d_self = d_combined.astype(jnp.bfloat16)
    d_cross = (d_combined * cross_tanh[:, None, None, None]).astype(jnp.bfloat16)

    def cross_head(operands):
        query_h, tkey_h, tvalue_h, lse_h, dout_h = operands
        d_query, unused_delta, d_key, d_value = attend_back(
            query_h, tkey_h, tvalue_h, None, lse_h, dout_h
        )
        return (d_query, d_key, d_value)

    d_query_cross, d_text_key_heads, d_text_value_heads = lax.map(
        cross_head, (query_heads, text_key_heads, text_value_heads, cross_lse, d_cross)
    )

    def full_head(operands):
        query_h, key_h, value_h, lse_h, dout_h = operands
        d_query, unused_delta, d_key, d_value = attend_back(
            query_h, key_h, value_h, key_valid, lse_h, dout_h
        )
        return (d_query, d_key, d_value)

    d_query_self, d_key_heads, d_value_heads = lax.map(
        full_head, (query_heads, key_heads, value_heads, self_lse, d_self)
    )
    d_key_own, d_value_own = (
        lax.psum_scatter(
            jnp.moveaxis(d_key_heads, 0, 2)
            .reshape(ITEMS, capacity, local_width)
            .astype(jnp.bfloat16),
            "seq",
            scatter_dimension=1,
            tiled=True,
        ).astype(jnp.float32),
        lax.psum_scatter(
            jnp.moveaxis(d_value_heads, 0, 2)
            .reshape(ITEMS, capacity, local_width)
            .astype(jnp.bfloat16),
            "seq",
            scatter_dimension=1,
            tiled=True,
        ).astype(jnp.float32),
    )
    d_key_rot = d_key_own.reshape(head_shape)
    d_query_rot = jnp.moveaxis(d_query_self + d_query_cross, 0, 2)
    d_query_raw, query_gain_part = head_norm_back(
        rotate(d_query_rot, cosines, -sines), query_unit, query_inverse, query_gain_vec
    )
    d_key_raw, key_gain_part = head_norm_back(
        rotate(d_key_rot, cosines, -sines), key_unit, key_inverse, key_gain_vec
    )
    d_query_low = d_query_raw.reshape(tok_dev, local_width).astype(jnp.bfloat16)
    d_key_low = d_key_raw.reshape(tok_dev, local_width).astype(jnp.bfloat16)
    d_value_low = d_value_own.reshape(tok_dev, local_width).astype(jnp.bfloat16)
    query_grad = jnp.dot(attn_in.T, d_query_low, preferred_element_type=jnp.float32)
    key_grad = jnp.dot(attn_in.T, d_key_low, preferred_element_type=jnp.float32)
    value_grad = jnp.dot(attn_in.T, d_value_low, preferred_element_type=jnp.float32)
    d_attn_in = feature_total(
        jnp.dot(d_query_low, query_weight.T, preferred_element_type=jnp.float32)
        + jnp.dot(d_key_low, key_weight.T, preferred_element_type=jnp.float32)
        + jnp.dot(d_value_low, value_weight.T, preferred_element_type=jnp.float32)
    )
    d_input_norm, attn_gain_part, scale_attn_part = token_norm_back(
        d_attn_in.reshape(ITEMS, SLOT, model_width), normed_one, inverse_one, attn_gain, scale_attn
    )
    tokens_grad = (d_middle + d_input_norm).reshape(tok_dev, model_width).astype(jnp.bfloat16)
    d_text_key_own, d_text_value_own = (
        lax.psum_scatter(
            jnp.moveaxis(d_text_key_heads, 0, 2)
            .reshape(ITEMS * NTXT, local_width)
            .astype(jnp.bfloat16),
            "seq",
            scatter_dimension=0,
            tiled=True,
        ).astype(jnp.float32),
        lax.psum_scatter(
            jnp.moveaxis(d_text_value_heads, 0, 2)
            .reshape(ITEMS * NTXT, local_width)
            .astype(jnp.bfloat16),
            "seq",
            scatter_dimension=0,
            tiled=True,
        ).astype(jnp.float32),
    )
    d_text_key_raw, text_gain_part = head_norm_back(
        d_text_key_own.reshape(text_rows, local_heads, HDIM), text_unit, text_inverse, text_gain_vec
    )
    d_text_key_low = d_text_key_raw.reshape(text_rows, local_width).astype(jnp.bfloat16)
    d_text_value_low = d_text_value_own.astype(jnp.bfloat16)
    text_key_grad = jnp.dot(text_states.T, d_text_key_low, preferred_element_type=jnp.float32)
    text_value_grad = jnp.dot(text_states.T, d_text_value_low, preferred_element_type=jnp.float32)
    text_grad = lax.psum_scatter(
        (
            jnp.dot(d_text_key_low, text_key_weight.T, preferred_element_type=jnp.float32)
            + jnp.dot(d_text_value_low, text_value_weight.T, preferred_element_type=jnp.float32)
        ).astype(jnp.bfloat16),
        "tp",
        scatter_dimension=1,
        tiled=True,
    ).astype(jnp.float32)
    gate_attn_item = jnp.sum(gate_attn_tok, axis=1) * (1.0 - gate_attn[:, 0] * gate_attn[:, 0])
    gate_ffn_item = jnp.sum(gate_ffn_tok, axis=1) * (1.0 - gate_ffn[:, 0] * gate_ffn[:, 0])
    item_grad = jnp.concatenate(
        [scale_attn_part, gate_attn_item, scale_ffn_part, gate_ffn_item], axis=1
    )
    band_grad = jnp.dot(band_onehot.T, item_grad, precision=HIGHEST)
    local_band_grad = lax.dynamic_slice_in_dim(band_grad, tp_index * mod_cols, mod_cols, 1)
    ada_grad = jnp.dot(silu_embed.T, local_band_grad, precision=HIGHEST)
    ada_bias_part = jnp.sum(local_band_grad, axis=0)
    summed = (
        lax.psum_scatter(
            query_grad.astype(jnp.bfloat16), "seq", scatter_dimension=0, tiled=True
        ).astype(jnp.float32),
        lax.psum_scatter(
            key_grad.astype(jnp.bfloat16), "seq", scatter_dimension=0, tiled=True
        ).astype(jnp.float32),
        lax.psum_scatter(
            value_grad.astype(jnp.bfloat16), "seq", scatter_dimension=0, tiled=True
        ).astype(jnp.float32),
        lax.psum_scatter(
            gate_grad.astype(jnp.bfloat16), "seq", scatter_dimension=0, tiled=True
        ).astype(jnp.float32),
        lax.psum_scatter(
            up_grad.astype(jnp.bfloat16), "seq", scatter_dimension=0, tiled=True
        ).astype(jnp.float32),
        lax.psum_scatter(
            text_key_grad.astype(jnp.bfloat16), "seq", scatter_dimension=0, tiled=True
        ).astype(jnp.float32),
        lax.psum_scatter(
            text_value_grad.astype(jnp.bfloat16), "seq", scatter_dimension=0, tiled=True
        ).astype(jnp.float32),
        lax.psum_scatter(
            ada_grad.astype(jnp.bfloat16), "seq", scatter_dimension=0, tiled=True
        ).astype(jnp.float32),
        lax.psum_scatter(
            out_grad.astype(jnp.bfloat16), "seq", scatter_dimension=1, tiled=True
        ).astype(jnp.float32),
        lax.psum_scatter(
            down_grad.astype(jnp.bfloat16), "seq", scatter_dimension=1, tiled=True
        ).astype(jnp.float32),
    )
    smalls = lax.psum(
        (
            attn_gain_part,
            ffn_gain_part,
            query_gain_part.reshape(local_width),
            key_gain_part.reshape(local_width),
            text_gain_part.reshape(local_width),
            cross_gate_part,
            ada_bias_part,
        ),
        "seq",
    )
    return (
        block_out,
        tokens_grad,
        text_grad,
        summed[7],
        smalls[6],
        smalls[0],
        smalls[1],
        summed[0],
        summed[1],
        summed[2],
        smalls[2],
        smalls[3],
        smalls[5],
        summed[5],
        summed[6],
        smalls[4],
        summed[8],
        summed[3],
        summed[4],
        summed[9],
    )


MESH_AXES = ("z", "y", "x", "c")
PLANE_AXES = ("y", "x")
PLANE = 4
STRIPS = 4
CORES = 2


def device_pairs(target):
    pairs = []
    for strip in range(STRIPS):
        for place in range(PLANE):
            for core in range(CORES):
                aim = target(strip, place, core)
                pairs.append(
                    (
                        (strip * PLANE + place) * CORES + core,
                        (aim[0] * PLANE + aim[1]) * CORES + aim[2],
                    )
                )
    return pairs


FLIP_CORE = device_pairs(lambda strip, place, core: (strip, place, 1 - core))
FLIP_FIRST = device_pairs(lambda strip, place, core: (strip, place ^ (1 + core), core))
FLIP_SECOND = device_pairs(lambda strip, place, core: (strip, place ^ (2 - core), core))
FLIP_PLACE = {
    mask: device_pairs(lambda strip, place, core, mask=mask: (strip, place ^ mask, core))
    for mask in (1, 2, 3)
}
FLIP_STRIP = {
    mask: device_pairs(lambda strip, place, core, mask=mask: (strip ^ mask, place, core))
    for mask in (1, 2, 3)
}


def move(value, pairs):
    return lax.ppermute(value, MESH_AXES, pairs)


def gather_by(value, table):
    return [value] + [move(value, table[mask]) for mask in (1, 2, 3)]


def after(value, *earlier):
    return lax.optimization_barrier((value, earlier))[0]


def plane_gather(own, beside=()):
    own = jnp.concatenate([own, move(own, FLIP_FIRST)])
    own = jnp.concatenate([own, after(move(own, FLIP_SECOND), beside)])
    return own, move(own, FLIP_CORE)


SCATTER_STEPS = (FLIP_CORE, FLIP_SECOND, FLIP_FIRST)


def core_half(whole):
    half = whole.shape[0] // 2
    arrived = move(whole[half:], FLIP_CORE)
    return whole[:half].astype(jnp.float32) + arrived.astype(jnp.float32)


def plane_scatter(whole, *besides):
    for step, pairs in enumerate(SCATTER_STEPS[-(whole.shape[0] // 256).bit_length() :]):
        half = whole.shape[0] // 2
        arrived = move(whole[half:].astype(jnp.bfloat16), pairs)
        if step < len(besides):
            arrived = after(arrived, besides[step])
        whole = whole[:half].astype(jnp.float32) + arrived.astype(jnp.float32)
    return whole


def pair_sum(four):
    return (four[0] + four[1]) + (four[2] + four[3])


def absolute(relative, index):
    odd = (index & 1) == 1
    high = (index & 2) == 2
    step = [jnp.where(odd, relative[i ^ 1], relative[i]) for i in range(4)]
    return [jnp.where(high, step[i ^ 2], step[i]) for i in range(4)]


def across(value, axes, split, concat):
    return lax.all_to_all(value, axes, split, concat, tiled=True)


def contract(left, right, left_dim, right_dim):
    return lax.dot_general(
        left,
        right,
        (((left_dim,), (right_dim,)), ((), ())),
        preferred_element_type=jnp.float32,
    )


def turn(block, cosine, sine):
    a, b, c, d = block[0:16], block[16:32], block[32:48], block[48:64]
    cr, cc = cosine[0:16], cosine[16:32]
    sr, sc = sine[0:16], sine[16:32]
    return jnp.concatenate(
        [a * cr - b * sr, a * sr + b * cr, c * cc - d * sc, c * sc + d * cc], axis=0
    )


def unit_of(raw):
    inverse = lax.rsqrt(jnp.mean(raw * raw, axis=0, keepdims=True) + EPSILON)
    return raw * inverse, inverse


def unit_back(incoming, unit, inverse, gain):
    lifted = incoming * gain
    gain_part = jnp.sum(incoming * unit, axis=1, keepdims=True)
    raw_part = inverse * (lifted - unit * jnp.mean(lifted * unit, axis=0, keepdims=True))
    return raw_part, gain_part


QBLOCK = 256
VMEM_LIMIT = 56 * 1024 * 1024


def lanes_of(ref):
    return jnp.concatenate([ref[i] for i in range(PLANE)], axis=-1)


def text_of(ref, kind):
    part = ref.shape[-1] // 2
    lanes = slice(kind * part, (kind + 1) * part)
    return jnp.concatenate([ref[i, :, lanes] for i in range(PLANE)], axis=-1)


def attend_kernel(
    spot_ref,
    q_ref,
    k_ref,
    v_ref,
    text_ref,
    norm_ref,
    cos_ref,
    sin_ref,
    valid_ref,
    gate_ref,
    comb_ref,
    self_ref,
    cross_ref,
    qlow_ref,
    klow_ref,
    tlow_ref,
    rinv_ref,
):
    cosine, sine, valid = cos_ref[...], sin_ref[...], valid_ref[...]
    query = turn(unit_of(q_ref[...])[0] * norm_ref[:, 0:1], cosine, sine).astype(jnp.bfloat16)
    key = turn(unit_of(k_ref[...])[0] * norm_ref[:, 1:2], cosine, sine)
    qlow_ref[...] = query
    klow_ref[...] = key.astype(jnp.bfloat16)
    key_rows = key.T.astype(jnp.bfloat16)
    text_key = unit_of(text_of(text_ref, 0))[0] * norm_ref[:, 2:3]
    tlow_ref[...] = text_key.astype(jnp.bfloat16)
    text_rows = text_key.T.astype(jnp.bfloat16)
    value = v_ref[...].astype(jnp.bfloat16).astype(jnp.float32) * valid
    lanes = value.shape[1]
    value_ones = jnp.concatenate(
        [value, jnp.broadcast_to(valid, (16, lanes))], axis=0
    ).astype(jnp.bfloat16)
    tvalue = text_of(text_ref, 1)
    tvalue_ones = jnp.concatenate(
        [tvalue, jnp.ones((16, tvalue.shape[1]), jnp.float32)], axis=0
    ).astype(jnp.bfloat16)
    gate = gate_ref[0:1, 0:1]
    scaled = (query.astype(jnp.float32) * 0.125).astype(jnp.bfloat16)
    for chunk in range(lanes // QBLOCK):
        cols = slice(chunk * QBLOCK, (chunk + 1) * QBLOCK)
        weight = jnp.exp(contract(key_rows, scaled[:, cols], 1, 0)).astype(jnp.bfloat16)
        total = contract(value_ones, weight, 1, 0)
        rinv = 1.0 / total[64:65]
        own = total[:64] * rinv
        tweight = jnp.exp(contract(text_rows, scaled[:, cols], 1, 0)).astype(jnp.bfloat16)
        ttotal = contract(tvalue_ones, tweight, 1, 0)
        trinv = 1.0 / ttotal[64:65]
        text = ttotal[:64] * trinv
        self_ref[:, cols] = own
        cross_ref[:, cols] = text
        rinv_ref[0:1, cols] = rinv
        rinv_ref[1:2, cols] = trinv
        comb_ref[chunk] = (own + gate * text).astype(jnp.bfloat16)


def attend_back_kernel(
    spot_ref,
    q_ref,
    k_ref,
    v_ref,
    text_ref,
    norm_ref,
    cos_ref,
    sin_ref,
    valid_ref,
    gate_ref,
    self_ref,
    cross_ref,
    qlow_ref,
    klow_ref,
    tlow_ref,
    rinv_ref,
    dcomb_ref,
    dqkv_ref,
    dtext_ref,
    gains_ref,
):
    cosine, sine, valid = cos_ref[...], sin_ref[...], valid_ref[...]
    lanes = valid.shape[1]
    gate = gate_ref[0:1, 0:1]
    dcomb = lanes_of(dcomb_ref).astype(jnp.float32)
    cross = cross_ref[...]
    dself = dcomb.astype(jnp.bfloat16)
    dcross = (dcomb * gate).astype(jnp.bfloat16)
    delta = jnp.sum(dself.astype(jnp.float32) * self_ref[...], axis=0, keepdims=True)
    tdelta = jnp.sum(dcross.astype(jnp.float32) * cross, axis=0, keepdims=True)
    gate_part = jnp.sum(
        jnp.sum(dcomb * cross, axis=0, keepdims=True), axis=1, keepdims=True
    ) * (1.0 - gate * gate)
    query = qlow_ref[...]
    scaled = (query.astype(jnp.float32) * 0.125).astype(jnp.bfloat16)
    key = klow_ref[...].astype(jnp.float32)
    key_rows = key.T.astype(jnp.bfloat16)
    key_held = (key * valid * 0.125).astype(jnp.bfloat16)
    value_rows = v_ref[...].T.astype(jnp.bfloat16)
    text_key = tlow_ref[...].astype(jnp.float32)
    text_rows = text_key.T.astype(jnp.bfloat16)
    text_held = (text_key * 0.125).astype(jnp.bfloat16)
    tvalue_rows = text_of(text_ref, 1).T.astype(jnp.bfloat16)
    dkey = dvalue = dtkey = dtvalue = 0.0
    dquery = []
    for start in range(0, lanes, QBLOCK):
        cols = slice(start, start + QBLOCK)
        probs = jnp.exp(contract(key_rows, scaled[:, cols], 1, 0)) * rinv_ref[0:1, cols]
        dprobs = contract(value_rows, dself[:, cols], 1, 0)
        dscore = (probs * (dprobs - delta[:, cols])).astype(jnp.bfloat16)
        dvalue += contract(dself[:, cols], probs.astype(jnp.bfloat16), 1, 1)
        dkey += contract(scaled[:, cols], dscore, 1, 1)
        turned = contract(key_held, dscore, 1, 0)
        tprobs = jnp.exp(contract(text_rows, scaled[:, cols], 1, 0)) * rinv_ref[1:2, cols]
        dtprobs = contract(tvalue_rows, dcross[:, cols], 1, 0)
        dtscore = (tprobs * (dtprobs - tdelta[:, cols])).astype(jnp.bfloat16)
        dtvalue += contract(dcross[:, cols], tprobs.astype(jnp.bfloat16), 1, 1)
        dtkey += contract(scaled[:, cols], dtscore, 1, 1)
        dquery.append(turned + contract(text_held, dtscore, 1, 0))
    dquery = jnp.concatenate(dquery, axis=1)
    unit, inverse = unit_of(q_ref[...])
    draw_q, query_gain = unit_back(turn(dquery, cosine, -sine), unit, inverse, norm_ref[:, 0:1])
    unit, inverse = unit_of(k_ref[...])
    draw_k, key_gain = unit_back(turn(dkey * valid, cosine, -sine), unit, inverse, norm_ref[:, 1:2])
    unit, inverse = unit_of(text_of(text_ref, 0))
    draw_t, text_gain = unit_back(dtkey, unit, inverse, norm_ref[:, 2:3])
    dvalue = dvalue * valid
    for chunk in range(PLANE):
        cols = slice(chunk * QBLOCK, (chunk + 1) * QBLOCK)
        dqkv_ref[chunk, 0:64] = draw_q[:, cols].astype(jnp.bfloat16)
        dqkv_ref[chunk, 64:128] = draw_k[:, cols].astype(jnp.bfloat16)
        dqkv_ref[chunk, 128:192] = dvalue[:, cols].astype(jnp.bfloat16)
        size = draw_t.shape[1] // PLANE
        cols = slice(chunk * size, (chunk + 1) * size)
        dtext_ref[chunk] = jnp.concatenate([draw_t[:, cols], dtvalue[:, cols]], axis=1).astype(
            jnp.bfloat16
        )
    gains_ref[:, 0:128] = jnp.broadcast_to(query_gain, (64, 128))
    gains_ref[:, 128:256] = jnp.broadcast_to(key_gain, (64, 128))
    gains_ref[:, 256:384] = jnp.broadcast_to(text_gain, (64, 128))
    gains_ref[:, 384:512] = jnp.broadcast_to(gate_part, (64, 128))


def head_block(width, offset=0):
    return pl.BlockSpec((HDIM, width), lambda h, s: (h + offset, 0))


def shared_block(rows, width):
    return pl.BlockSpec((rows, width), lambda h, s: (0, 0))


def params():
    return pltpu.CompilerParams(vmem_limit_bytes=VMEM_LIMIT)


def cost(flops, moved):
    return pl.CostEstimate(flops=flops, bytes_accessed=moved, transcendentals=0)


def attention_call(heads, lanes, texts, backward):
    f32, b16 = jnp.float32, jnp.bfloat16
    part = texts // PLANE
    specs = [
        head_block(lanes),
        head_block(lanes, heads),
        head_block(lanes, 2 * heads),
        pl.BlockSpec((PLANE, HDIM, 2 * part), lambda h, s: (0, h, 0)),
        pl.BlockSpec((HDIM, 3), lambda h, s: (s[0] * heads + h, 0)),
        shared_block(32, lanes),
        shared_block(32, lanes),
        shared_block(1, lanes),
        pl.BlockSpec((8, 128), lambda h, s: (s[0] * heads + h, 0)),
    ]
    wide = heads * HDIM
    chunk_spec = pl.BlockSpec((PLANE, HDIM, QBLOCK), lambda h, s: (0, h, 0))
    rinv_spec = pl.BlockSpec((8, lanes), lambda h, s: (h, 0))
    saved = [head_block(lanes)] * 4 + [head_block(texts), rinv_spec]
    shape = jax.ShapeDtypeStruct
    pairs = heads * lanes * (lanes + texts)
    if not backward:
        out_specs = [chunk_spec] + saved
        out_shape = [
            shape((PLANE, wide, lanes // PLANE), b16),
            shape((wide, lanes), f32),
            shape((wide, lanes), f32),
            shape((wide, lanes), b16),
            shape((wide, lanes), b16),
            shape((wide, texts), b16),
            shape((heads * 8, lanes), f32),
        ]
        body, passes = attend_kernel, 2
    else:
        specs = specs + saved + [chunk_spec]
        out_specs = [
            pl.BlockSpec((PLANE, 3 * HDIM, QBLOCK), lambda h, s: (0, h, 0)),
            pl.BlockSpec((PLANE, HDIM, 2 * part), lambda h, s: (0, h, 0)),
            head_block(512),
        ]
        out_shape = [
            shape((PLANE, 3 * wide, lanes // PLANE), b16),
            shape((PLANE, wide, 2 * part), b16),
            shape((wide, 512), f32),
        ]
        body, passes = attend_back_kernel, 5
    return pl.pallas_call(
        body,
        grid_spec=pltpu.PrefetchScalarGridSpec(
            num_scalar_prefetch=1, grid=(heads,), in_specs=specs, out_specs=out_specs
        ),
        out_shape=out_shape,
        compiler_params=params(),
        cost_estimate=cost(8 * pairs * HDIM * passes, 8 * wide * lanes),
    )


def project_kernel(spot_ref, own_ref, other_ref, lift_ref, weight_ref, in_ref, qkv_ref, turned):
    @pl.when(pl.program_id(0) == 0)
    def _():
        turned[...] = weight_ref[...].T

    first = spot_ref[1] == 0
    own, other = own_ref[...].astype(jnp.float32), other_ref[...].astype(jnp.float32)
    values = jnp.concatenate([jnp.where(first, own, other), jnp.where(first, other, own)])
    normed = (values * rms_inverse(values) * lift_ref[...]).astype(jnp.bfloat16)
    in_ref[...] = normed
    qkv_ref[...] = contract(turned[...], normed, 1, 1)


def project(spot, halves, lift, weight):
    rows, width = halves[0].shape
    wide = weight.shape[1]
    block = rows // PLANE
    return pl.pallas_call(
        project_kernel,
        grid_spec=pltpu.PrefetchScalarGridSpec(
            num_scalar_prefetch=1,
            grid=(PLANE,),
            in_specs=[
                pl.BlockSpec((block, width), lambda i, s: (i, 0)),
                pl.BlockSpec((block, width), lambda i, s: (i % 2 * 2 + i // 2, 0)),
                pl.BlockSpec((1, width), lambda i, s: (0, 0)),
                pl.BlockSpec((width, wide), lambda i, s: (0, 0)),
            ],
            out_specs=[
                pl.BlockSpec((2 * block, width), lambda i, s: (s[2 + i] // 2, 0)),
                pl.BlockSpec((wide, 2 * block), lambda i, s: (0, s[2 + i] // 2)),
            ],
            scratch_shapes=[pltpu.VMEM((wide, width), jnp.bfloat16)],
        ),
        out_shape=[
            jax.ShapeDtypeStruct((2 * rows, width), jnp.bfloat16),
            jax.ShapeDtypeStruct((wide, 2 * rows), jnp.float32),
        ],
        compiler_params=params(),
        cost_estimate=cost(4 * rows * width * wide, 16 * rows * width),
    )(spot, *halves, lift, weight)


def ffn_kernel(spot_ref, a_ref, b_ref, d0_ref, d1_ref, gw_ref, uw_ref, dw_ref, h_ref, din_ref):
    early = pl.program_id(0) < 2
    rows_in = jnp.where(early, a_ref[...], b_ref[...])
    d_out = jnp.concatenate([d0_ref[...], d1_ref[...]])
    size = gw_ref.shape[1]
    gate_pre = jnp.dot(rows_in, gw_ref[...], preferred_element_type=jnp.float32)
    up_pre = jnp.dot(rows_in, uw_ref[...], preferred_element_type=jnp.float32)
    d_hidden = contract(d_out, dw_ref[...], 1, 1)
    gate_sig = jax.nn.sigmoid(gate_pre)
    swish = gate_pre * gate_sig
    d_gate = (d_hidden * up_pre * (gate_sig + swish * (1.0 - gate_sig))).astype(jnp.bfloat16)
    d_up = (d_hidden * swish).astype(jnp.bfloat16)
    h_ref[:, 0:size] = d_gate
    h_ref[:, size : 2 * size] = d_up
    h_ref[:, 2 * size : 3 * size] = (swish * up_pre).astype(jnp.bfloat16)
    din_ref[...] = (
        contract(d_gate, gw_ref[...], 1, 1) + contract(d_up, uw_ref[...], 1, 1)
    ).astype(jnp.bfloat16)


def ffn(spot, halves, d_ffn, gate_weight, up_weight, down_weight):
    rows, width = halves[0].shape
    size = gate_weight.shape[1] // PLANE
    block = rows // 2
    early = pl.BlockSpec((block, width), lambda i, s: (jnp.minimum(i, 1), 0))
    late = pl.BlockSpec((block, width), lambda i, s: (jnp.maximum(i - 2, 0), 0))
    col = pl.BlockSpec((width, size), lambda i, s: (0, s[0]))
    return pl.pallas_call(
        ffn_kernel,
        grid_spec=pltpu.PrefetchScalarGridSpec(
            num_scalar_prefetch=1,
            grid=(4,),
            in_specs=[
                early,
                late,
                pl.BlockSpec((block // 2, width), lambda i, s: (s[2 + 2 * i], 0)),
                pl.BlockSpec((block // 2, width), lambda i, s: (s[3 + 2 * i], 0)),
                col,
                col,
                pl.BlockSpec((size, width), lambda i, s: (s[0], 0)),
            ],
            out_specs=[
                pl.BlockSpec((block, 3 * size), lambda i, s: (i, 0)),
                pl.BlockSpec((block, width), lambda i, s: (i, 0)),
            ],
        ),
        out_shape=[
            jax.ShapeDtypeStruct((2 * rows, 3 * size), jnp.bfloat16),
            jax.ShapeDtypeStruct((2 * rows, width), jnp.bfloat16),
        ],
        compiler_params=params(),
        cost_estimate=cost(20 * rows * width * size, 16 * rows * width),
    )(spot, *halves, d_ffn, d_ffn, gate_weight, up_weight, down_weight)


def ffn_grad_kernel(
    spot_ref, a_ref, b_ref, d_ref, inner_ref, hid_ref, dw_ref, grad_ref, out_ref
):
    rows = a_ref.shape[0]
    size = hid_ref.shape[1]
    block = rows // 4
    starts = [pl.multiple_of(spot_ref[2 + i] * block, block) for i in range(8)]
    d_rows = jnp.concatenate([d_ref[pl.ds(start, block), :] for start in starts])
    in_rows = jnp.concatenate([a_ref[...], b_ref[...]])
    hidden = hid_ref[...]
    grad_ref[:, : 2 * size] = contract(in_rows, inner_ref[...], 0, 0).astype(jnp.bfloat16)
    grad_ref[:, 2 * size :] = contract(d_rows, hidden, 0, 0).astype(jnp.bfloat16)
    out_ref[...] = jnp.dot(hidden, dw_ref[...], preferred_element_type=jnp.float32).astype(
        jnp.bfloat16
    )


def ffn_grad(spot, halves, d_ffn, inner, down_weight):
    rows, width = halves[0].shape
    size = inner.shape[1] // 3
    tile = width // 3
    return pl.pallas_call(
        ffn_grad_kernel,
        grid_spec=pltpu.PrefetchScalarGridSpec(
            num_scalar_prefetch=1,
            grid=(3,),
            in_specs=[
                pl.BlockSpec((rows, tile), lambda i, s: (0, i)),
                pl.BlockSpec((rows, tile), lambda i, s: (0, i)),
                pl.BlockSpec((2 * rows, tile), lambda i, s: (0, i)),
                pl.BlockSpec((2 * rows, 2 * size), lambda i, s: (0, 0)),
                pl.BlockSpec((2 * rows, size), lambda i, s: (0, 2)),
                pl.BlockSpec((size, tile), lambda i, s: (s[0], i)),
            ],
            out_specs=[
                pl.BlockSpec((tile, 3 * size), lambda i, s: (i, 0)),
                pl.BlockSpec((2 * rows, tile), lambda i, s: (0, i)),
            ],
        ),
        out_shape=[
            jax.ShapeDtypeStruct((width, 3 * size), jnp.bfloat16),
            jax.ShapeDtypeStruct((2 * rows, width), jnp.bfloat16),
        ],
        compiler_params=params(),
        cost_estimate=cost(16 * rows * width * size, 16 * rows * width),
    )(spot, *halves, d_ffn, inner, inner, down_weight)


def by_kind(block, kind, heads):
    return jnp.concatenate(
        [
            block[i, (3 * h + kind) * HDIM : (3 * h + kind + 1) * HDIM]
            for i in range(block.shape[0])
            for h in range(heads)
        ],
        axis=0,
    )


def input_grad_kernel(d_ref, qw_ref, kw_ref, vw_ref, out_ref):
    heads = d_ref.shape[1] // (3 * HDIM)
    total = 0.0
    for kind, weight in enumerate((qw_ref, kw_ref, vw_ref)):
        total += contract(by_kind(d_ref, kind, heads).T, weight[...], 1, 1)
    out_ref[...] = total


def input_grad(d_qkv, query_weight, key_weight, value_weight):
    width, wide = query_weight.shape
    rows = d_qkv.shape[2]
    tile = width // 3
    weight = pl.BlockSpec((tile, wide), lambda i: (i, 0))
    return pl.pallas_call(
        input_grad_kernel,
        grid=(3,),
        in_specs=[pl.BlockSpec(d_qkv.shape, lambda i: (0, 0, 0)), weight, weight, weight],
        out_specs=pl.BlockSpec((rows, tile), lambda i: (0, i)),
        out_shape=jax.ShapeDtypeStruct((rows, width), jnp.float32),
        compiler_params=params(),
        cost_estimate=cost(6 * rows * width * wide, 6 * width * wide),
    )(d_qkv, query_weight, key_weight, value_weight)


def attn_grad_kernel(spot_ref, in_ref, own_ref, other_ref, d_ref, comb_ref, out_ref):
    places, _, rows = d_ref.shape
    wide = comb_ref.shape[1]
    heads = wide // HDIM
    first = spot_ref[1] == 0
    total = branch = 0.0
    for place in range(places):
        part = slice(place * rows, (place + 1) * rows)
        block = d_ref[place : place + 1]
        ordered = jnp.concatenate([by_kind(block, kind, heads) for kind in range(3)])
        total += contract(in_ref[part].T, ordered, 1, 1)
        own, other = own_ref[place], other_ref[place]
        d_attn = jnp.concatenate([jnp.where(first, own, other), jnp.where(first, other, own)])
        branch += contract(d_attn.T, comb_ref[place], 1, 1)
    out_ref[:, : 3 * wide] = total.astype(jnp.bfloat16)
    out_ref[:, 3 * wide :] = branch.astype(jnp.bfloat16)


def attn_grad(spot, attn_in, own_d_attn, other_d_attn, d_qkv, combined):
    rows, width = attn_in.shape
    wide = combined.shape[1]
    tile = width // 3
    core_rows = pl.BlockSpec(own_d_attn.shape[:2] + (tile,), lambda i, s: (0, 0, i))
    return pl.pallas_call(
        attn_grad_kernel,
        grid_spec=pltpu.PrefetchScalarGridSpec(
            num_scalar_prefetch=1,
            grid=(3,),
            in_specs=[
                pl.BlockSpec((rows, tile), lambda i, s: (0, i)),
                core_rows,
                core_rows,
                pl.BlockSpec(d_qkv.shape, lambda i, s: (0, 0, 0)),
                pl.BlockSpec(combined.shape, lambda i, s: (0, 0, 0)),
            ],
            out_specs=pl.BlockSpec((tile, 4 * wide), lambda i, s: (i, 0)),
        ),
        out_shape=jax.ShapeDtypeStruct((width, 4 * wide), jnp.bfloat16),
        compiler_params=params(),
        cost_estimate=cost(8 * rows * width * wide, 4 * rows * width),
    )(spot, attn_in, own_d_attn, other_d_attn, d_qkv, combined)


def strips_kernel(in_ref, out_ref):
    size = out_ref.shape[2]
    for strip in range(out_ref.shape[0]):
        out_ref[strip] = in_ref[:, strip * size : (strip + 1) * size]


def by_strips(states):
    rows, cols = states.shape
    return pl.pallas_call(
        strips_kernel,
        out_shape=jax.ShapeDtypeStruct((STRIPS, rows, cols // STRIPS), states.dtype),
        compiler_params=params(),
        cost_estimate=cost(0, 4 * rows * cols),
    )(states)


def text_grad_kernel(where_ref, states, *refs):
    d_text, out_ref = refs[:STRIPS], refs[STRIPS]
    own = where_ref[0]
    part = d_text[0].shape[2] // 2
    total = 0.0
    for place in range(PLANE):
        blocks = [
            jnp.concatenate([piece[place, :, :part], piece[place, :, part:]]) for piece in d_text
        ]
        starts = [(place * STRIPS + (own ^ strip)) * part for strip in range(STRIPS)]
        rows = [states[pl.ds(pl.multiple_of(start, part), part), :] for start in starts]
        total += jnp.dot(
            jnp.concatenate(blocks, axis=-1),
            jnp.concatenate(rows),
            preferred_element_type=jnp.float32,
        )
    size = total.shape[1] // PLANE
    for place in range(PLANE):
        out_ref[place] = total[:, place * size : (place + 1) * size].astype(jnp.bfloat16)


def text_weight_grad(strip, states, strips):
    rows, cols = states.shape
    wide = 2 * strips[0].shape[1]
    whole = pl.BlockSpec(memory_space=pltpu.VMEM)
    return pl.pallas_call(
        text_grad_kernel,
        in_specs=[pl.BlockSpec(memory_space=pltpu.SMEM)] + [whole] * 5,
        out_specs=whole,
        out_shape=jax.ShapeDtypeStruct((PLANE, wide, cols // PLANE), jnp.bfloat16),
        compiler_params=params(),
        cost_estimate=cost(2 * rows * cols * wide, 2 * rows * cols),
    )(strip, states, *strips)


def split_three(value):
    high = lax.reduce_precision(value, 8, 7)
    middle = lax.reduce_precision(value - high, 8, 7)
    return jnp.concatenate([high, middle, value - high - middle]).astype(jnp.bfloat16)


def strip_shards(
    tokens,
    cotangent,
    step_embed,
    item_band,
    item_length,
    item_width,
    text_states,
    ada_weight,
    ada_bias,
    attn_gain,
    ffn_gain,
    query_weight,
    key_weight,
    value_weight,
    query_gain,
    key_gain,
    cross_gate,
    text_key_weight,
    text_value_weight,
    text_key_gain,
    out_weight,
    gate_weight,
    up_weight,
    down_weight,
):
    f32, b16 = jnp.float32, jnp.bfloat16
    strip = lax.axis_index("z")
    place = lax.axis_index("y") * 2 + lax.axis_index("x")
    core = lax.axis_index("c")
    first_core = core == 0
    spot = [place, core]
    for block in range(2 * PLANE):
        from_core = core ^ (block // PLANE)
        from_place = place
        if block & 1:
            from_place = from_place ^ (1 + from_core)
        if block & 2:
            from_place = from_place ^ (2 - from_core)
        spot.append(from_place * CORES + from_core)
    spot = jnp.stack(spot).astype(jnp.int32)
    width = tokens.shape[1]
    half = SLOT // CORES
    own_rows = STRIPS * half
    lanes = own_rows * PLANE * CORES
    wide = query_weight.shape[1] // PLANE
    heads = wide // HDIM
    hidden_wide = gate_weight.shape[1] // PLANE
    text_own = text_states.shape[0]
    texts = text_own * PLANE

    def both_cores(own, axis=0):
        other = move(own, FLIP_CORE)
        low = jnp.where(first_core, own, other)
        high = jnp.where(first_core, other, own)
        return jnp.concatenate([low, high], axis=axis)

    def core_scatter(partial, axis=0):
        size = partial.shape[axis] // CORES
        sent = lax.dynamic_slice_in_dim(partial, (1 - core) * size, size, axis)
        kept = lax.dynamic_slice_in_dim(partial, core * size, size, axis)
        return kept.astype(f32) + move(sent.astype(b16), FLIP_CORE).astype(f32)

    def to_items(*arrays):
        parts = [
            lax.dynamic_slice_in_dim(a.reshape(ITEMS, SLOT, width), core * half, half, 1)
            for a in arrays
        ]
        parts = across(jnp.concatenate(parts, axis=1), "z", 0, 0)
        parts = parts.reshape(STRIPS, len(arrays), half, width)
        return [parts[:, i].reshape(own_rows, width) for i in range(len(arrays))]

    def from_items(beside, *arrays):
        parts = jnp.concatenate([a.reshape(STRIPS, half, width) for a in arrays], axis=1)
        parts = across(parts, "z", 0, 0)
        other = move(after(parts, beside), FLIP_CORE)
        outs = []
        for i in range(len(arrays)):
            own_part, other_part = (p[:, i * half : (i + 1) * half] for p in (parts, other))
            low = jnp.where(first_core, own_part, other_part)
            high = jnp.where(first_core, other_part, own_part)
            outs.append(jnp.concatenate([low, high], axis=1).reshape(ITEMS * SLOT, width))
        return outs

    own_tokens, incoming_low = to_items(tokens, cotangent)
    text_raw = jnp.concatenate(
        [
            contract(text_key_weight, text_states, 0, 1),
            contract(text_value_weight, text_states, 0, 1).astype(b16).astype(f32),
        ],
        axis=1,
    ).reshape(PLANE, wide, 2 * text_own)
    qkv_weight = jnp.concatenate(
        [
            lax.dynamic_slice_in_dim(weight, place * wide, wide, 1)
            for weight in (query_weight, key_weight, value_weight)
        ],
        axis=1,
    )
    silu_embed = jax.nn.silu(step_embed.astype(f32))
    products = jnp.dot(split_three(silu_embed), ada_weight, preferred_element_type=f32)
    local_mod = products[0:4] + products[4:8] + products[8:12] + ada_bias
    own_tokens = after(own_tokens, text_raw, qkv_weight, local_mod)
    pair = jnp.concatenate([own_tokens, move(own_tokens, FLIP_FIRST)])
    pair_arrived = move(pair, FLIP_SECOND)
    text_raw = across(after(text_raw, pair), PLANE_AXES, 0, 0)

    other_mod = move(after(local_mod, own_tokens), FLIP_CORE)
    low_mod = jnp.where(first_core, local_mod, other_mod)
    high_mod = jnp.where(first_core, other_mod, local_mod)

    item_ids = jnp.arange(ITEMS, dtype=jnp.int32)
    band_mask = (item_band[:, None] == item_ids[None, :]).astype(f32)
    own_mask = jnp.sum(jnp.where(item_ids[:, None] == strip, band_mask, 0.0), axis=0)

    own_low = jnp.sum(own_mask[:, None] * low_mod, axis=0)
    own_high = jnp.sum(own_mask[:, None] * high_mod, axis=0)
    scale_attn, scale_ffn = own_low[:width], own_high[:width]
    lift_attn = attn_gain * (1.0 + scale_attn)
    lift_ffn = ffn_gain * (1.0 + scale_ffn)
    gate_attn = jnp.tanh(own_low[width:])
    gate_ffn = jnp.tanh(own_high[width:])

    lane = jnp.arange(lanes, dtype=jnp.int32)
    from_place = lane // (own_rows * CORES)
    from_core = (lane // own_rows) % CORES
    from_strip = (lane % own_rows) // half
    position = (from_strip * PLANE + from_place) * SLOT + from_core * half + lane % half
    chosen = jnp.where(item_ids[:, None] == strip, 1, 0)
    width_here = jnp.sum(chosen * after(item_width, pair)[:, None], axis=0)
    length_here = jnp.sum(chosen * item_length[:, None], axis=0)
    grid_row = (position // width_here).astype(f32)
    grid_col = (position % width_here).astype(f32)
    quarter = HDIM // 4
    frequency = ROPE_BASE ** (-jnp.arange(quarter, dtype=f32) / quarter)
    angles = jnp.concatenate(
        [frequency[:, None] * grid_row[None, :], frequency[:, None] * grid_col[None, :]]
    )
    cosine, sine = jnp.cos(angles), jnp.sin(angles)
    valid = (position < length_here).astype(f32)[None, :]

    norm_gains = jnp.stack([query_gain, key_gain, text_key_gain], axis=1)
    gate_tiles = jnp.broadcast_to(jnp.tanh(cross_gate)[:, None, None], (cross_gate.shape[0], 8, 128))
    gate_tiles = gate_tiles.reshape(-1, 128)

    low_half = jnp.concatenate(
        [pair, after(pair_arrived, lift_attn, text_raw, cosine, sine, norm_gains, gate_tiles)]
    )
    incoming = after(incoming_low, pair).astype(f32)
    own_d_ffn = (gate_ffn * incoming).astype(b16)
    high_half = after(move(low_half, FLIP_CORE), own_d_ffn)
    d_ffn = lax.all_gather(after(own_d_ffn, low_half), PLANE_AXES + ("c",), axis=0, tiled=True)
    attn_in, qkv = project(spot, (low_half, high_half), lift_attn[None, :], qkv_weight)
    common = (
        spot,
        qkv,
        qkv,
        qkv,
        text_raw,
        norm_gains,
        cosine,
        sine,
        valid,
        gate_tiles,
    )
    combined, *saved = attention_call(heads, lanes, texts, False)(*common)
    chip_combined = across(combined, PLANE_AXES, 0, 0).reshape(-1, own_rows * CORES)
    attn_branch = core_scatter(contract(chip_combined, out_weight, 0, 0))

    residual = own_tokens.astype(f32)
    middle = residual + gate_attn * attn_branch
    inverse_two = rms_inverse(middle)
    normed_two = middle * inverse_two
    own_ffn_in = (normed_two * lift_ffn).astype(b16)
    own_ffn_in = after(own_ffn_in, d_ffn)
    states_wide = text_states.shape[1] // STRIPS
    states = by_strips(after(text_states, own_ffn_in))
    states = across(states, "z", 0, 0).reshape(texts, states_wide)
    ffn_in = plane_gather(own_ffn_in, (states,))
    states = lax.all_gather(states, PLANE_AXES, axis=0, tiled=True)
    inner, d_ffn_in = ffn(spot, ffn_in, d_ffn, gate_weight, up_weight, down_weight)
    ffn_grads, ffn_branch = ffn_grad(spot, ffn_in, d_ffn, inner, down_weight)
    branch_half = core_half(ffn_branch)
    d_ffn_in = plane_scatter(d_ffn_in, (ffn_grads,), (branch_half,))
    d_normed = d_ffn_in * normed_two
    u_ffn = jnp.sum(d_normed, axis=0)
    d_middle = incoming + inverse_two * (
        d_ffn_in * lift_ffn
        - normed_two * jnp.mean(d_normed * lift_ffn, axis=-1, keepdims=True)
    )
    w_attn = jnp.sum(d_middle * attn_branch, axis=0) * (1.0 - gate_attn * gate_attn)
    own_d_attn = (gate_attn * d_middle).astype(b16)
    d_attn = both_cores(own_d_attn)

    d_comb = contract(out_weight, d_attn, 1, 1).astype(b16).reshape(PLANE, wide, -1)
    d_comb = across(d_comb, PLANE_AXES, 0, 0)
    d_qkv, d_text, gains = attention_call(heads, lanes, texts, True)(*common, *saved, d_comb)
    own_rows_d = jnp.broadcast_to(after(own_d_attn, d_comb), (PLANE, own_rows, width))
    own_rows_d = across(own_rows_d, PLANE_AXES, 0, 0)
    own_rows_d = after(own_rows_d, d_qkv)
    attn_grads = attn_grad(spot, attn_in, own_rows_d, move(own_rows_d, FLIP_CORE), d_qkv, combined)
    chip_d_qkv = after(across(d_qkv, PLANE_AXES, 0, 0), attn_grads)
    ffn_branch = plane_scatter(after(branch_half, chip_d_qkv))
    d_attn_in = core_scatter(input_grad(chip_d_qkv, query_weight, key_weight, value_weight))
    inverse_one = rms_inverse(residual)
    normed_one = residual * inverse_one
    d_normed = d_attn_in * normed_one
    u_attn = jnp.sum(d_normed, axis=0)
    tokens_grad = d_middle + inverse_one * (
        d_attn_in * lift_attn
        - normed_one * jnp.mean(d_normed * lift_attn, axis=-1, keepdims=True)
    )

    w_ffn = jnp.sum(incoming * ffn_branch, axis=0) * (1.0 - gate_ffn * gate_ffn)
    block_out = (middle + gate_ffn * ffn_branch).astype(b16)

    def spread(own):
        blocks = own.reshape(PLANE, own.shape[0] // PLANE, own.shape[1])
        return across(blocks, PLANE_AXES, 0, 0)

    def sheet(blocks, start, size):
        return jnp.concatenate(
            [blocks[i, :, start : start + size] for i in range(PLANE)], axis=1
        ).astype(f32)

    ffn_own = lax.psum_scatter(after(ffn_grads, states), "z", scatter_dimension=0, tiled=True)
    d_text_all = gather_by(d_text, FLIP_STRIP)
    attn_grads = lax.psum_scatter(after(attn_grads, ffn_own, d_text_all), "z", scatter_dimension=0, tiled=True)
    ffn_blocks = spread(ffn_own)
    attn_blocks = spread(attn_grads)
    gate_grad = sheet(ffn_blocks, 0, hidden_wide)
    up_grad = sheet(ffn_blocks, hidden_wide, hidden_wide)
    down_grad = sheet(ffn_blocks, 2 * hidden_wide, hidden_wide).T
    out_grad = sheet(attn_blocks, 3 * wide, wide).T
    query_grad = sheet(attn_blocks, 0, wide)
    key_grad = sheet(attn_blocks, wide, wide)
    value_grad = sheet(attn_blocks, 2 * wide, wide)

    back = across(after(d_text, chip_d_qkv), PLANE_AXES, 0, 0)
    back = back.reshape(-1, 2 * text_own)
    back = [back[:, :text_own], back[:, text_own:]]
    text_part = contract(back[0], text_key_weight, 0, 1)
    text_part = text_part + contract(back[1], text_value_weight, 0, 1)
    text_grad = core_scatter(text_part, 1)
    where_here = jnp.stack([strip]).astype(jnp.int32)
    states = after(states, ffn_blocks)
    text_sum = text_weight_grad(where_here, states, d_text_all)
    text_blocks = across(text_sum, PLANE_AXES, 0, 0)
    block_out, tokens_grad = from_items((ffn_blocks, text_part, text_blocks, attn_grads), block_out, tokens_grad.astype(b16))
    text_key_grad = text_blocks[:, :wide].reshape(PLANE * wide, -1).T.astype(f32)
    text_value_grad = text_blocks[:, wide:].reshape(PLANE * wide, -1).T.astype(f32)

    own_sums = jnp.concatenate([u_attn, u_ffn, w_ffn, w_attn])
    own_sums = own_sums + move(own_sums, FLIP_CORE)
    count = own_sums.shape[0]
    parts = jnp.concatenate(
        [own_sums, gains[:, 0], gains[:, 128], gains[:, 256], gains[:, 384]]
    )
    parts = gather_by(parts, FLIP_PLACE)
    head_parts = absolute([p[count:].reshape(4, wide) for p in parts], place)
    parts = jnp.concatenate(
        [pair_sum([p[:count] for p in parts]), jnp.concatenate(head_parts, axis=1).reshape(-1)]
    )
    parts = gather_by(after(parts, attn_grads), FLIP_STRIP)
    head_parts = pair_sum([p[count:] for p in parts]).reshape(4, PLANE * wide)
    sums = [p[:count].reshape(4, width) for p in absolute(parts, strip)]
    items = []
    for item in range(ITEMS):
        low_part = jnp.concatenate([attn_gain * sums[item][0], sums[item][3]])
        high_part = jnp.concatenate([ffn_gain * sums[item][1], sums[item][2]])
        items.append(jnp.where(first_core, low_part, high_part))
    ada_bias_grad = pair_sum(items)
    def by_item(table):
        return jnp.sum(band_mask[:, :, None] * table[None], axis=1)

    scales = by_item(low_mod[:, :width]), by_item(high_mod[:, :width])
    attn_gain_grad = pair_sum([sums[i][0] * (1.0 + scales[0][i]) for i in range(ITEMS)])
    ffn_gain_grad = pair_sum([sums[i][1] * (1.0 + scales[1][i]) for i in range(ITEMS)])
    ada_rows = silu_embed.shape[1] // (STRIPS * PLANE)
    silu_own = lax.dynamic_slice_in_dim(
        silu_embed, (strip * PLANE + place) * ada_rows, ada_rows, 1
    )
    ada_grad = lax.dot_general(
        by_item(silu_own), jnp.stack(items), (((0,), (0,)), ((), ())), precision=HIGHEST
    )
    return (
        block_out,
        tokens_grad,
        text_grad,
        ada_grad,
        ada_bias_grad,
        attn_gain_grad,
        ffn_gain_grad,
        query_grad,
        key_grad,
        value_grad,
        head_parts[0],
        head_parts[1],
        head_parts[3].reshape(-1, HDIM)[:, 0],
        text_key_grad,
        text_value_grad,
        head_parts[2],
        out_grad,
        gate_grad,
        up_grad,
        down_grad,
    )


def placements(seq, tp):
    ins = (
        P(seq, None),
        P(seq, None),
        P(),
        P(),
        P(),
        P(),
        P(seq, None),
        P(None, tp),
        P(tp),
        P(),
        P(),
        P(None, tp),
        P(None, tp),
        P(None, tp),
        P(tp),
        P(tp),
        P(tp),
        P(None, tp),
        P(None, tp),
        P(tp),
        P(tp, None),
        P(None, tp),
        P(None, tp),
        P(tp, None),
    )
    outs = (
        P(seq, None),
        P(seq, None),
        P(seq, tp),
        P(seq, tp),
        P(tp),
        P(),
        P(),
        P(seq, tp),
        P(seq, tp),
        P(seq, tp),
        P(tp),
        P(tp),
        P(tp),
        P(seq, tp),
        P(seq, tp),
        P(tp),
        P(tp, seq),
        P(seq, tp),
        P(seq, tp),
        P(tp, seq),
    )
    return ins, outs


def solution(mesh):
    if mesh.shape["seq"] == STRIPS * PLANE and mesh.shape["tp"] == CORES:
        body, seq, tp = strip_shards, ("z", "y", "x"), "c"
        mesh = Mesh(mesh.devices.reshape(STRIPS, 2, 2, CORES), MESH_AXES)
    else:
        body, seq, tp = shards, "seq", "tp"
    ins, outs = placements(seq, tp)
    return jax.shard_map(body, mesh=mesh, in_specs=ins, out_specs=outs, check_vma=False)
```
